512 devices in a mesh: section: 64 (over z_lo, x, core), dp: 8 (over z_hi, y).
Axes of the slice: x: 4, y: 4, z: 16 (z_hi: 2, z_lo: 8; z = z_hi * 8 + z_lo), core: 2. Of those that a mesh axis runs over, the one named last changes fastest.
Arguments:
- inputs: bfloat16 [1024, 3072], P('dp'), may hold values from -6 to 6
- cotangent: bfloat16 [1024, 3072], P('dp'), may hold values from -6 to 6
- weight: bfloat16 [3072, 6144], P('dp', 'section'), may hold values from -6 to 6
- moment1: float32 [3072, 6144], P('dp', 'section'), may hold values from -2 to 2
- moment2: float32 [3072, 6144], P('dp', 'section'), may hold values from 0.05 to 1
Outputs:
- spare: bfloat16 [1024, 6144], P('dp', 'section')
- input_gradient: bfloat16 [1024, 6144], P('dp', 'section')
- new_weight: bfloat16 [3072, 6144], P('dp', 'section')
- new_moment1: float32 [3072, 6144], P('dp', 'section')
- new_moment2: float32 [3072, 6144], P('dp', 'section')
- new_copy: bfloat16 [3072, 6144], P('dp', 'section')
The draws below stay inside these ranges and needn't reach their ends.
All inputs are finite; a program needn't handle non-finite values.
Results may differ from the reference program's by a relative error of at most 0.0058.
Values may be sent and summed in bfloat16 or wider, within the bound.
A program may use at most 64 MiB of HBM per device.

```python
import math
import jax
import jax.numpy as jnp
from jax import lax

D = 3072
SECTIONS = 2
TOK_DEV = 128
TOKENS = 1024
N_DP = 8


def shard_levels(stream_key, dims, split, low, high):
    def one(dim, parts):
        steps = jax.random.uniform(jax.random.fold_in(jax.random.fold_in(stream_key, 6), dim), (parts,), jnp.float32, low / len(split), high / len(split))
        return jnp.repeat(jnp.exp(steps), dims[dim] // parts).reshape((-1,) + (1,) * (len(dims) - dim - 1))

    level = one(*split[0])
    for cut in split[1:]:
        level = level * one(*cut)
    return level


def bell_draw(key, extent, deviation, limit, cuts=(), held_as=jnp.bfloat16):
    values = deviation * jax.random.normal(key, extent, jnp.float32)
    if cuts:
        values = values * shard_levels(key, extent, cuts, -0.22, 0.18)
    return jnp.clip(values, -limit, limit).astype(held_as)


def setup_inputs(seed: int = 0) -> dict:
    key_list = jax.random.split(jax.random.key(seed), 6)
    inputs = bell_draw(key_list[0], (TOKENS, D), 1.0, 6.0, ((0, 8),))
    cotangent = bell_draw(key_list[1], (TOKENS, D), 1.0, 6.0, ((0, 8),))
    weight = bell_draw(key_list[2], (D, SECTIONS * D), 1.0, 6.0, ((0, 8), (1, 64)))
    moment1 = bell_draw(key_list[3], (D, SECTIONS * D), 0.3, 2.0, ((0, 8), (1, 64)), jnp.float32)
    moment2 = jnp.clip(jnp.exp(math.log(1.0) - 2.9957323 * jax.random.uniform(key_list[4], (D, SECTIONS * D), jnp.float32) ** shard_levels(key_list[4], (D, SECTIONS * D), ((0, 8), (1, 64)), -0.2, 0.2)), 0.05, 1.0)
    return {"inputs": inputs, "cotangent": cotangent, "weight": weight, "moment1": moment1, "moment2": moment2}


NORM_EPS = 1e-05
FIRST_FIX = 0.6513215599
SECOND_FIX = 0.4012630607

def gelu_value(z):
    return 0.5 * z * (1.0 + lax.erf(z * 0.7071067811865476))

def gelu_slope(z):
    return 0.5 * (1.0 + lax.erf(z * 0.7071067811865476)) + z * jnp.exp(-0.5 * z * z) * 0.3989422804014327

def layer_norm(rows):
    centre = lax.optimization_barrier(jnp.mean(rows, axis=1, keepdims=True))
    centred = rows - centre
    variance = lax.optimization_barrier(jnp.mean(centred * centred, axis=1, keepdims=True))
    inverse = lax.rsqrt(variance + NORM_EPS)
    return (centred * inverse, inverse)

def reference(inputs, cotangent, weight, moment1, moment2):
    scale = 1.0 / math.sqrt(D)
    current = inputs
    saved = []
    outputs = []
    for section in range(SECTIONS):
        block = weight[:, section * D:(section + 1) * D]
        normed, inverse = layer_norm(current.astype(jnp.float32))
        lowered = normed.astype(jnp.bfloat16)
        mixed = jnp.dot(lowered, block, preferred_element_type=jnp.float32) * scale
        output = (current.astype(jnp.float32) + gelu_value(mixed)).astype(jnp.bfloat16)
        saved.append((normed, inverse, lowered, mixed))
        outputs.append(output)
        current = output
    spare = jnp.concatenate(outputs[1:] + [jnp.zeros((inputs.shape[0], D), jnp.bfloat16)], axis=1)
    upstream = cotangent
    blocks = [None] * SECTIONS
    grads = [None] * SECTIONS
    for section in reversed(range(SECTIONS)):
        normed, inverse, lowered, mixed = saved[section]
        block = weight[:, section * D:(section + 1) * D]
        slope = (upstream.astype(jnp.float32) * gelu_slope(mixed)).astype(jnp.bfloat16)
        total = jnp.zeros((D, D), jnp.float32)
        for replica in range(N_DP):
            rows_low = lowered[replica * TOK_DEV:(replica + 1) * TOK_DEV]
            rows_slope = slope[replica * TOK_DEV:(replica + 1) * TOK_DEV]
            partial_term = (jnp.dot(rows_low.T, rows_slope, preferred_element_type=jnp.float32) * scale).astype(jnp.bfloat16)
            total = total + partial_term.astype(jnp.float32)
        blocks[section] = total
        back = jnp.dot(slope, block.T, preferred_element_type=jnp.float32) * scale
        first = lax.optimization_barrier(jnp.mean(back, axis=1, keepdims=True))
        second = lax.optimization_barrier(jnp.mean(back * normed, axis=1, keepdims=True))
        change = inverse * (back - first - normed * second)
        upstream = (upstream.astype(jnp.float32) + change).astype(jnp.bfloat16)
        grads[section] = upstream
    input_gradient = jnp.concatenate(grads, axis=1)
    gradient = jnp.concatenate(blocks, axis=1)
    new_moment1 = 0.9 * moment1 + 0.1 * gradient
    new_moment2 = 0.95 * moment2 + 0.05 * gradient * gradient
    update = new_moment1 / FIRST_FIX / (jnp.sqrt(new_moment2 / SECOND_FIX) + 1e-08)
    plain = weight.astype(jnp.float32)
    new_weight = (plain - 0.05 * (update + 0.1 * plain)).astype(jnp.bfloat16)
    new_copy = jnp.concatenate([new_weight[:, D:], jnp.zeros((D, D), jnp.bfloat16)], axis=1)
    return (spare, input_gradient, new_weight, new_moment1, new_moment2, new_copy)
```

```python
import math

import jax
import jax.numpy as jnp
from jax import lax
from jax.experimental import pallas as pl
from jax.experimental.pallas import tpu as pltpu
from jax.sharding import PartitionSpec as P

D = 3072
SECTIONS = 2
NORM_EPS = 1e-05
FIRST_FIX = 0.6513215599
SECOND_FIX = 0.4012630607
SCALE = 1.0 / math.sqrt(D)
HALF = 64
LANE = 96
PAIR = 192
WIDE = 256
ROWS = 384
F32 = jnp.float32
BF16 = jnp.bfloat16

W_Z, W_Y, W_ZY, W_C = 0, 1, 4, 7
X_UP, X_Z, X_X = 15, 16, 19
LOW, X2, SPARE, SLOPE = 31, 32, 33, 34
B_X, B_Z = 35, 47
G_DOWN, G_C = 50, 51
G_YO, G_YS, G_Z, COPY = 52, 55, 58, 59
SLOTS = 60


def gelu_both(z):
    cdf = 0.5 * (1.0 + lax.erf(z * 0.7071067811865476))
    return z * cdf, cdf + z * jnp.exp(-0.5 * z * z) * 0.3989422804014327


def kernel(
    inputs, cotangent, w, m1, m2,
    spare, grad, new_w, new_m1, new_m2, copy,
    xin, cot, wv, m1v, m2v, wp, csum, low, xg, xout, normed, inv, mixed, slope_of, up, g_in,
    slope_t, sl, x2_t, x2, spare_in, bsend, brecv, zacc, zsend, zrecv,
    gout, g_t, gc, gsend, grecv, gzs, gzr, copy_out, copy_in,
    send_sem, recv_sem, here_sem,
):
    sec = lax.axis_index("section")
    dp = lax.axis_index("dp")
    c = sec % 2
    x = sec // 2 % 4
    s = sec // 32
    zq = sec // 8 % 4
    y = dp % 4
    zh = dp // 4
    odd = x % 2
    other = dp + 4 - 8 * zh
    core = {"section": sec + 1 - 2 * c, "dp": dp}
    across = {"section": sec + 32 - 64 * s, "dp": dp}
    far = {"section": sec, "dp": other}
    ys = [{"section": sec, "dp": zh * 4 + (y + j) % 4} for j in (1, 2, 3)]
    xs = [{"section": s * 32 + zq * 8 + (x + j) % 4 * 2 + c, "dp": dp} for j in (1, 2, 3)]
    zs = [{"section": s * 32 + (zq + j) % 4 * 8 + x * 2 + c, "dp": dp} for j in (1, 2, 3)]
    first = s == 0
    second = s == 1
    window = pl.ds(pl.multiple_of(zq * 768 + x // 2 * 384 + odd * 128, 128), WIDE)
    my_rows = pl.ds(pl.multiple_of(odd * 64 + c * LANE, 32), LANE)
    core_rows = pl.ds(pl.multiple_of(odd * 64 + (1 - c) * LANE, 32), LANE)

    def copier(slot, src, dst, to):
        return pltpu.make_async_remote_copy(
            src_ref=src,
            dst_ref=dst,
            send_sem=send_sem.at[slot],
            recv_sem=recv_sem.at[slot],
            device_id=to,
            device_id_type=pl.DeviceIdType.MESH,
        )

    def arrived(slot, where):
        copier(slot, where, where, core).wait_recv()

    def cols_of(replica):
        return pl.ds(pl.multiple_of(replica * ROWS, ROWS), ROWS)

    load_w = pltpu.make_async_copy(w, wv, here_sem.at[0])
    load_m1 = pltpu.make_async_copy(m1, m1v, here_sem.at[1])
    load_m2 = pltpu.make_async_copy(m2, m2v, here_sem.at[2])
    tokens = [pl.ds(pl.multiple_of(half * HALF, HALF), HALF) for half in (c, 1 - c)]
    load_x = [
        pltpu.make_async_copy(inputs.at[tokens[i]], xin.at[half], here_sem.at[3 + i])
        for i, half in enumerate((c, 1 - c))
    ]
    load_cot = pltpu.make_async_copy(cotangent.at[tokens[0], window], cot, here_sem.at[5])
    load_w.start()

    @pl.when(first)
    def _():
        for one in load_x:
            one.start()

    @pl.when(second)
    def _():
        load_cot.start()

    load_m1.start()
    load_m2.start()

    barrier = pltpu.get_barrier_semaphore()
    peers = [core, across, far] + ys + xs + zs
    for peer in peers:
        pl.semaphore_signal(barrier, inc=1, device_id=peer, device_id_type=pl.DeviceIdType.MESH)
    load_w.wait()
    pl.semaphore_wait(barrier, len(peers))

    mine = wp.at[my_rows, cols_of(dp)]
    sent = [copier(W_Z, wv, mine, far)]
    sent += [copier(W_Y + j, wv, mine, ys[j]) for j in range(3)]
    sent.append(copier(W_C, wv, mine, core))
    for one in sent:
        one.start()
    wp[my_rows, cols_of(dp)] = wv[...]
    blank = pl.ds(pl.multiple_of((1 - odd) * PAIR, 64), WIDE - PAIR)
    wp[blank, :] = jnp.zeros((WIDE - PAIR, D), BF16)

    def normalise(rows):
        centre = jnp.mean(rows, axis=1, keepdims=True)
        gap = rows - centre
        scale = lax.rsqrt(jnp.mean(gap * gap, axis=1, keepdims=True) + NORM_EPS)
        return (gap * scale).astype(BF16), centre, scale

    def keep_stats(block, centre, scale):
        inv[...] = jnp.broadcast_to(scale, (HALF, 128))
        normed[...] = (block.astype(F32) - centre) * scale

    @pl.when(first)
    def _():
        load_x[0].wait()
        low[c], centre, scale = normalise(xin[c].astype(F32))
        keep_stats(xin[c, :, window], centre, scale)

    def to_core(slot, replica):
        block = wp.at[my_rows, cols_of(replica)]
        one = copier(slot, block, block, core)
        one.start()
        sent.append(one)

    from_y = [zh * 4 + (y + 4 - j) % 4 for j in (1, 2, 3)]
    from_zy = [(1 - zh) * 4 + (y + 4 - j) % 4 for j in (1, 2, 3)]
    held = wp.at[my_rows, cols_of(other)]
    arrived(W_Z, held)
    for j in range(3):
        one = copier(W_ZY + j, held, held, ys[j])
        one.start()
        sent.append(one)
    to_core(W_C + 1, other)
    for j in range(3):
        arrived(W_Y + j, wp.at[my_rows, cols_of(from_y[j])])
        to_core(W_C + 2 + j, from_y[j])
    for j in range(3):
        arrived(W_ZY + j, wp.at[my_rows, cols_of(from_zy[j])])
        to_core(W_C + 5 + j, from_zy[j])
    for i, replica in enumerate([dp, other] + from_y + from_zy):
        arrived(W_C + i, wp.at[core_rows, cols_of(replica)])

    def column_sums():
        csum[...] = lax.dot_general(
            jnp.ones((16, D), BF16), wp[...], (((1,), (1,)), ((), ())), preferred_element_type=F32
        )

    own = xg.at[x, zq]
    x_up = copier(X_UP, xout, own, across)
    x_z = [copier(X_Z + j, own, own, zs[j]) for j in range(3)]
    x_x = []
    for i in range(4):
        block = xg.at[x, (zq + 4 - i) % 4]
        x_x.append([copier(X_X + 3 * i + j, block, block, xs[j]) for j in range(3)])
    swap_low = copier(LOW, low.at[c], low.at[c], core)

    @pl.when(second)
    def _():
        column_sums()
        arrived(X_UP, own)
        for one in x_z + x_x[0]:
            one.start()
        for j in range(3):
            arrived(X_Z + j, xg.at[x, (zq + 3 - j) % 4])
            for one in x_x[j + 1]:
                one.start()
        for i in range(4):
            for j in range(3):
                arrived(X_X + 3 * i + j, xg.at[(x + 3 - j) % 4, (zq + 4 - i) % 4])
        left = lax.broadcasted_iota(jnp.int32, (HALF, 128), 1) < HALF
        parts = []
        for m in range(8):
            even = xg[m % 2 * 2, m // 2].astype(F32)
            late = xg[m % 2 * 2 + 1, m // 2].astype(F32)
            middle = jnp.where(left, even[:, 128:], late[:, :128])
            parts += [even[:, :128], middle, late[:, 128:]]
        low[c], centre, scale = normalise(jnp.concatenate(parts, axis=1))
        swap_low.start()
        keep_stats(xg[x, zq], centre, scale)
        load_cot.wait()
        up[...] = cot[...].astype(F32)

    z = SCALE * lax.dot_general(
        low[c], wp[...], (((1,), (1,)), ((), ())), preferred_element_type=F32
    )
    value, slope_value = gelu_both(z)
    mixed[...] = z
    slope_of[...] = slope_value

    @pl.when(first)
    def _():
        xout[...] = (xin[c, :, window].astype(F32) + value).astype(BF16)
        x_up.start()
        load_x[1].wait()
        low[1 - c], _, _ = normalise(xin[1 - c].astype(F32))
        column_sums()
        arrived(G_DOWN, g_in)
        up[...] = g_in[...].astype(F32)

    slope = (up[...] * slope_of[...]).astype(BF16)
    swap_slope = copier(SLOPE, slope_t.at[core_rows], sl.at[c], core)
    b_x = []
    for i in range(4):
        q = (zq + 1 + i) % 4
        b_x.append(
            [copier(B_X + 3 * i + j, bsend.at[(x + 1 + j) % 4, q], brecv.at[j, q], xs[j])
             for j in range(3)]
        )

    def give_slope():
        slope_t[...] = slope.T
        swap_slope.start()
        sl[c] = slope_t[my_rows, :]

    def back():
        wide = slope.astype(F32)
        r1 = jnp.sum(wide * csum[0:1, :], axis=1, keepdims=True) * (SCALE / D)
        r2 = jnp.sum(wide * mixed[...], axis=1, keepdims=True) * (1.0 / D)
        h1 = r1.astype(BF16).astype(F32)
        h2 = r2.astype(BF16).astype(F32)
        lane = lax.broadcasted_iota(jnp.int32, (HALF, 128), 1)
        spot = lane % 64
        sums = jnp.where(
            spot == 0, h1, jnp.where(spot == 1, r1 - h1, jnp.where(spot == 2, h2, r2 - h2))
        )
        for i in range(4):
            q = (zq + 1 + i) % 4
            for half in range(2):
                cols = pl.ds(pl.multiple_of(q * 768 + half * 384, 384), 384)
                part = SCALE * jnp.dot(slope, wp[:, cols], preferred_element_type=F32)
                middle = part[:, 128:256]
                bsend[2 * half, q, :, :128] = part[:, :128].astype(BF16)
                bsend[2 * half, q, :, 128:] = jnp.where(lane < 64, middle, sums).astype(BF16)
                bsend[2 * half + 1, q, :, :128] = jnp.where(lane < 64, sums, middle).astype(BF16)
                bsend[2 * half + 1, q, :, 128:] = part[:, 256:].astype(BF16)
            for one in b_x[i]:
                one.start()

    swap_x2 = copier(X2, x2_t.at[core_rows], x2.at[c], core)

    @pl.when(second)
    def _():
        back()
        give_slope()
        x2_t[...] = (xg[x, zq].astype(F32) + value).astype(BF16).T
        swap_x2.start()
        x2[c] = x2_t[my_rows, :]
        arrived(LOW, low.at[1 - c])

    @pl.when(first)
    def _():
        give_slope()

    arrived(SLOPE, sl.at[1 - c])
    whole = jnp.concatenate([sl[0], sl[1]], axis=1)
    g_y = []
    for i, half in enumerate((1 - zh, zh)):
        for j in range(4):
            to = (y + 1 + j) % 4
            cols = cols_of(half * 4 + to)
            rows = low[:, :, cols].reshape(2 * HALF, ROWS)
            part = jnp.dot(whole, rows, preferred_element_type=F32)
            gsend[half, to] = (part * SCALE).astype(BF16)
            if j < 3:
                one = copier(G_YO + 3 * i + j, gsend.at[half, to], grecv.at[i, j], ys[j])
                one.start()
                g_y.append(one)

    @pl.when(first)
    def _():
        back()

    b_z = []
    for i in range(4):
        q = (zq + 1 + i) % 4
        total = bsend[x, q].astype(F32)
        for j in range(3):
            arrived(B_X + 3 * i + j, brecv.at[j, q])
            total = total + brecv[j, q].astype(F32)
        if i < 3:
            zsend[q] = total.astype(BF16)
            one = copier(B_Z + i, zsend.at[q], zrecv.at[i], zs[i])
            one.start()
            b_z.append(one)
        else:
            zacc[...] = total

    send_far = copier(G_Z, gzs, gzr, far)

    def reduce_far():
        total = gsend[1 - zh, y].astype(F32)
        for j in range(3):
            arrived(G_YO + j, grecv.at[0, j])
            total = total + grecv[0, j].astype(F32)
        gzs[...] = total.astype(BF16)
        send_far.start()

    @pl.when(first)
    def _():
        reduce_far()

    total = zacc[...]
    for j in range(3):
        arrived(B_Z + j, zrecv.at[j])
        total = total + zrecv[j].astype(F32)
    tail = jnp.where(odd == 0, total[:, PAIR:], total[:, : WIDE - PAIR])
    r1 = tail[:, 0:1] + tail[:, 1:2]
    r2 = tail[:, 2:3] + tail[:, 3:4]
    change = inv[:, 0:1] * (total - r1 - normed[...] * r2)
    renewed = (up[...] + change).astype(BF16)
    gout[...] = renewed
    g_down = copier(G_DOWN, gout, g_in, across)

    @pl.when(second)
    def _():
        g_down.start()

    g_t[...] = renewed.T
    swap_g = copier(G_C, g_t.at[core_rows], gc.at[c], core)
    swap_g.start()
    gc[c] = g_t[my_rows, :]

    send_spare = copier(SPARE, x2, spare_in, across)

    @pl.when(second)
    def _():
        reduce_far()
        arrived(X2, x2.at[1 - c])
        send_spare.start()

    total = gsend[zh, y].astype(F32)
    for j in range(3):
        arrived(G_YS + j, grecv.at[1, j])
        total = total + grecv[1, j].astype(F32)
    load_m1.wait()
    load_m2.wait()
    arrived(G_Z, gzr)
    gradient = total + gzr[...].astype(F32)
    moment1 = 0.9 * m1v[...] + 0.1 * gradient
    moment2 = 0.95 * m2v[...] + 0.05 * gradient * gradient
    update = moment1 / FIRST_FIX / (jnp.sqrt(moment2 / SECOND_FIX) + 1e-08)
    plain = wv[...].astype(F32)
    stepped = (plain - 0.05 * (update + 0.1 * plain)).astype(BF16)
    copy_out[...] = stepped
    send_copy = copier(COPY, copy_out, copy_in, across)

    @pl.when(second)
    def _():
        send_copy.start()
        spare[...] = jnp.zeros_like(spare)
        copy[...] = jnp.zeros_like(copy)

    new_m1[...] = moment1
    new_m2[...] = moment2
    new_w[...] = stepped

    arrived(G_C, gc.at[1 - c])
    grad[...] = jnp.concatenate([gc[0], gc[1]], axis=1)

    @pl.when(first)
    def _():
        arrived(SPARE, spare_in)
        spare[...] = jnp.concatenate([spare_in[0], spare_in[1]], axis=1)
        arrived(COPY, copy_in)
        copy[...] = copy_in[...]
        x_up.wait_send()

    for one in sent + [swap_slope, swap_g, send_far] + sum(b_x, []) + b_z + g_y:
        one.wait_send()

    @pl.when(second)
    def _():
        for one in x_z + sum(x_x, []) + [swap_low, swap_x2, g_down, send_spare, send_copy]:
            one.wait_send()


def per_device(inputs, cotangent, weight, moment1, moment2):
    vmem = pl.BlockSpec(memory_space=pltpu.VMEM)
    anywhere = pl.BlockSpec(memory_space=pl.ANY)
    shape = jax.ShapeDtypeStruct
    outs = [
        shape((LANE, 2 * HALF), BF16),
        shape((LANE, 2 * HALF), BF16),
        shape((LANE, ROWS), BF16),
        shape((LANE, ROWS), F32),
        shape((LANE, ROWS), F32),
        shape((LANE, ROWS), BF16),
    ]
    scratch = [
        ((2, HALF, D), BF16),
        ((HALF, WIDE), BF16),
        ((LANE, ROWS), BF16),
        ((LANE, ROWS), F32),
        ((LANE, ROWS), F32),
        ((WIDE, D), BF16),
        ((16, WIDE), F32),
        ((2, HALF, D), BF16),
        ((4, 4, HALF, WIDE), BF16),
        ((HALF, WIDE), BF16),
        ((HALF, WIDE), F32),
        ((HALF, 128), F32),
        ((HALF, WIDE), F32),
        ((HALF, WIDE), F32),
        ((HALF, WIDE), F32),
        ((HALF, WIDE), BF16),
        ((WIDE, HALF), BF16),
        ((2, LANE, HALF), BF16),
        ((WIDE, HALF), BF16),
        ((2, LANE, HALF), BF16),
        ((2, LANE, HALF), BF16),
        ((4, 4, HALF, WIDE), BF16),
        ((3, 4, HALF, WIDE), BF16),
        ((HALF, WIDE), F32),
        ((4, HALF, WIDE), BF16),
        ((3, HALF, WIDE), BF16),
        ((HALF, WIDE), BF16),
        ((WIDE, HALF), BF16),
        ((2, LANE, HALF), BF16),
        ((2, 4, LANE, ROWS), BF16),
        ((2, 3, LANE, ROWS), BF16),
        ((LANE, ROWS), BF16),
        ((LANE, ROWS), BF16),
        ((LANE, ROWS), BF16),
        ((LANE, ROWS), BF16),
    ]
    results = pl.pallas_call(
        kernel,
        out_shape=outs,
        in_specs=[anywhere] * 5,
        out_specs=[vmem] * 6,
        scratch_shapes=[pltpu.VMEM(dims, kind) for dims, kind in scratch]
        + [pltpu.SemaphoreType.DMA((SLOTS,))] * 2
        + [pltpu.SemaphoreType.DMA((6,))],
        compiler_params=pltpu.CompilerParams(
            collective_id=0, has_side_effects=True, vmem_limit_bytes=40 * 2**20
        ),
    )(inputs, cotangent, weight.T, moment1.T, moment2.T)
    return tuple(one.T for one in results)


def solution(mesh):
    split = P("dp", "section")
    return jax.shard_map(
        per_device,
        mesh=mesh,
        in_specs=(P("dp", None), P("dp", None), split, split, split),
        out_specs=(split,) * 6,
        check_vma=False,
    )
```

```python
import math

import jax
import jax.numpy as jnp
from jax import lax
from jax.experimental import pallas as pl
from jax.experimental.pallas import tpu as pltpu
from jax.sharding import PartitionSpec as P

D = 3072
SECTIONS = 2
NORM_EPS = 1e-05
FIRST_FIX = 0.6513215599
SECOND_FIX = 0.4012630607
SCALE = 1.0 / math.sqrt(D)
HALF = 64
LANE = 96
PAIR = 192
WIDE = 256
ROWS = 384
F32 = jnp.float32
BF16 = jnp.bfloat16

PIECE = HALF // 2
CUT = LANE // 2

W_Z, W_Y, W_ZY, W_C = 0, 2, 5, 11
X_UP, X_Z, X_X = 19, 21, 27
LOW, X2, SPARE, SLOPE = 51, 52, 53, 54
B_X, B_Z = 55, 79
G_DOWN, G_C = 85, 87
G_YO, G_YS, G_Z, COPY = 88, 94, 97, 99
SLOTS = 100


def gelu_both(z):
    cdf = 0.5 * (1.0 + lax.erf(z * 0.7071067811865476))
    return z * cdf, cdf + z * jnp.exp(-0.5 * z * z) * 0.3989422804014327


def kernel(
    inputs, cotangent, w, m1, m2,
    spare, grad, new_w, new_m1, new_m2, copy,
    xin, cot, wv, m1v, m2v, wp, csum, low, xg, xout, normed, inv, mixed, slope_of, up, g_in,
    slope_t, sl, x2_t, x2, spare_in, bsend, brecv, zacc, zsend, zrecv,
    gout, g_t, gc, gsend, grecv, gzs, gzr, copy_out, copy_in, slopes, x2_w,
    send_sem, recv_sem, here_sem, go,
):
    sec = lax.axis_index("section")
    dp = lax.axis_index("dp")
    c = sec % 2
    x = sec // 2 % 4
    s = sec // 32
    zq = sec // 8 % 4
    y = dp % 4
    zh = dp // 4
    odd = x % 2
    other = dp + 4 - 8 * zh
    core = {"section": sec + 1 - 2 * c, "dp": dp}
    across = {"section": sec + 32 - 64 * s, "dp": dp}
    far = {"section": sec, "dp": other}
    ys = [{"section": sec, "dp": zh * 4 + (y + j) % 4} for j in (1, 2, 3)]
    xs = [{"section": s * 32 + zq * 8 + (x + j) % 4 * 2 + c, "dp": dp} for j in (1, 2, 3)]
    zs = [{"section": s * 32 + (zq + j) % 4 * 8 + x * 2 + c, "dp": dp} for j in (1, 2, 3)]
    first = s == 0
    second = s == 1
    window = pl.ds(pl.multiple_of(zq * 768 + x // 2 * 384 + odd * 128, 128), WIDE)
    my_rows = pl.ds(pl.multiple_of(odd * 64 + c * LANE, 32), LANE)
    core_rows = pl.ds(pl.multiple_of(odd * 64 + (1 - c) * LANE, 32), LANE)

    def copier(slot, src, dst, to):
        return pltpu.make_async_remote_copy(
            src_ref=src,
            dst_ref=dst,
            send_sem=send_sem.at[slot],
            recv_sem=recv_sem.at[slot],
            device_id=to,
            device_id_type=pl.DeviceIdType.MESH,
        )

    def arrived(slot, where):
        copier(slot, where, where, core).wait_recv()

    def cols_of(replica):
        return pl.ds(pl.multiple_of(replica * ROWS, ROWS), ROWS)

    load_w = pltpu.make_async_copy(w, wv, here_sem.at[0])
    load_m1 = pltpu.make_async_copy(m1, m1v, here_sem.at[1])
    load_m2 = pltpu.make_async_copy(m2, m2v, here_sem.at[2])
    tokens = [pl.ds(pl.multiple_of(half * HALF, HALF), HALF) for half in (c, 1 - c)]
    load_x = [
        pltpu.make_async_copy(inputs.at[tokens[i]], xin.at[half], here_sem.at[3 + i])
        for i, half in enumerate((c, 1 - c))
    ]
    load_cot = pltpu.make_async_copy(cotangent.at[tokens[0], window], cot, here_sem.at[5])
    load_w.start()

    @pl.when(first)
    def _():
        for one in load_x:
            one.start()

    @pl.when(second)
    def _():
        load_cot.start()

    load_m1.start()
    load_m2.start()

    barrier = pltpu.get_barrier_semaphore()
    peers = [core, across, far] + ys + xs + zs
    for peer in peers:
        pl.semaphore_signal(barrier, inc=1, device_id=peer, device_id_type=pl.DeviceIdType.MESH)
    load_w.wait()
    pl.semaphore_wait(barrier, len(peers))

    pieces = [pl.ds(PIECE * t, PIECE) for t in range(2)]
    cuts = [pl.ds(CUT * t, CUT) for t in range(2)]
    my_cuts = [pl.ds(pl.multiple_of(odd * 64 + c * LANE + CUT * t, 16), CUT) for t in range(2)]

    w_far = [copier(W_Z + t, wv.at[cuts[t]], wp.at[my_cuts[t], cols_of(dp)], far) for t in range(2)]
    mine = wp.at[my_rows, cols_of(dp)]
    sent = [copier(W_Y + j, wv, mine, ys[j]) for j in range(3)]
    sent.append(copier(W_C, wv, mine, core))

    @pl.when(first)
    def _():
        for one in w_far:
            one.start()

    for one in sent:
        one.start()
    sent += w_far
    wp[my_rows, cols_of(dp)] = wv[...]
    blank = pl.ds(pl.multiple_of((1 - odd) * PAIR, 64), WIDE - PAIR)
    wp[blank, :] = jnp.zeros((WIDE - PAIR, D), BF16)

    def normalise(rows):
        centre = jnp.mean(rows, axis=1, keepdims=True)
        gap = rows - centre
        scale = lax.rsqrt(jnp.mean(gap * gap, axis=1, keepdims=True) + NORM_EPS)
        return (gap * scale).astype(BF16), centre, scale

    def keep_stats(rows, block, centre, scale):
        inv[rows, :] = jnp.broadcast_to(scale, (scale.shape[0], 128))
        normed[rows, :] = (block.astype(F32) - centre) * scale

    @pl.when(first)
    def _():
        load_x[0].wait()
        low[c], centre, scale = normalise(xin[c].astype(F32))
        keep_stats(slice(None), xin[c, :, window], centre, scale)

    def to_core(slot, replica):
        block = wp.at[my_rows, cols_of(replica)]
        one = copier(slot, block, block, core)
        one.start()
        sent.append(one)

    from_y = [zh * 4 + (y + 4 - j) % 4 for j in (1, 2, 3)]
    from_zy = [(1 - zh) * 4 + (y + 4 - j) % 4 for j in (1, 2, 3)]
    for j in range(3):
        arrived(W_Y + j, wp.at[my_rows, cols_of(from_y[j])])
        to_core(W_C + 2 + j, from_y[j])

    @pl.when(second)
    def _():
        pl.semaphore_wait(go, 1)
        for one in w_far:
            one.start()

    for t in range(2):
        held = wp.at[my_cuts[t], cols_of(other)]
        arrived(W_Z + t, held)
        for j in range(3):
            one = copier(W_ZY + 3 * t + j, held, held, ys[j])
            one.start()
            sent.append(one)

    @pl.when(first)
    def _():
        pl.semaphore_signal(go, inc=1, device_id=across, device_id_type=pl.DeviceIdType.MESH)

    to_core(W_C + 1, other)
    for j in range(3):
        for t in range(2):
            arrived(W_ZY + 3 * t + j, wp.at[my_cuts[t], cols_of(from_zy[j])])
        to_core(W_C + 5 + j, from_zy[j])
    for i, replica in enumerate([dp, other] + from_y + from_zy):
        arrived(W_C + i, wp.at[core_rows, cols_of(replica)])

    def column_sums():
        csum[...] = lax.dot_general(
            jnp.ones((16, D), BF16), wp[...], (((1,), (1,)), ((), ())), preferred_element_type=F32
        )

    own = [xg.at[x, zq, rows] for rows in pieces]
    x_up = [copier(X_UP + t, xout.at[pieces[t]], own[t], across) for t in range(2)]
    x_z = [copier(X_Z + 3 * t + j, own[t], own[t], zs[j]) for t in range(2) for j in range(3)]
    x_x = []
    for t in range(2):
        for i in range(4):
            block = xg.at[x, (zq + 4 - i) % 4, pieces[t]]
            x_x += [copier(X_X + 12 * t + 3 * i + j, block, block, xs[j]) for j in range(3)]
    swap_low = copier(LOW, low.at[c], low.at[c], core)
    b_x = []
    for t in range(2):
        for i in range(4):
            q = (zq + 1 + i) % 4
            for j in range(3):
                block = bsend.at[(x + 1 + j) % 4, q, pieces[t]]
                landing = brecv.at[j, q, pieces[t]]
                b_x.append(copier(B_X + 12 * t + 3 * i + j, block, landing, xs[j]))

    @pl.when(second)
    def _():
        column_sums()
        for t in range(2):
            arrived(X_UP + t, own[t])
            for one in x_z[3 * t : 3 * t + 3] + x_x[12 * t : 12 * t + 3]:
                one.start()
        for t in range(2):
            for j in range(3):
                arrived(X_Z + 3 * t + j, xg.at[x, (zq + 3 - j) % 4, pieces[t]])
                for one in x_x[12 * t + 3 * j + 3 : 12 * t + 3 * j + 6]:
                    one.start()
        load_cot.wait()

    def gathered(t):
        for i in range(4):
            for j in range(3):
                block = xg.at[(x + 3 - j) % 4, (zq + 4 - i) % 4, pieces[t]]
                arrived(X_X + 12 * t + 3 * i + j, block)
        rows = pieces[t]
        left = lax.broadcasted_iota(jnp.int32, (PIECE, 128), 1) < 64
        parts = []
        for m in range(8):
            even = xg[m % 2 * 2, m // 2, rows].astype(F32)
            late = xg[m % 2 * 2 + 1, m // 2, rows].astype(F32)
            middle = jnp.where(left, even[:, 128:], late[:, :128])
            parts += [even[:, :128], middle, late[:, 128:]]
        low[c, rows], centre, scale = normalise(jnp.concatenate(parts, axis=1))
        keep_stats(rows, xg[x, zq, rows], centre, scale)

    def find_slope(rows, upstream):
        up[rows, :] = upstream.astype(F32)
        slopes[rows, :] = (up[rows, :] * slope_of[rows, :]).astype(BF16)

    def back(rows, size, messages):
        slope = slopes[rows, :]
        wide = slope.astype(F32)
        r1 = jnp.sum(wide * csum[0:1, :], axis=1, keepdims=True) * (SCALE / D)
        r2 = jnp.sum(wide * mixed[rows, :], axis=1, keepdims=True) * (1.0 / D)
        h1 = r1.astype(BF16).astype(F32)
        h2 = r2.astype(BF16).astype(F32)
        lane = lax.broadcasted_iota(jnp.int32, (size, 128), 1)
        spot = lane % 64
        sums = jnp.where(
            spot == 0, h1, jnp.where(spot == 1, r1 - h1, jnp.where(spot == 2, h2, r2 - h2))
        )
        for i in range(4):
            q = (zq + 1 + i) % 4
            for half in range(2):
                cols = pl.ds(pl.multiple_of(q * 768 + half * 384, 384), 384)
                part = SCALE * jnp.dot(slope, wp[:, cols], preferred_element_type=F32)
                middle = part[:, 128:256]
                even = jnp.concatenate([part[:, :128], jnp.where(lane < 64, middle, sums)], axis=1)
                late = jnp.concatenate([jnp.where(lane < 64, sums, middle), part[:, 256:]], axis=1)
                bsend[2 * half, q, rows] = even.astype(BF16)
                bsend[2 * half + 1, q, rows] = late.astype(BF16)
            for one in messages[3 * i : 3 * i + 3] + messages[3 * i + 12 : 3 * i + 15]:
                one.start()

    for t in range(2):
        rows = pieces[t]

        @pl.when(second)
        def _():
            gathered(t)

        z = SCALE * lax.dot_general(
            low[c, rows], wp[...], (((1,), (1,)), ((), ())), preferred_element_type=F32
        )
        value, slope_value = gelu_both(z)
        mixed[rows, :] = z
        slope_of[rows, :] = slope_value

        @pl.when(first)
        def _():
            xout[rows, :] = (xin[c, rows, window].astype(F32) + value).astype(BF16)
            x_up[t].start()

        @pl.when(second)
        def _():
            find_slope(rows, cot[rows, :])
            back(rows, PIECE, b_x[12 * t : 12 * t + 12])
            x2_w[rows, :] = (xg[x, zq, rows].astype(F32) + value).astype(BF16)

    @pl.when(first)
    def _():
        load_x[1].wait()
        low[1 - c], _, _ = normalise(xin[1 - c].astype(F32))
        column_sums()
        for t in range(2):
            arrived(G_DOWN + t, g_in.at[pieces[t]])
            find_slope(pieces[t], g_in[pieces[t], :])

    swap_slope = copier(SLOPE, slope_t.at[core_rows], sl.at[c], core)
    slope_t[...] = slopes[...].T
    swap_slope.start()
    sl[c] = slope_t[my_rows, :]
    swap_x2 = copier(X2, x2_t.at[core_rows], x2.at[c], core)

    @pl.when(second)
    def _():
        swap_low.start()
        x2_t[...] = x2_w[...].T
        swap_x2.start()
        x2[c] = x2_t[my_rows, :]
        arrived(LOW, low.at[1 - c])

    arrived(SLOPE, sl.at[1 - c])
    whole = jnp.concatenate([sl[0], sl[1]], axis=1)
    g_y = []
    for i, half in enumerate((1 - zh, zh)):
        for j in range(4):
            to = (y + 1 + j) % 4
            cols = cols_of(half * 4 + to)
            rows = low[:, :, cols].reshape(2 * HALF, ROWS)
            part = jnp.dot(whole, rows, preferred_element_type=F32)
            gsend[half, to] = (part * SCALE).astype(BF16)
            if j < 3:
                if i == 0:
                    some = [
                        copier(G_YO + 2 * j + t, gsend.at[half, to, cuts[t]], grecv.at[i, j, cuts[t]], ys[j])
                        for t in range(2)
                    ]
                else:
                    some = [copier(G_YS + j, gsend.at[half, to], grecv.at[i, j], ys[j])]
                for one in some:
                    one.start()
                g_y += some

    send_far = [copier(G_Z + t, gzs.at[cuts[t]], gzr.at[cuts[t]], far) for t in range(2)]

    def reduce_far():
        for t in range(2):
            total = gsend[1 - zh, y, cuts[t]].astype(F32)
            for j in range(3):
                arrived(G_YO + 2 * j + t, grecv.at[0, j, cuts[t]])
                total = total + grecv[0, j, cuts[t]].astype(F32)
            gzs[cuts[t], :] = total.astype(BF16)
            send_far[t].start()

    @pl.when(first)
    def _():
        back(slice(None), HALF, b_x)
        reduce_far()

    b_z = []
    for t in range(2):
        rows = pieces[t]
        for i in range(4):
            q = (zq + 1 + i) % 4
            total = bsend[x, q, rows].astype(F32)
            for j in range(3):
                arrived(B_X + 12 * t + 3 * i + j, brecv.at[j, q, rows])
                total = total + brecv[j, q, rows].astype(F32)
            if i < 3:
                zsend[q, rows] = total.astype(BF16)
                one = copier(B_Z + 3 * t + i, zsend.at[q, rows], zrecv.at[i, rows], zs[i])
                one.start()
                b_z.append(one)
            else:
                zacc[rows, :] = total

    g_down = [copier(G_DOWN + t, gout.at[pieces[t]], g_in.at[pieces[t]], across) for t in range(2)]
    for t in range(2):
        rows = pieces[t]
        total = zacc[rows, :]
        for j in range(3):
            arrived(B_Z + 3 * t + j, zrecv.at[j, rows])
            total = total + zrecv[j, rows].astype(F32)
        tail = jnp.where(odd == 0, total[:, PAIR:], total[:, : WIDE - PAIR])
        r1 = tail[:, 0:1] + tail[:, 1:2]
        r2 = tail[:, 2:3] + tail[:, 3:4]
        change = inv[rows, 0:1] * (total - r1 - normed[rows, :] * r2)
        gout[rows, :] = (up[rows, :] + change).astype(BF16)

        @pl.when(second)
        def _():
            g_down[t].start()

    @pl.when(second)
    def _():
        reduce_far()

    g_t[...] = gout[...].T
    swap_g = copier(G_C, g_t.at[core_rows], gc.at[c], core)
    swap_g.start()
    gc[c] = g_t[my_rows, :]

    send_spare = copier(SPARE, x2, spare_in, across)

    @pl.when(second)
    def _():
        arrived(X2, x2.at[1 - c])
        send_spare.start()

    total = gsend[zh, y].astype(F32)
    for j in range(3):
        arrived(G_YS + j, grecv.at[1, j])
        total = total + grecv[1, j].astype(F32)
    load_m1.wait()
    load_m2.wait()
    for t in range(2):
        arrived(G_Z + t, gzr.at[cuts[t]])
    gradient = total + gzr[...].astype(F32)
    moment1 = 0.9 * m1v[...] + 0.1 * gradient
    moment2 = 0.95 * m2v[...] + 0.05 * gradient * gradient
    update = moment1 / FIRST_FIX / (jnp.sqrt(moment2 / SECOND_FIX) + 1e-08)
    plain = wv[...].astype(F32)
    stepped = (plain - 0.05 * (update + 0.1 * plain)).astype(BF16)
    copy_out[...] = stepped
    send_copy = copier(COPY, copy_out, copy_in, across)

    @pl.when(second)
    def _():
        send_copy.start()
        spare[...] = jnp.zeros_like(spare)
        copy[...] = jnp.zeros_like(copy)

    new_m1[...] = moment1
    new_m2[...] = moment2
    new_w[...] = stepped

    arrived(G_C, gc.at[1 - c])
    grad[...] = jnp.concatenate([gc[0], gc[1]], axis=1)

    @pl.when(first)
    def _():
        arrived(SPARE, spare_in)
        spare[...] = jnp.concatenate([spare_in[0], spare_in[1]], axis=1)
        arrived(COPY, copy_in)
        copy[...] = copy_in[...]
        for one in x_up:
            one.wait_send()

    for one in sent + [swap_slope, swap_g] + send_far + b_x + b_z + g_y:
        one.wait_send()

    @pl.when(second)
    def _():
        for one in x_z + x_x + g_down + [swap_low, swap_x2, send_spare, send_copy]:
            one.wait_send()


def per_device(inputs, cotangent, weight, moment1, moment2):
    vmem = pl.BlockSpec(memory_space=pltpu.VMEM)
    anywhere = pl.BlockSpec(memory_space=pl.ANY)
    shape = jax.ShapeDtypeStruct
    outs = [
        shape((LANE, 2 * HALF), BF16),
        shape((LANE, 2 * HALF), BF16),
        shape((LANE, ROWS), BF16),
        shape((LANE, ROWS), F32),
        shape((LANE, ROWS), F32),
        shape((LANE, ROWS), BF16),
    ]
    scratch = [
        ((2, HALF, D), BF16),
        ((HALF, WIDE), BF16),
        ((LANE, ROWS), BF16),
        ((LANE, ROWS), F32),
        ((LANE, ROWS), F32),
        ((WIDE, D), BF16),
        ((16, WIDE), F32),
        ((2, HALF, D), BF16),
        ((4, 4, HALF, WIDE), BF16),
        ((HALF, WIDE), BF16),
        ((HALF, WIDE), F32),
        ((HALF, 128), F32),
        ((HALF, WIDE), F32),
        ((HALF, WIDE), F32),
        ((HALF, WIDE), F32),
        ((HALF, WIDE), BF16),
        ((WIDE, HALF), BF16),
        ((2, LANE, HALF), BF16),
        ((WIDE, HALF), BF16),
        ((2, LANE, HALF), BF16),
        ((2, LANE, HALF), BF16),
        ((4, 4, HALF, WIDE), BF16),
        ((3, 4, HALF, WIDE), BF16),
        ((HALF, WIDE), F32),
        ((4, HALF, WIDE), BF16),
        ((3, HALF, WIDE), BF16),
        ((HALF, WIDE), BF16),
        ((WIDE, HALF), BF16),
        ((2, LANE, HALF), BF16),
        ((2, 4, LANE, ROWS), BF16),
        ((2, 3, LANE, ROWS), BF16),
        ((LANE, ROWS), BF16),
        ((LANE, ROWS), BF16),
        ((LANE, ROWS), BF16),
        ((LANE, ROWS), BF16),
        ((HALF, WIDE), BF16),
        ((HALF, WIDE), BF16),
    ]
    results = pl.pallas_call(
        kernel,
        out_shape=outs,
        in_specs=[anywhere] * 5,
        out_specs=[vmem] * 6,
        scratch_shapes=[pltpu.VMEM(dims, kind) for dims, kind in scratch]
        + [pltpu.SemaphoreType.DMA((SLOTS,))] * 2
        + [pltpu.SemaphoreType.DMA((6,)), pltpu.SemaphoreType.REGULAR],
        compiler_params=pltpu.CompilerParams(
            collective_id=0, has_side_effects=True, vmem_limit_bytes=53 * 2**20
        ),
    )(inputs, cotangent, weight.T, moment1.T, moment2.T)
    return tuple(one.T for one in results)


def solution(mesh):
    split = P("dp", "section")
    return jax.shard_map(
        per_device,
        mesh=mesh,
        in_specs=(P("dp", None), P("dp", None), split, split, split),
        out_specs=(split,) * 6,
        check_vma=False,
    )
```

```python
import math

import jax
import jax.numpy as jnp
from jax import lax
from jax.experimental import pallas as pl
from jax.experimental.pallas import tpu as pltpu
from jax.sharding import PartitionSpec as P

D = 3072
SECTIONS = 2
NORM_EPS = 1e-05
FIRST_FIX = 0.6513215599
SECOND_FIX = 0.4012630607
SCALE = 1.0 / math.sqrt(D)
HALF = 64
LANE = 96
PAIR = 192
WIDE = 256
ROWS = 384
F32 = jnp.float32
BF16 = jnp.bfloat16

PIECE = HALF // 2
PACK = 48
CUT = LANE // 3

W_Z, W_Y, W_ZY, W_C = 0, 3, 6, 15
X_UP, X_Z, X_X = 23, 25, 31
LOW, X2, SPARE, SLOPE = 63, 64, 65, 66
B_X, B_Z, R_X, R_Z = 67, 99, 105, 108
G_DOWN, G_C = 111, 113
G_YO, G_YS, G_Z, COPY = 114, 123, 126, 129
SLOTS = 130


def gelu_both(z):
    cdf = 0.5 * (1.0 + lax.erf(z * 0.7071067811865476))
    return z * cdf, cdf + z * jnp.exp(-0.5 * z * z) * 0.3989422804014327


def kernel(
    inputs, cotangent, w, m1, m2,
    spare, grad, new_w, new_m1, new_m2, copy,
    xin, cot, wv, m1v, m2v, wp, csum, low, xg, xout, normed, inv, mixed, slope_of, up, g_in,
    slope_t, sl, x2_t, x2, spare_in, bsend, halves, brecv, zacc, zsend, zrecv,
    rsend, rrecv, rzsend, rzrecv, gpack, gout, g_t, gc, gsend, grecv, gzs, gzr, copy_out, copy_in, slopes, x2_w,
    send_sem, recv_sem, here_sem, go,
):
    sec = lax.axis_index("section")
    dp = lax.axis_index("dp")
    c = sec % 2
    x = sec // 2 % 4
    s = sec // 32
    zq = sec // 8 % 4
    y = dp % 4
    zh = dp // 4
    odd = x % 2
    other = dp + 4 - 8 * zh
    core = {"section": sec + 1 - 2 * c, "dp": dp}
    across = {"section": sec + 32 - 64 * s, "dp": dp}
    far = {"section": sec, "dp": other}
    ys = [{"section": sec, "dp": zh * 4 + (y + j) % 4} for j in (1, 2, 3)]
    xs = [{"section": s * 32 + zq * 8 + (x + j) % 4 * 2 + c, "dp": dp} for j in (1, 2, 3)]
    zs = [{"section": s * 32 + (zq + j) % 4 * 8 + x * 2 + c, "dp": dp} for j in (1, 2, 3)]
    first = s == 0
    second = s == 1
    window = pl.ds(pl.multiple_of(zq * 768 + x // 2 * 384 + odd * 128, 128), WIDE)
    my_rows = pl.ds(pl.multiple_of(odd * 64 + c * LANE, 32), LANE)
    core_rows = pl.ds(pl.multiple_of(odd * 64 + (1 - c) * LANE, 32), LANE)

    def copier(slot, src, dst, to):
        return pltpu.make_async_remote_copy(
            src_ref=src,
            dst_ref=dst,
            send_sem=send_sem.at[slot],
            recv_sem=recv_sem.at[slot],
            device_id=to,
            device_id_type=pl.DeviceIdType.MESH,
        )

    def arrived(slot, where):
        copier(slot, where, where, core).wait_recv()

    def cols_of(replica):
        return pl.ds(pl.multiple_of(replica * ROWS, ROWS), ROWS)

    load_w = pltpu.make_async_copy(w, wv, here_sem.at[0])
    load_m1 = pltpu.make_async_copy(m1, m1v, here_sem.at[1])
    load_m2 = pltpu.make_async_copy(m2, m2v, here_sem.at[2])
    tokens = [pl.ds(pl.multiple_of(half * HALF, HALF), HALF) for half in (c, 1 - c)]
    load_x = [
        pltpu.make_async_copy(inputs.at[tokens[i]], xin.at[half], here_sem.at[3 + i])
        for i, half in enumerate((c, 1 - c))
    ]
    load_cot = pltpu.make_async_copy(cotangent.at[tokens[0], window], cot, here_sem.at[5])
    load_w.start()

    @pl.when(first)
    def _():
        for one in load_x:
            one.start()

    @pl.when(second)
    def _():
        load_cot.start()

    load_m1.start()
    load_m2.start()

    barrier = pltpu.get_barrier_semaphore()
    peers = [core, across, far] + ys + xs + zs
    for peer in peers:
        pl.semaphore_signal(barrier, inc=1, device_id=peer, device_id_type=pl.DeviceIdType.MESH)
    load_w.wait()
    pl.semaphore_wait(barrier, len(peers))

    pieces = [pl.ds(PIECE * t, PIECE) for t in range(2)]
    cuts = [pl.ds(CUT * t, CUT) for t in range(3)]
    my_cuts = [pl.ds(pl.multiple_of(odd * 64 + c * LANE + CUT * t, 32), CUT) for t in range(3)]

    w_far = [copier(W_Z + t, wv.at[cuts[t]], wp.at[my_cuts[t], cols_of(dp)], far) for t in range(3)]
    mine = wp.at[my_rows, cols_of(dp)]
    sent = [copier(W_Y + j, wv, mine, ys[j]) for j in range(3)]
    sent.append(copier(W_C, wv, mine, core))

    @pl.when(first)
    def _():
        for one in w_far:
            one.start()

    for one in sent:
        one.start()
    sent += w_far
    wp[my_rows, cols_of(dp)] = wv[...]
    blank = pl.ds(pl.multiple_of((1 - odd) * PAIR, 64), WIDE - PAIR)
    wp[blank, :] = jnp.zeros((WIDE - PAIR, D), BF16)

    def normalise(rows):
        centre = jnp.mean(rows, axis=1, keepdims=True)
        gap = rows - centre
        scale = lax.rsqrt(jnp.mean(gap * gap, axis=1, keepdims=True) + NORM_EPS)
        return (gap * scale).astype(BF16), centre, scale

    def keep_stats(rows, block, centre, scale):
        inv[rows, :] = jnp.broadcast_to(scale, (scale.shape[0], 128))
        normed[rows, :] = (block.astype(F32) - centre) * scale

    @pl.when(first)
    def _():
        load_x[0].wait()
        low[c], centre, scale = normalise(xin[c].astype(F32))
        keep_stats(slice(None), xin[c, :, window], centre, scale)

    def to_core(slot, replica):
        block = wp.at[my_rows, cols_of(replica)]
        one = copier(slot, block, block, core)
        one.start()
        sent.append(one)

    from_y = [zh * 4 + (y + 4 - j) % 4 for j in (1, 2, 3)]
    from_zy = [(1 - zh) * 4 + (y + 4 - j) % 4 for j in (1, 2, 3)]
    for j in range(3):
        arrived(W_Y + j, wp.at[my_rows, cols_of(from_y[j])])
        to_core(W_C + 2 + j, from_y[j])

    @pl.when(second)
    def _():
        pl.semaphore_wait(go, 1)
        for one in w_far:
            one.start()

    for t in range(3):
        held = wp.at[my_cuts[t], cols_of(other)]
        arrived(W_Z + t, held)
        for j in range(3):
            one = copier(W_ZY + 3 * t + j, held, held, ys[j])
            one.start()
            sent.append(one)

    @pl.when(first)
    def _():
        pl.semaphore_signal(go, inc=1, device_id=across, device_id_type=pl.DeviceIdType.MESH)

    to_core(W_C + 1, other)
    for j in range(3):
        for t in range(3):
            arrived(W_ZY + 3 * t + j, wp.at[my_cuts[t], cols_of(from_zy[j])])
        to_core(W_C + 5 + j, from_zy[j])
    for i, replica in enumerate([dp, other] + from_y + from_zy):
        arrived(W_C + i, wp.at[core_rows, cols_of(replica)])

    def column_sums():
        csum[...] = lax.dot_general(
            jnp.ones((16, D), BF16), wp[...], (((1,), (1,)), ((), ())), preferred_element_type=F32
        )

    left = lax.broadcasted_iota(jnp.int32, (PIECE, 128), 1) < 64
    left16 = lax.broadcasted_iota(jnp.int32, (16, 128), 1) < 64

    def turn(block):
        return pltpu.roll(block, 64, 1)

    def pack(full, shared, shift):
        turned = turn(shared)
        near, away = (turned, shared) if shift else (shared, turned)
        return jnp.concatenate([full, jnp.where(left16, near[:16], away[16:])], axis=0)

    def pack_own(wide):
        low_form = pack(wide[:, :128], wide[:, 128:], False)
        return jnp.where(odd == 0, low_form, pack(wide[:, 128:], wide[:, :128], True))

    def shared_part(packed, shift):
        end = packed[PIECE:]
        turned = turn(end)
        return jnp.concatenate([turned, end] if shift else [end, turned], axis=0)

    def unpack_own(packed):
        full = packed[:PIECE]
        low_form = jnp.concatenate([full, shared_part(packed, False)], axis=1)
        high_form = jnp.concatenate([shared_part(packed, True), full], axis=1)
        return jnp.where(odd == 0, low_form, high_form)

    upward = [pl.ds(0, 16 if i % 2 == 0 else 32) for i in range(4)]
    downward = [pl.ds(16, 32) if i % 2 == 0 else pl.ds(32, 16) for i in range(4)]
    ways = [(upward, xs[0]), (downward, xs[2])]

    own = [xg.at[x, zq, t] for t in range(2)]
    x_up = [copier(X_UP + t, xout.at[t], own[t], across) for t in range(2)]
    x_z = [copier(X_Z + 3 * t + j, own[t], own[t], zs[j]) for t in range(2) for j in range(3)]
    x_x = {}
    for t in range(2):
        for i in range(4):
            q = (zq + 4 - i) % 4
            for way in range(2):
                slot = X_X + 16 * t + 4 * i + way
                block = xg.at[x, q, t]
                x_x[t, i, way] = copier(slot, block, block, ways[way][1])
                part = xg.at[(x + 3 + 2 * way) % 4, q, t, ways[way][0][i]]
                x_x[t, i, way + 2] = copier(slot + 2, part, part, ways[way][1])
    swap_low = copier(LOW, low.at[c], low.at[c], core)

    @pl.when(second)
    def _():
        column_sums()
        for t in range(2):
            arrived(X_UP + t, own[t])
            for one in x_z[3 * t : 3 * t + 3] + [x_x[t, 0, 0], x_x[t, 0, 1]]:
                one.start()
        for t in range(2):
            for j in range(3):
                arrived(X_Z + 3 * t + j, xg.at[x, (zq + 3 - j) % 4, t])
                x_x[t, j + 1, 0].start()
                x_x[t, j + 1, 1].start()
        load_cot.wait()
        for t in range(2):
            for i in range(4):
                for way in range(2):
                    block = xg.at[(x + 3 + 2 * way) % 4, (zq + 4 - i) % 4, t]
                    arrived(X_X + 16 * t + 4 * i + way, block)
                    x_x[t, i, way + 2].start()

    def gathered(t):
        for i in range(4):
            for way in range(2):
                block = xg.at[(x + 2) % 4, (zq + 4 - i) % 4, t, ways[way][0][i]]
                arrived(X_X + 16 * t + 4 * i + way + 2, block)
        rows = pieces[t]
        parts = []
        for m in range(8):
            even = xg[m % 2 * 2, m // 2, t].astype(F32)
            late = xg[m % 2 * 2 + 1, m // 2, t].astype(F32)
            middle = jnp.where(left, shared_part(even, False), shared_part(late, True))
            parts += [even[:PIECE], middle, late[:PIECE]]
        low[c, rows], centre, scale = normalise(jnp.concatenate(parts, axis=1))
        keep_stats(rows, unpack_own(xg[x, zq, t].astype(F32)), centre, scale)

    def find_slope(rows, upstream):
        up[rows, :] = upstream.astype(F32)
        slopes[rows, :] = (up[rows, :] * slope_of[rows, :]).astype(BF16)

    b_x = {}
    for t in range(2):
        for i in range(4):
            q = (zq + 1 + i) % 4
            for way in range(2):
                slot = B_X + 16 * t + 4 * i + way
                rows, to = ways[way][0][i], ways[way][1]
                opposite = bsend.at[(x + 2) % 4, q, t, rows]
                b_x[t, i, way] = copier(slot, opposite, halves.at[way, q, t, rows], to)
                block = bsend.at[(x + 1 + 2 * way) % 4, q, t]
                b_x[t, i, way + 2] = copier(slot + 2, block, brecv.at[way, q, t], to)

    def back(t):
        slope = slopes[pieces[t], :]
        for i in range(4):
            q = (zq + 1 + i) % 4
            for half in range(2):
                cols = pl.ds(pl.multiple_of(q * 768 + half * 384, 384), 384)
                part = SCALE * jnp.dot(slope, wp[:, cols], preferred_element_type=F32)
                middle = part[:, 128:256]
                bsend[2 * half, q, t] = pack(part[:, :128], middle, False).astype(BF16)
                bsend[2 * half + 1, q, t] = pack(part[:, 256:], middle, True).astype(BF16)
            b_x[t, i, 0].start()
            b_x[t, i, 1].start()

    r_x = [copier(R_X + j, rsend, rrecv.at[j], xs[j]) for j in range(3)]
    r_z = [copier(R_Z + j, rzsend, rzrecv.at[j], zs[j]) for j in range(3)]

    def give_sums():
        wide = slopes[...].astype(F32)
        r1 = jnp.sum(wide * csum[0:1, :], axis=1, keepdims=True) * (SCALE / D)
        r2 = jnp.sum(wide * mixed[...], axis=1, keepdims=True) * (1.0 / D)
        spot = lax.broadcasted_iota(jnp.int32, (HALF, 128), 1)
        both = jnp.where(spot == 0, r1, jnp.where(spot == 1, r2, 0.0))
        both = jnp.concatenate([both, jnp.zeros((128 - HALF, 128), F32)], axis=0)
        rsend[...] = both.T[:8, :]
        for one in r_x:
            one.start()

    def pass_terms():
        for t in range(2):
            for i in range(4):
                q = (zq + 1 + i) % 4
                for way in range(2):
                    rows = ways[way][0][i]
                    to = (x + 1 + 2 * way) % 4
                    arrived(B_X + 16 * t + 4 * i + way, halves.at[way, q, t, rows])
                    mine = bsend[to, q, t, rows].astype(F32)
                    mine = mine + halves[way, q, t, rows].astype(F32)
                    bsend[to, q, t, rows] = mine.astype(BF16)
                    b_x[t, i, way + 2].start()

    for t in range(2):
        rows = pieces[t]

        @pl.when(second)
        def _():
            gathered(t)

        z = SCALE * lax.dot_general(
            low[c, rows], wp[...], (((1,), (1,)), ((), ())), preferred_element_type=F32
        )
        value, slope_value = gelu_both(z)
        mixed[rows, :] = z
        slope_of[rows, :] = slope_value

        @pl.when(first)
        def _():
            xout[t] = pack_own(xin[c, rows, window].astype(F32) + value).astype(BF16)
            x_up[t].start()

        @pl.when(second)
        def _():
            find_slope(rows, cot[rows, :])
            back(t)
            x2_w[rows, :] = (unpack_own(xg[x, zq, t].astype(F32)) + value).astype(BF16)

    @pl.when(first)
    def _():
        load_x[1].wait()
        low[1 - c], _, _ = normalise(xin[1 - c].astype(F32))
        column_sums()
        for t in range(2):
            arrived(G_DOWN + t, g_in.at[t])
            find_slope(pieces[t], unpack_own(g_in[t].astype(F32)))

    swap_slope = copier(SLOPE, slope_t.at[core_rows], sl.at[c], core)
    slope_t[...] = slopes[...].T
    swap_slope.start()
    sl[c] = slope_t[my_rows, :]
    swap_x2 = copier(X2, x2_t.at[core_rows], x2.at[c], core)

    @pl.when(second)
    def _():
        give_sums()
        pass_terms()
        swap_low.start()
        x2_t[...] = x2_w[...].T
        swap_x2.start()
        x2[c] = x2_t[my_rows, :]
        arrived(LOW, low.at[1 - c])

    arrived(SLOPE, sl.at[1 - c])
    whole = jnp.concatenate([sl[0], sl[1]], axis=1)
    g_y = []
    for i, half in enumerate((1 - zh, zh)):
        for j in range(4):
            to = (y + 1 + j) % 4
            cols = cols_of(half * 4 + to)
            rows = low[:, :, cols].reshape(2 * HALF, ROWS)
            part = jnp.dot(whole, rows, preferred_element_type=F32)
            gsend[half, to] = (part * SCALE).astype(BF16)
            if j < 3:
                if i == 0:
                    some = [
                        copier(
                            G_YO + 3 * j + t,
                            gsend.at[half, to, cuts[t]],
                            grecv.at[i, j, cuts[t]],
                            ys[j],
                        )
                        for t in range(3)
                    ]
                else:
                    some = [copier(G_YS + j, gsend.at[half, to], grecv.at[i, j], ys[j])]
                for one in some:
                    one.start()
                g_y += some

    send_far = [copier(G_Z + t, gzs.at[cuts[t]], gzr.at[cuts[t]], far) for t in range(3)]

    def reduce_far():
        for t in range(3):
            total = gsend[1 - zh, y, cuts[t]].astype(F32)
            for j in range(3):
                arrived(G_YO + 3 * j + t, grecv.at[0, j, cuts[t]])
                total = total + grecv[0, j, cuts[t]].astype(F32)
            gzs[cuts[t], :] = total.astype(BF16)
            send_far[t].start()

    @pl.when(first)
    def _():
        back(0)
        back(1)
        give_sums()
        reduce_far()
        pass_terms()

    b_z = []
    for t in range(2):
        for i in range(4):
            q = (zq + 1 + i) % 4
            total = bsend[x, q, t].astype(F32)
            for way in range(2):
                arrived(B_X + 16 * t + 4 * i + way + 2, brecv.at[way, q, t])
                total = total + brecv[way, q, t].astype(F32)
            if i < 3:
                zsend[q, t] = total.astype(BF16)
                one = copier(B_Z + 3 * t + i, zsend.at[q, t], zrecv.at[i, t], zs[i])
                one.start()
                b_z.append(one)
            else:
                zacc[t] = total
        if t == 0:
            sums = rsend[...]
            for j in range(3):
                arrived(R_X + j, rrecv.at[j])
                sums = sums + rrecv[j]
            rzsend[...] = sums
            for one in r_z:
                one.start()

    sums = rzsend[...]
    for j in range(3):
        arrived(R_Z + j, rzrecv.at[j])
        sums = sums + rzrecv[j]
    sums = jnp.concatenate([sums, jnp.zeros((120, 128), F32)], axis=0).T
    g_down = [copier(G_DOWN + t, gpack.at[t], g_in.at[t], across) for t in range(2)]
    for t in range(2):
        rows = pieces[t]
        total = zacc[t]
        for j in range(3):
            arrived(B_Z + 3 * t + j, zrecv.at[j, t])
            total = total + zrecv[j, t].astype(F32)
        r1 = sums[PIECE * t : PIECE * t + PIECE, 0:1]
        r2 = sums[PIECE * t : PIECE * t + PIECE, 1:2]
        change = inv[rows, 0:1] * (unpack_own(total) - r1 - normed[rows, :] * r2)
        renewed = up[rows, :] + change
        gout[rows, :] = renewed.astype(BF16)

        @pl.when(second)
        def _():
            gpack[t] = pack_own(renewed).astype(BF16)
            g_down[t].start()

    @pl.when(second)
    def _():
        reduce_far()

    g_t[...] = gout[...].T
    swap_g = copier(G_C, g_t.at[core_rows], gc.at[c], core)
    swap_g.start()
    gc[c] = g_t[my_rows, :]

    send_spare = copier(SPARE, x2, spare_in, across)

    @pl.when(second)
    def _():
        arrived(X2, x2.at[1 - c])
        send_spare.start()

    total = gsend[zh, y].astype(F32)
    for j in range(3):
        arrived(G_YS + j, grecv.at[1, j])
        total = total + grecv[1, j].astype(F32)
    load_m1.wait()
    load_m2.wait()
    for t in range(3):
        arrived(G_Z + t, gzr.at[cuts[t]])
    gradient = total + gzr[...].astype(F32)
    moment1 = 0.9 * m1v[...] + 0.1 * gradient
    moment2 = 0.95 * m2v[...] + 0.05 * gradient * gradient
    update = moment1 / FIRST_FIX / (jnp.sqrt(moment2 / SECOND_FIX) + 1e-08)
    plain = wv[...].astype(F32)
    stepped = (plain - 0.05 * (update + 0.1 * plain)).astype(BF16)
    copy_out[...] = stepped
    send_copy = copier(COPY, copy_out, copy_in, across)

    @pl.when(second)
    def _():
        send_copy.start()
        spare[...] = jnp.zeros_like(spare)
        copy[...] = jnp.zeros_like(copy)

    new_m1[...] = moment1
    new_m2[...] = moment2
    new_w[...] = stepped

    arrived(G_C, gc.at[1 - c])
    grad[...] = jnp.concatenate([gc[0], gc[1]], axis=1)

    @pl.when(first)
    def _():
        arrived(SPARE, spare_in)
        spare[...] = jnp.concatenate([spare_in[0], spare_in[1]], axis=1)
        arrived(COPY, copy_in)
        copy[...] = copy_in[...]
        for one in x_up:
            one.wait_send()

    for one in sent + [swap_slope, swap_g] + send_far + list(b_x.values()) + b_z + g_y + r_x + r_z:
        one.wait_send()

    @pl.when(second)
    def _():
        for one in x_z + list(x_x.values()) + g_down + [swap_low, swap_x2, send_spare, send_copy]:
            one.wait_send()


def per_device(inputs, cotangent, weight, moment1, moment2):
    vmem = pl.BlockSpec(memory_space=pltpu.VMEM)
    anywhere = pl.BlockSpec(memory_space=pl.ANY)
    shape = jax.ShapeDtypeStruct
    outs = [
        shape((LANE, 2 * HALF), BF16),
        shape((LANE, 2 * HALF), BF16),
        shape((LANE, ROWS), BF16),
        shape((LANE, ROWS), F32),
        shape((LANE, ROWS), F32),
        shape((LANE, ROWS), BF16),
    ]
    scratch = [
        ((2, HALF, D), BF16),
        ((HALF, WIDE), BF16),
        ((LANE, ROWS), BF16),
        ((LANE, ROWS), F32),
        ((LANE, ROWS), F32),
        ((WIDE, D), BF16),
        ((16, WIDE), F32),
        ((2, HALF, D), BF16),
        ((4, 4, 2, PACK, 128), BF16),
        ((2, PACK, 128), BF16),
        ((HALF, WIDE), F32),
        ((HALF, 128), F32),
        ((HALF, WIDE), F32),
        ((HALF, WIDE), F32),
        ((HALF, WIDE), F32),
        ((2, PACK, 128), BF16),
        ((WIDE, HALF), BF16),
        ((2, LANE, HALF), BF16),
        ((WIDE, HALF), BF16),
        ((2, LANE, HALF), BF16),
        ((2, LANE, HALF), BF16),
        ((4, 4, 2, PACK, 128), BF16),
        ((2, 4, 2, PACK, 128), BF16),
        ((2, 4, 2, PACK, 128), BF16),
        ((2, PACK, 128), F32),
        ((4, 2, PACK, 128), BF16),
        ((3, 2, PACK, 128), BF16),
        ((8, 128), F32),
        ((3, 8, 128), F32),
        ((8, 128), F32),
        ((3, 8, 128), F32),
        ((2, PACK, 128), BF16),
        ((HALF, WIDE), BF16),
        ((WIDE, HALF), BF16),
        ((2, LANE, HALF), BF16),
        ((2, 4, LANE, ROWS), BF16),
        ((2, 3, LANE, ROWS), BF16),
        ((LANE, ROWS), BF16),
        ((LANE, ROWS), BF16),
        ((LANE, ROWS), BF16),
        ((LANE, ROWS), BF16),
        ((HALF, WIDE), BF16),
        ((HALF, WIDE), BF16),
    ]
    results = pl.pallas_call(
        kernel,
        out_shape=outs,
        in_specs=[anywhere] * 5,
        out_specs=[vmem] * 6,
        scratch_shapes=[pltpu.VMEM(dims, kind) for dims, kind in scratch]
        + [pltpu.SemaphoreType.DMA((SLOTS,))] * 2
        + [pltpu.SemaphoreType.DMA((6,)), pltpu.SemaphoreType.REGULAR],
        compiler_params=pltpu.CompilerParams(
            collective_id=0, has_side_effects=True, vmem_limit_bytes=54656 * 2**10
        ),
    )(inputs, cotangent, weight.T, moment1.T, moment2.T)
    return tuple(one.T for one in results)


def solution(mesh):
    split = P("dp", "section")
    return jax.shard_map(
        per_device,
        mesh=mesh,
        in_specs=(P("dp", None), P("dp", None), split, split, split),
        out_specs=(split,) * 6,
        check_vma=False,
    )
```

```python
import math

import jax
import jax.numpy as jnp
from jax import lax
from jax.experimental import pallas as pl
from jax.experimental.pallas import tpu as pltpu
from jax.sharding import PartitionSpec as P

D = 3072
SECTIONS = 2
NORM_EPS = 1e-05
FIRST_FIX = 0.6513215599
SECOND_FIX = 0.4012630607
SCALE = 1.0 / math.sqrt(D)
HALF = 64
LANE = 96
PAIR = 192
WIDE = 256
ROWS = 384
F32 = jnp.float32
BF16 = jnp.bfloat16

PIECE = HALF // 2
PACK = 48
CUT = LANE // 3

W_Z, W_Y, W_ZY, W_C = 0, 3, 6, 15
X_UP, X_Z, X_X = 23, 25, 31
LOW, X2, SPARE, SLOPE = 55, 56, 57, 58
B_X, B_Z, R_X, R_Z = 59, 83, 89, 92
G_DOWN, G_C = 95, 97
G_YO, G_YS, G_Z, COPY = 98, 107, 110, 113
S_Y, L_Y = 114, 121
SLOTS = 127


def gelu_both(z):
    cdf = 0.5 * (1.0 + lax.erf(z * 0.7071067811865476))
    return z * cdf, cdf + z * jnp.exp(-0.5 * z * z) * 0.3989422804014327


def kernel(
    inputs, cotangent, w, m1, m2,
    spare, grad, new_w, new_m1, new_m2, copy,
    xin, cot, wv, m1v, m2v, wp, csum, low, xg, xout, normed, inv, mixed, slope_of, up, g_in,
    slope_t, sl, x2_t, x2, spare_in, bsend, brecv, zacc, zsend, zrecv,
    rsend, rrecv, rzsend, rzrecv, gpack, gout, g_t, gc, gsend, grecv, gzs, gzr, copy_out, copy_in, slopes, x2_w,
    spack, sg, lowx, gown,
    send_sem, recv_sem, here_sem, go,
):
    sec = lax.axis_index("section")
    dp = lax.axis_index("dp")
    c = sec % 2
    x = sec // 2 % 4
    s = sec // 32
    zq = sec // 8 % 4
    y = dp % 4
    zh = dp // 4
    odd = x % 2
    other = dp + 4 - 8 * zh
    core = {"section": sec + 1 - 2 * c, "dp": dp}
    across = {"section": sec + 32 - 64 * s, "dp": dp}
    far = {"section": sec, "dp": other}
    ys = [{"section": sec, "dp": zh * 4 + (y + j) % 4} for j in (1, 2, 3)]
    xs = [{"section": s * 32 + zq * 8 + (x + j) % 4 * 2 + c, "dp": dp} for j in (1, 2, 3)]
    zs = [{"section": s * 32 + (zq + j) % 4 * 8 + x * 2 + c, "dp": dp} for j in (1, 2, 3)]
    first = s == 0
    second = s == 1
    window = pl.ds(pl.multiple_of(zq * 768 + x // 2 * 384 + odd * 128, 128), WIDE)
    my_rows = pl.ds(pl.multiple_of(odd * 64 + c * LANE, 32), LANE)
    core_rows = pl.ds(pl.multiple_of(odd * 64 + (1 - c) * LANE, 32), LANE)

    def copier(slot, src, dst, to):
        return pltpu.make_async_remote_copy(
            src_ref=src,
            dst_ref=dst,
            send_sem=send_sem.at[slot],
            recv_sem=recv_sem.at[slot],
            device_id=to,
            device_id_type=pl.DeviceIdType.MESH,
        )

    def arrived(slot, where):
        copier(slot, where, where, core).wait_recv()

    def cols_of(replica):
        return pl.ds(pl.multiple_of(replica * ROWS, ROWS), ROWS)

    load_w = pltpu.make_async_copy(w, wv, here_sem.at[0])
    load_m1 = pltpu.make_async_copy(m1, m1v, here_sem.at[1])
    load_m2 = pltpu.make_async_copy(m2, m2v, here_sem.at[2])
    tokens = [pl.ds(pl.multiple_of(half * HALF, HALF), HALF) for half in (c, 1 - c)]
    load_x = [
        pltpu.make_async_copy(inputs.at[tokens[i]], xin.at[half], here_sem.at[3 + i])
        for i, half in enumerate((c, 1 - c))
    ]
    load_cot = pltpu.make_async_copy(cotangent.at[tokens[0], window], cot, here_sem.at[5])
    load_w.start()

    @pl.when(first)
    def _():
        for one in load_x:
            one.start()

    @pl.when(second)
    def _():
        load_cot.start()

    load_m1.start()
    load_m2.start()

    barrier = pltpu.get_barrier_semaphore()
    ys_core = [{"section": core["section"], "dp": one["dp"]} for one in ys]
    peers = [core, across, far] + ys + ys_core + xs + zs
    for peer in peers:
        pl.semaphore_signal(barrier, inc=1, device_id=peer, device_id_type=pl.DeviceIdType.MESH)
    load_w.wait()
    pl.semaphore_wait(barrier, len(peers))

    pieces = [pl.ds(PIECE * t, PIECE) for t in range(2)]
    cuts = [pl.ds(CUT * t, CUT) for t in range(3)]
    my_cuts = [pl.ds(pl.multiple_of(odd * 64 + c * LANE + CUT * t, 32), CUT) for t in range(3)]

    w_far = [copier(W_Z + t, wv.at[cuts[t]], wp.at[my_cuts[t], cols_of(dp)], far) for t in range(3)]
    mine = wp.at[my_rows, cols_of(dp)]
    sent = [copier(W_Y + j, wv, mine, ys[j]) for j in range(3)]
    sent.append(copier(W_C, wv, mine, core))

    @pl.when(first)
    def _():
        for one in w_far:
            one.start()

    for one in sent:
        one.start()
    sent += w_far
    wp[my_rows, cols_of(dp)] = wv[...]
    blank = pl.ds(pl.multiple_of((1 - odd) * PAIR, 64), WIDE - PAIR)
    wp[blank, :] = jnp.zeros((WIDE - PAIR, D), BF16)

    def normalise(rows):
        centre = jnp.mean(rows, axis=1, keepdims=True)
        gap = rows - centre
        scale = lax.rsqrt(jnp.mean(gap * gap, axis=1, keepdims=True) + NORM_EPS)
        return (gap * scale).astype(BF16), centre, scale

    def keep_stats(rows, block, centre, scale):
        inv[rows, :] = jnp.broadcast_to(scale, (scale.shape[0], 128))
        normed[rows, :] = (block.astype(F32) - centre) * scale

    @pl.when(first)
    def _():
        load_x[0].wait()
        low[c], centre, scale = normalise(xin[c].astype(F32))
        keep_stats(slice(None), xin[c, :, window], centre, scale)

    def to_core(slot, replica):
        block = wp.at[my_rows, cols_of(replica)]
        one = copier(slot, block, block, core)
        one.start()
        sent.append(one)

    from_y = [zh * 4 + (y + 4 - j) % 4 for j in (1, 2, 3)]
    from_zy = [(1 - zh) * 4 + (y + 4 - j) % 4 for j in (1, 2, 3)]
    for j in range(3):
        arrived(W_Y + j, wp.at[my_rows, cols_of(from_y[j])])
        to_core(W_C + 2 + j, from_y[j])

    @pl.when(second)
    def _():
        pl.semaphore_wait(go, 1)
        for one in w_far:
            one.start()

    for t in range(3):
        held = wp.at[my_cuts[t], cols_of(other)]
        arrived(W_Z + t, held)
        for j in range(3):
            one = copier(W_ZY + 3 * t + j, held, held, ys[j])
            one.start()
            sent.append(one)

    @pl.when(first)
    def _():
        pl.semaphore_signal(go, inc=1, device_id=across, device_id_type=pl.DeviceIdType.MESH)

    to_core(W_C + 1, other)
    for j in range(3):
        for t in range(3):
            arrived(W_ZY + 3 * t + j, wp.at[my_cuts[t], cols_of(from_zy[j])])
        to_core(W_C + 5 + j, from_zy[j])
    for i, replica in enumerate([dp, other] + from_y + from_zy):
        arrived(W_C + i, wp.at[core_rows, cols_of(replica)])

    def column_sums():
        csum[...] = lax.dot_general(
            jnp.ones((16, D), BF16), wp[...], (((1,), (1,)), ((), ())), preferred_element_type=F32
        )

    left = lax.broadcasted_iota(jnp.int32, (PIECE, 128), 1) < 64
    left16 = lax.broadcasted_iota(jnp.int32, (16, 128), 1) < 64

    def turn(block):
        return pltpu.roll(block, 64, 1)

    def pack(full, shared, shift):
        turned = turn(shared)
        near, away = (turned, shared) if shift else (shared, turned)
        return jnp.concatenate([full, jnp.where(left16, near[:16], away[16:])], axis=0)

    def pack_own(wide):
        low_form = pack(wide[:, :128], wide[:, 128:], False)
        return jnp.where(odd == 0, low_form, pack(wide[:, 128:], wide[:, :128], True))

    def shared_part(packed, shift):
        end = packed[PIECE:]
        turned = turn(end)
        return jnp.concatenate([turned, end] if shift else [end, turned], axis=0)

    def unpack_own(packed):
        full = packed[:PIECE]
        low_form = jnp.concatenate([full, shared_part(packed, False)], axis=1)
        high_form = jnp.concatenate([shared_part(packed, True), full], axis=1)
        return jnp.where(odd == 0, low_form, high_form)

    own = [xg.at[x, zq, t] for t in range(2)]
    x_up = [copier(X_UP + t, xout.at[t], own[t], across) for t in range(2)]
    x_z = [copier(X_Z + 3 * t + j, own[t], own[t], zs[j]) for t in range(2) for j in range(3)]
    x_x = {}
    for t in range(2):
        for i in range(4):
            block = xg.at[x, (zq + 4 - i) % 4, t]
            for j in range(3):
                x_x[t, i, j] = copier(X_X + 12 * t + 3 * i + j, block, block, xs[j])
    swap_low = copier(LOW, low.at[c], low.at[c], core)

    @pl.when(second)
    def _():
        column_sums()
        for t in range(2):
            arrived(X_UP + t, own[t])
            for one in x_z[3 * t : 3 * t + 3] + [x_x[t, 0, j] for j in range(3)]:
                one.start()
        for t in range(2):
            for j in range(3):
                arrived(X_Z + 3 * t + j, xg.at[x, (zq + 3 - j) % 4, t])
                for k in range(3):
                    x_x[t, j + 1, k].start()
        load_cot.wait()

    def gathered(t):
        for i in range(4):
            for j in range(3):
                block = xg.at[(x + 3 - j) % 4, (zq + 4 - i) % 4, t]
                arrived(X_X + 12 * t + 3 * i + j, block)
        rows = pieces[t]
        parts = []
        for m in range(8):
            even = xg[m % 2 * 2, m // 2, t].astype(F32)
            late = xg[m % 2 * 2 + 1, m // 2, t].astype(F32)
            middle = jnp.where(left, shared_part(even, False), shared_part(late, True))
            parts += [even[:PIECE], middle, late[:PIECE]]
        low[c, rows], centre, scale = normalise(jnp.concatenate(parts, axis=1))
        keep_stats(rows, unpack_own(xg[x, zq, t].astype(F32)), centre, scale)

    def find_slope(rows, upstream):
        up[rows, :] = upstream.astype(F32)
        slopes[rows, :] = (up[rows, :] * slope_of[rows, :]).astype(BF16)

    b_x = {}
    for t in range(2):
        for i in range(4):
            q = (zq + 1 + i) % 4
            for j in range(3):
                block = bsend.at[(x + 1 + j) % 4, q, t]
                b_x[t, i, j] = copier(B_X + 12 * t + 3 * i + j, block, brecv.at[j, q, t], xs[j])

    def back(t):
        slope = slopes[pieces[t], :]
        for i in range(4):
            q = (zq + 1 + i) % 4
            for half in range(2):
                cols = pl.ds(pl.multiple_of(q * 768 + half * 384, 384), 384)
                part = SCALE * jnp.dot(slope, wp[:, cols], preferred_element_type=F32)
                middle = part[:, 128:256]
                bsend[2 * half, q, t] = pack(part[:, :128], middle, False).astype(BF16)
                bsend[2 * half + 1, q, t] = pack(part[:, 256:], middle, True).astype(BF16)
            for j in range(3):
                b_x[t, i, j].start()

    r_x = [copier(R_X + j, rsend, rrecv.at[j], xs[j]) for j in range(3)]
    r_z = [copier(R_Z + j, rzsend, rzrecv.at[j], zs[j]) for j in range(3)]

    def give_sums():
        wide = slopes[...].astype(F32)
        r1 = jnp.sum(wide * csum[0:1, :], axis=1, keepdims=True) * (SCALE / D)
        r2 = jnp.sum(wide * mixed[...], axis=1, keepdims=True) * (1.0 / D)
        spot = lax.broadcasted_iota(jnp.int32, (HALF, 128), 1)
        both = jnp.where(spot == 0, r1, jnp.where(spot == 1, r2, 0.0))
        both = jnp.concatenate([both, jnp.zeros((128 - HALF, 128), F32)], axis=0)
        rsend[...] = both.T[:8, :]
        for one in r_x:
            one.start()

    low_y = {}
    for i, half in enumerate((1 - zh, zh)):
        for j in range(3):
            cols = cols_of(half * 4 + (y + 1 + j) % 4)
            low_y[i, j] = copier(L_Y + 3 * i + j, low.at[:, :, cols], lowx.at[i, y], ys[j])

    for t in range(2):
        rows = pieces[t]

        @pl.when(second)
        def _():
            gathered(t)

        z = SCALE * lax.dot_general(
            low[c, rows], wp[...], (((1,), (1,)), ((), ())), preferred_element_type=F32
        )
        value, slope_value = gelu_both(z)
        mixed[rows, :] = z
        slope_of[rows, :] = slope_value

        @pl.when(first)
        def _():
            xout[t] = pack_own(xin[c, rows, window].astype(F32) + value).astype(BF16)
            x_up[t].start()

        @pl.when(second)
        def _():
            find_slope(rows, cot[rows, :])
            back(t)
            x2_w[rows, :] = (unpack_own(xg[x, zq, t].astype(F32)) + value).astype(BF16)

    @pl.when(first)
    def _():
        load_x[1].wait()
        low[1 - c], _, _ = normalise(xin[1 - c].astype(F32))
        for one in low_y.values():
            one.start()
        for i, half in enumerate((1 - zh, zh)):
            lowx[i, y] = low[:, :, cols_of(half * 4 + y)]
        column_sums()
        for t in range(2):
            arrived(G_DOWN + t, g_in.at[t])
            find_slope(pieces[t], unpack_own(g_in[t].astype(F32)))
            back(t)

    give_sums()
    slope_t[...] = slopes[...].T
    swap_slope = copier(SLOPE, slope_t.at[core_rows], sl.at[c], core)
    swap_x2 = copier(X2, x2_t.at[core_rows], x2.at[c], core)
    send_far = [copier(G_Z + t, gzs.at[cuts[t]], gzr.at[cuts[t]], far) for t in range(3)]

    def reduce_far():
        for t in range(3):
            total = gsend[1 - zh, y, cuts[t]].astype(F32)
            for j in range(3):
                arrived(G_YO + 3 * j + t, grecv.at[0, j, cuts[t]])
                total = total + grecv[0, j, cuts[t]].astype(F32)
            gzs[cuts[t], :] = total.astype(BF16)
            send_far[t].start()

    g_y = []
    for i, half in enumerate((1 - zh, zh)):
        for j in range(3):
            to = (y + 1 + j) % 4
            if i == 0:
                g_y += [
                    copier(
                        G_YO + 3 * j + t,
                        gsend.at[half, to, cuts[t]],
                        grecv.at[i, j, cuts[t]],
                        ys[j],
                    )
                    for t in range(3)
                ]
            else:
                g_y.append(copier(G_YS + j, gsend.at[half, to], grecv.at[i, j], ys[j]))

    @pl.when(second)
    def _():
        swap_slope.start()
        sl[c] = slope_t[my_rows, :]
        swap_low.start()
        x2_t[...] = x2_w[...].T
        swap_x2.start()
        x2[c] = x2_t[my_rows, :]
        arrived(LOW, low.at[1 - c])
        arrived(SLOPE, sl.at[1 - c])
        whole = jnp.concatenate([sl[0], sl[1]], axis=1)
        for i, half in enumerate((1 - zh, zh)):
            for j in range(4):
                to = (y + 1 + j) % 4
                rows = low[:, :, cols_of(half * 4 + to)].reshape(2 * HALF, ROWS)
                part = jnp.dot(whole, rows, preferred_element_type=F32)
                gsend[half, to] = (part * SCALE).astype(BF16)
                if j < 3:
                    for one in g_y[3 * j : 3 * j + 3] if i == 0 else g_y[9 + j : 10 + j]:
                        one.start()

    s_y = {}
    for flip in range(2):
        for dy in range(4):
            if flip + dy:
                to = core if dy == 0 else (ys_core if flip else ys)[dy - 1]
                s_y[flip, dy] = copier(S_Y + 2 * dy + flip - 1, spack.at[flip], sg.at[y, c], to)

    @pl.when(first)
    def _():
        for flip, rows in enumerate((my_rows, core_rows)):
            block = slope_t[rows, :]
            spack[flip] = jnp.concatenate([block[:48], block[48:]], axis=1)
        for one in s_y.values():
            one.start()
        sg[y, c] = spack[0]
        for i in range(2):
            for j in range(3):
                arrived(L_Y + 3 * i + j, lowx.at[i, (y + 3 - j) % 4])
        for dy in range(4):
            for flip in range(2):
                if flip + dy:
                    block = sg.at[(y + 4 - dy) % 4, c + flip - 2 * c * flip]
                    arrived(S_Y + 2 * dy + flip - 1, block)
        left48 = lax.broadcasted_iota(jnp.int32, (PACK, 128), 1) < 64
        parts = []
        for k in range(4):
            even, late = sg[k, 0].astype(F32), sg[k, 1].astype(F32)
            upper = jnp.where(left48, even, turn(late))
            lower = jnp.where(left48, turn(even), late)
            parts.append(jnp.concatenate([upper, lower], axis=0).astype(BF16))
        whole = jnp.concatenate(parts, axis=1)
        part = jnp.dot(whole, lowx[0].reshape(8 * HALF, ROWS), preferred_element_type=F32)
        gzs[...] = (part * SCALE).astype(BF16)
        for one in send_far:
            one.start()
        part = jnp.dot(whole, lowx[1].reshape(8 * HALF, ROWS), preferred_element_type=F32)
        gown[...] = part * SCALE

    b_z = []
    for t in range(2):
        for i in range(4):
            q = (zq + 1 + i) % 4
            total = bsend[x, q, t].astype(F32)
            for j in range(3):
                arrived(B_X + 12 * t + 3 * i + j, brecv.at[j, q, t])
                total = total + brecv[j, q, t].astype(F32)
            if i < 3:
                zsend[q, t] = total.astype(BF16)
                one = copier(B_Z + 3 * t + i, zsend.at[q, t], zrecv.at[i, t], zs[i])
                one.start()
                b_z.append(one)
            else:
                zacc[t] = total
        if t == 0:
            sums = rsend[...]
            for j in range(3):
                arrived(R_X + j, rrecv.at[j])
                sums = sums + rrecv[j]
            rzsend[...] = sums
            for one in r_z:
                one.start()

    sums = rzsend[...]
    for j in range(3):
        arrived(R_Z + j, rzrecv.at[j])
        sums = sums + rzrecv[j]
    sums = jnp.concatenate([sums, jnp.zeros((120, 128), F32)], axis=0).T
    g_down = [copier(G_DOWN + t, gpack.at[t], g_in.at[t], across) for t in range(2)]
    for t in range(2):
        rows = pieces[t]
        total = zacc[t]
        for j in range(3):
            arrived(B_Z + 3 * t + j, zrecv.at[j, t])
            total = total + zrecv[j, t].astype(F32)
        r1 = sums[PIECE * t : PIECE * t + PIECE, 0:1]
        r2 = sums[PIECE * t : PIECE * t + PIECE, 1:2]
        change = inv[rows, 0:1] * (unpack_own(total) - r1 - normed[rows, :] * r2)
        renewed = up[rows, :] + change
        gout[rows, :] = renewed.astype(BF16)

        @pl.when(second)
        def _():
            gpack[t] = pack_own(renewed).astype(BF16)
            g_down[t].start()

    @pl.when(second)
    def _():
        reduce_far()

    g_t[...] = gout[...].T
    swap_g = copier(G_C, g_t.at[core_rows], gc.at[c], core)
    swap_g.start()
    gc[c] = g_t[my_rows, :]

    send_spare = copier(SPARE, x2, spare_in, across)

    @pl.when(second)
    def _():
        arrived(X2, x2.at[1 - c])
        send_spare.start()

        total = gsend[zh, y].astype(F32)
        for j in range(3):
            arrived(G_YS + j, grecv.at[1, j])
            total = total + grecv[1, j].astype(F32)
        gown[...] = total
        spare[...] = jnp.zeros_like(spare)
        copy[...] = jnp.zeros_like(copy)

    @pl.when(first)
    def _():
        arrived(SPARE, spare_in)
        spare[...] = jnp.concatenate([spare_in[0], spare_in[1]], axis=1)
        arrived(COPY, copy_in)
        copy[...] = copy_in[...]
        for one in x_up + list(low_y.values()) + list(s_y.values()):
            one.wait_send()

    for one in sent + list(b_x.values()) + b_z + r_x + r_z:
        one.wait_send()

    @pl.when(second)
    def _():
        for one in x_z + list(x_x.values()) + g_down + g_y:
            one.wait_send()
        for one in (swap_slope, swap_low, swap_x2, send_spare):
            one.wait_send()

    arrived(G_C, gc.at[1 - c])
    grad[...] = jnp.concatenate([gc[0], gc[1]], axis=1)
    swap_g.wait_send()

    load_m1.wait()
    load_m2.wait()
    for t in range(3):
        arrived(G_Z + t, gzr.at[cuts[t]])
    gradient = gown[...] + gzr[...].astype(F32)
    moment1 = 0.9 * m1v[...] + 0.1 * gradient
    moment2 = 0.95 * m2v[...] + 0.05 * gradient * gradient
    update = moment1 / FIRST_FIX / (jnp.sqrt(moment2 / SECOND_FIX) + 1e-08)
    plain = wv[...].astype(F32)
    stepped = (plain - 0.05 * (update + 0.1 * plain)).astype(BF16)
    copy_out[...] = stepped
    send_copy = copier(COPY, copy_out, copy_in, across)

    @pl.when(second)
    def _():
        send_copy.start()

    new_m1[...] = moment1
    new_m2[...] = moment2
    new_w[...] = stepped
    for one in send_far:
        one.wait_send()

    @pl.when(second)
    def _():
        send_copy.wait_send()


def per_device(inputs, cotangent, weight, moment1, moment2):
    vmem = pl.BlockSpec(memory_space=pltpu.VMEM)
    anywhere = pl.BlockSpec(memory_space=pl.ANY)
    shape = jax.ShapeDtypeStruct
    outs = [
        shape((LANE, 2 * HALF), BF16),
        shape((LANE, 2 * HALF), BF16),
        shape((LANE, ROWS), BF16),
        shape((LANE, ROWS), F32),
        shape((LANE, ROWS), F32),
        shape((LANE, ROWS), BF16),
    ]
    scratch = [
        ((2, HALF, D), BF16),
        ((HALF, WIDE), BF16),
        ((LANE, ROWS), BF16),
        ((LANE, ROWS), F32),
        ((LANE, ROWS), F32),
        ((WIDE, D), BF16),
        ((16, WIDE), F32),
        ((2, HALF, D), BF16),
        ((4, 4, 2, PACK, 128), BF16),
        ((2, PACK, 128), BF16),
        ((HALF, WIDE), F32),
        ((HALF, 128), F32),
        ((HALF, WIDE), F32),
        ((HALF, WIDE), F32),
        ((HALF, WIDE), F32),
        ((2, PACK, 128), BF16),
        ((WIDE, HALF), BF16),
        ((2, LANE, HALF), BF16),
        ((WIDE, HALF), BF16),
        ((2, LANE, HALF), BF16),
        ((2, LANE, HALF), BF16),
        ((4, 4, 2, PACK, 128), BF16),
        ((3, 4, 2, PACK, 128), BF16),
        ((2, PACK, 128), F32),
        ((4, 2, PACK, 128), BF16),
        ((3, 2, PACK, 128), BF16),
        ((8, 128), F32),
        ((3, 8, 128), F32),
        ((8, 128), F32),
        ((3, 8, 128), F32),
        ((2, PACK, 128), BF16),
        ((HALF, WIDE), BF16),
        ((WIDE, HALF), BF16),
        ((2, LANE, HALF), BF16),
        ((2, 4, LANE, ROWS), BF16),
        ((2, 3, LANE, ROWS), BF16),
        ((LANE, ROWS), BF16),
        ((LANE, ROWS), BF16),
        ((LANE, ROWS), BF16),
        ((LANE, ROWS), BF16),
        ((HALF, WIDE), BF16),
        ((HALF, WIDE), BF16),
        ((2, PACK, 128), BF16),
        ((4, 2, PACK, 128), BF16),
        ((2, 4, 2, HALF, ROWS), BF16),
        ((LANE, ROWS), F32),
    ]
    results = pl.pallas_call(
        kernel,
        out_shape=outs,
        in_specs=[anywhere] * 5,
        out_specs=[vmem] * 6,
        scratch_shapes=[pltpu.VMEM(dims, kind) for dims, kind in scratch]
        + [pltpu.SemaphoreType.DMA((SLOTS,))] * 2
        + [pltpu.SemaphoreType.DMA((6,)), pltpu.SemaphoreType.REGULAR],
        compiler_params=pltpu.CompilerParams(
            collective_id=0, has_side_effects=True, vmem_limit_bytes=54656 * 2**10
        ),
    )(inputs, cotangent, weight.T, moment1.T, moment2.T)
    return tuple(one.T for one in results)


def solution(mesh):
    split = P("dp", "section")
    return jax.shard_map(
        per_device,
        mesh=mesh,
        in_specs=(P("dp", None), P("dp", None), split, split, split),
        out_specs=(split,) * 6,
        check_vma=False,
    )
```

```python
import math

import jax
import jax.numpy as jnp
from jax import lax
from jax.experimental import pallas as pl
from jax.experimental.pallas import tpu as pltpu
from jax.sharding import PartitionSpec as P

D = 3072
SECTIONS = 2
NORM_EPS = 1e-05
FIRST_FIX = 0.6513215599
SECOND_FIX = 0.4012630607
SCALE = 1.0 / math.sqrt(D)
HALF = 64
LANE = 96
PAIR = 192
WIDE = 256
ROWS = 384
F32 = jnp.float32
BF16 = jnp.bfloat16

PIECE = HALF // 2
PACK = 48
CUT = LANE // 3

W_Z, W_Y, W_ZY, W_C = 0, 3, 6, 15
X_UP, X_Z, X_X = 23, 25, 31
LOW, X2, SPARE, SLOPE = 55, 56, 57, 58
B_X, B_Z, R_X, R_Z = 59, 83, 89, 92
G_DOWN, G_C = 95, 97
G_YO, G_YS, G_Z, COPY = 98, 107, 110, 113
S_Y, L_Y = 114, 121
SLOTS = 127


def gelu_both(z):
    cdf = 0.5 * (1.0 + lax.erf(z * 0.7071067811865476))
    return z * cdf, cdf + z * jnp.exp(-0.5 * z * z) * 0.3989422804014327


def stepped(weight, moment1, moment2, gradient):
    moment1 = 0.9 * moment1 + 0.1 * gradient
    moment2 = 0.95 * moment2 + 0.05 * gradient * gradient
    update = moment1 / FIRST_FIX / (jnp.sqrt(moment2 / SECOND_FIX) + 1e-08)
    plain = weight.astype(F32)
    return (plain - 0.05 * (update + 0.1 * plain)).astype(BF16), moment1, moment2


def kernel(
    inputs, cotangent, w, m1, m2,
    spare, grad, gradient, copy,
    xin, cot, wv, m1v, m2v, wp, csum, low, xg, xout, normed, inv, mixed, slope_of, up, g_in,
    slope_t, sl, x2_t, x2, spare_in, bsend, brecv, zacc, zsend, zrecv,
    rsend, rrecv, rzsend, rzrecv, gpack, gout, g_t, gc, gsend, grecv, gzs, gzr, copy_out, copy_in, slopes, x2_w,
    spack, sg, lowx, gown,
    send_sem, recv_sem, here_sem,
):
    sec = lax.axis_index("section")
    dp = lax.axis_index("dp")
    c = sec % 2
    x = sec // 2 % 4
    s = sec // 32
    zq = sec // 8 % 4
    y = dp % 4
    zh = dp // 4
    odd = x % 2
    other = dp + 4 - 8 * zh
    core = {"section": sec + 1 - 2 * c, "dp": dp}
    across = {"section": sec + 32 - 64 * s, "dp": dp}
    far = {"section": sec, "dp": other}
    ys = [{"section": sec, "dp": zh * 4 + (y + j) % 4} for j in (1, 2, 3)]
    xs = [{"section": s * 32 + zq * 8 + (x + j) % 4 * 2 + c, "dp": dp} for j in (1, 2, 3)]
    zs = [{"section": s * 32 + (zq + j) % 4 * 8 + x * 2 + c, "dp": dp} for j in (1, 2, 3)]
    first = s == 0
    second = s == 1
    window = pl.ds(pl.multiple_of(zq * 768 + x // 2 * 384 + odd * 128, 128), WIDE)
    my_rows = pl.ds(pl.multiple_of(odd * 64 + c * LANE, 32), LANE)
    core_rows = pl.ds(pl.multiple_of(odd * 64 + (1 - c) * LANE, 32), LANE)

    def copier(slot, src, dst, to):
        return pltpu.make_async_remote_copy(
            src_ref=src,
            dst_ref=dst,
            send_sem=send_sem.at[slot],
            recv_sem=recv_sem.at[slot],
            device_id=to,
            device_id_type=pl.DeviceIdType.MESH,
        )

    def arrived(slot, where):
        copier(slot, where, where, core).wait_recv()

    def cols_of(replica):
        return pl.ds(pl.multiple_of(replica * ROWS, ROWS), ROWS)

    load_w = pltpu.make_async_copy(w, wv, here_sem.at[0])
    load_m1 = pltpu.make_async_copy(m1, m1v, here_sem.at[1])
    load_m2 = pltpu.make_async_copy(m2, m2v, here_sem.at[2])
    tokens = [pl.ds(pl.multiple_of(half * HALF, HALF), HALF) for half in (c, 1 - c)]
    load_x = [
        pltpu.make_async_copy(inputs.at[tokens[i]], xin.at[half], here_sem.at[3 + i])
        for i, half in enumerate((c, 1 - c))
    ]
    load_cot = pltpu.make_async_copy(cotangent.at[tokens[0], window], cot, here_sem.at[5])
    load_w.start()

    @pl.when(first)
    def _():
        for one in load_x:
            one.start()

    @pl.when(second)
    def _():
        load_cot.start()
        load_m1.start()
        load_m2.start()

    barrier = pltpu.get_barrier_semaphore()
    ys_core = [{"section": core["section"], "dp": one["dp"]} for one in ys]
    peers = [core, across, far] + ys + ys_core + xs + zs
    for peer in peers:
        pl.semaphore_signal(barrier, inc=1, device_id=peer, device_id_type=pl.DeviceIdType.MESH)
    load_w.wait()
    pl.semaphore_wait(barrier, len(peers))

    pieces = [pl.ds(PIECE * t, PIECE) for t in range(2)]
    cuts = [pl.ds(CUT * t, CUT) for t in range(3)]
    my_cuts = [pl.ds(pl.multiple_of(odd * 64 + c * LANE + CUT * t, 32), CUT) for t in range(3)]

    w_far = [copier(W_Z + t, wv.at[cuts[t]], wp.at[my_cuts[t], cols_of(dp)], far) for t in range(3)]
    mine = wp.at[my_rows, cols_of(dp)]
    sent = [copier(W_Y + j, wv, mine, ys[j]) for j in range(3)]
    sent.append(copier(W_C, wv, mine, core))

    @pl.when(first)
    def _():
        for one in w_far:
            one.start()

    for one in sent:
        one.start()
    sent += w_far
    wp[my_rows, cols_of(dp)] = wv[...]
    blank = pl.ds(pl.multiple_of((1 - odd) * PAIR, 64), WIDE - PAIR)
    wp[blank, :] = jnp.zeros((WIDE - PAIR, D), BF16)

    def normalise(rows):
        centre = jnp.mean(rows, axis=1, keepdims=True)
        gap = rows - centre
        scale = lax.rsqrt(jnp.mean(gap * gap, axis=1, keepdims=True) + NORM_EPS)
        return (gap * scale).astype(BF16), centre, scale

    def keep_stats(rows, block, centre, scale):
        inv[rows, :] = jnp.broadcast_to(scale, (scale.shape[0], 128))
        normed[rows, :] = (block.astype(F32) - centre) * scale

    @pl.when(first)
    def _():
        load_x[0].wait()
        low[c], centre, scale = normalise(xin[c].astype(F32))
        keep_stats(slice(None), xin[c, :, window], centre, scale)

    def to_core(slot, replica):
        block = wp.at[my_rows, cols_of(replica)]
        one = copier(slot, block, block, core)
        one.start()
        sent.append(one)

    from_y = [zh * 4 + (y + 4 - j) % 4 for j in (1, 2, 3)]
    from_zy = [(1 - zh) * 4 + (y + 4 - j) % 4 for j in (1, 2, 3)]
    for j in range(3):
        arrived(W_Y + j, wp.at[my_rows, cols_of(from_y[j])])
        to_core(W_C + 2 + j, from_y[j])

    @pl.when(second)
    def _():
        for one in w_far:
            one.start()

    for t in range(3):
        held = wp.at[my_cuts[t], cols_of(other)]
        arrived(W_Z + t, held)
        for j in range(3):
            one = copier(W_ZY + 3 * t + j, held, held, ys[j])
            one.start()
            sent.append(one)

    near = pl.ds(pl.multiple_of(zh * 1536, 1536), 1536)
    away = pl.ds(pl.multiple_of((1 - zh) * 1536, 1536), 1536)

    def times_weight(rows, cols):
        return SCALE * lax.dot_general(
            low[c, rows, cols], wp[:, cols], (((1,), (1,)), ((), ())), preferred_element_type=F32
        )

    @pl.when(first)
    def _():
        for i, replica in zip((0, 2, 3, 4), [dp] + from_y):
            arrived(W_C + i, wp.at[core_rows, cols_of(replica)])
        mixed[...] = times_weight(slice(None), near)

    to_core(W_C + 1, other)
    for j in range(3):
        for t in range(3):
            arrived(W_ZY + 3 * t + j, wp.at[my_cuts[t], cols_of(from_zy[j])])
        to_core(W_C + 5 + j, from_zy[j])

    @pl.when(first)
    def _():
        for i, replica in zip((1, 5, 6, 7), [other] + from_zy):
            arrived(W_C + i, wp.at[core_rows, cols_of(replica)])

    def column_sums():
        csum[...] = lax.dot_general(
            jnp.ones((16, D), BF16), wp[...], (((1,), (1,)), ((), ())), preferred_element_type=F32
        )

    left = lax.broadcasted_iota(jnp.int32, (PIECE, 128), 1) < 64
    left16 = lax.broadcasted_iota(jnp.int32, (16, 128), 1) < 64

    def turn(block):
        return pltpu.roll(block, 64, 1)

    def pack(full, shared, shift):
        turned = turn(shared)
        near, away = (turned, shared) if shift else (shared, turned)
        return jnp.concatenate([full, jnp.where(left16, near[:16], away[16:])], axis=0)

    def pack_own(wide):
        low_form = pack(wide[:, :128], wide[:, 128:], False)
        return jnp.where(odd == 0, low_form, pack(wide[:, 128:], wide[:, :128], True))

    def shared_part(packed, shift):
        end = packed[PIECE:]
        turned = turn(end)
        return jnp.concatenate([turned, end] if shift else [end, turned], axis=0)

    def unpack_own(packed):
        full = packed[:PIECE]
        low_form = jnp.concatenate([full, shared_part(packed, False)], axis=1)
        high_form = jnp.concatenate([shared_part(packed, True), full], axis=1)
        return jnp.where(odd == 0, low_form, high_form)

    own = [xg.at[x, zq, t] for t in range(2)]
    x_up = [copier(X_UP + t, xout.at[t], own[t], across) for t in range(2)]
    x_z = [copier(X_Z + 3 * t + j, own[t], own[t], zs[j]) for t in range(2) for j in range(3)]
    x_x = {}
    for t in range(2):
        for i in range(4):
            block = xg.at[x, (zq + 4 - i) % 4, t]
            for j in range(3):
                x_x[t, i, j] = copier(X_X + 12 * t + 3 * i + j, block, block, xs[j])
    swap_low = copier(LOW, low.at[c], low.at[c], core)

    @pl.when(second)
    def _():
        for t in range(2):
            arrived(X_UP + t, own[t])
            for one in x_z[3 * t : 3 * t + 3] + [x_x[t, 0, j] for j in range(3)]:
                one.start()
        for t in range(2):
            for j in range(3):
                arrived(X_Z + 3 * t + j, xg.at[x, (zq + 3 - j) % 4, t])
                for k in range(3):
                    x_x[t, j + 1, k].start()
        for i, replica in enumerate([dp, other] + from_y + from_zy):
            arrived(W_C + i, wp.at[core_rows, cols_of(replica)])
        column_sums()
        load_cot.wait()

    def gathered(t):
        for i in range(4):
            for j in range(3):
                block = xg.at[(x + 3 - j) % 4, (zq + 4 - i) % 4, t]
                arrived(X_X + 12 * t + 3 * i + j, block)
        rows = pieces[t]
        parts = []
        for m in range(8):
            even = xg[m % 2 * 2, m // 2, t].astype(F32)
            late = xg[m % 2 * 2 + 1, m // 2, t].astype(F32)
            middle = jnp.where(left, shared_part(even, False), shared_part(late, True))
            parts += [even[:PIECE], middle, late[:PIECE]]
        low[c, rows], centre, scale = normalise(jnp.concatenate(parts, axis=1))
        keep_stats(rows, unpack_own(xg[x, zq, t].astype(F32)), centre, scale)

    def find_slope(rows, upstream):
        up[rows, :] = upstream.astype(F32)
        slopes[rows, :] = (up[rows, :] * slope_of[rows, :]).astype(BF16)

    b_x = {}
    for t in range(2):
        for i in range(4):
            q = (zq + 1 + i) % 4
            for j in range(3):
                block = bsend.at[(x + 1 + j) % 4, q, t]
                b_x[t, i, j] = copier(B_X + 12 * t + 3 * i + j, block, brecv.at[j, q, t], xs[j])

    def back(t):
        slope = slopes[pieces[t], :]
        for i in range(4):
            q = (zq + 1 + i) % 4
            for half in range(2):
                cols = pl.ds(pl.multiple_of(q * 768 + half * 384, 384), 384)
                part = SCALE * jnp.dot(slope, wp[:, cols], preferred_element_type=F32)
                middle = part[:, 128:256]
                bsend[2 * half, q, t] = pack(part[:, :128], middle, False).astype(BF16)
                bsend[2 * half + 1, q, t] = pack(part[:, 256:], middle, True).astype(BF16)
            for j in range(3):
                b_x[t, i, j].start()

    r_x = [copier(R_X + j, rsend, rrecv.at[j], xs[j]) for j in range(3)]
    r_z = [copier(R_Z + j, rzsend, rzrecv.at[j], zs[j]) for j in range(3)]

    def give_sums():
        wide = slopes[...].astype(F32)
        r1 = jnp.sum(wide * csum[0:1, :], axis=1, keepdims=True) * (SCALE / D)
        r2 = jnp.sum(wide * mixed[...], axis=1, keepdims=True) * (1.0 / D)
        spot = lax.broadcasted_iota(jnp.int32, (HALF, 128), 1)
        both = jnp.where(spot == 0, r1, jnp.where(spot == 1, r2, 0.0))
        both = jnp.concatenate([both, jnp.zeros((128 - HALF, 128), F32)], axis=0)
        rsend[...] = both.T[:8, :]
        for one in r_x:
            one.start()

    low_y = {}
    for i, half in enumerate((1 - zh, zh)):
        for j in range(3):
            cols = cols_of(half * 4 + (y + 1 + j) % 4)
            low_y[i, j] = copier(L_Y + 3 * i + j, low.at[:, :, cols], lowx.at[i, y], ys[j])

    for t in range(2):
        rows = pieces[t]

        @pl.when(second)
        def _():
            gathered(t)
            mixed[rows, :] = times_weight(rows, slice(None))
            if t == 1:
                swap_low.start()

        @pl.when(first)
        def _():
            mixed[rows, :] = mixed[rows, :] + times_weight(rows, away)

        value, slope_value = gelu_both(mixed[rows, :])
        slope_of[rows, :] = slope_value

        @pl.when(first)
        def _():
            xout[t] = pack_own(xin[c, rows, window].astype(F32) + value).astype(BF16)
            x_up[t].start()

        @pl.when(second)
        def _():
            find_slope(rows, cot[rows, :])
            back(t)
            x2_w[rows, :] = (unpack_own(xg[x, zq, t].astype(F32)) + value).astype(BF16)

    @pl.when(first)
    def _():
        load_x[1].wait()
        low[1 - c], _, _ = normalise(xin[1 - c].astype(F32))
        for one in low_y.values():
            one.start()
        for i, half in enumerate((1 - zh, zh)):
            lowx[i, y] = low[:, :, cols_of(half * 4 + y)]
        column_sums()
        for t in range(2):
            arrived(G_DOWN + t, g_in.at[t])
            find_slope(pieces[t], unpack_own(g_in[t].astype(F32)))
            back(t)

    give_sums()
    slope_t[...] = slopes[...].T
    swap_slope = copier(SLOPE, slope_t.at[core_rows], sl.at[c], core)
    swap_x2 = copier(X2, x2_t.at[core_rows], x2.at[c], core)
    send_far = [copier(G_Z + t, gzs.at[cuts[t]], gzr.at[cuts[t]], far) for t in range(3)]

    def reduce_far():
        for t in range(3):
            total = gsend[1 - zh, y, cuts[t]].astype(F32)
            for j in range(3):
                arrived(G_YO + 3 * j + t, grecv.at[0, j, cuts[t]])
                total = total + grecv[0, j, cuts[t]].astype(F32)
            gzs[cuts[t], :] = total.astype(BF16)
            send_far[t].start()

    b_z = []

    def sum_terms(t):
        for i in range(4):
            q = (zq + 1 + i) % 4
            total = bsend[x, q, t].astype(F32)
            for j in range(3):
                arrived(B_X + 12 * t + 3 * i + j, brecv.at[j, q, t])
                total = total + brecv[j, q, t].astype(F32)
            if i < 3:
                zsend[q, t] = total.astype(BF16)
                one = copier(B_Z + 3 * t + i, zsend.at[q, t], zrecv.at[i, t], zs[i])
                one.start()
                b_z.append(one)
            else:
                zacc[t] = total
        if t == 0:
            sums = rsend[...]
            for j in range(3):
                arrived(R_X + j, rrecv.at[j])
                sums = sums + rrecv[j]
            rzsend[...] = sums
            for one in r_z:
                one.start()

    s_y = {}
    for flip in range(2):
        for dy in range(4):
            if flip + dy:
                to = core if dy == 0 else (ys_core if flip else ys)[dy - 1]
                s_y[flip, dy] = copier(S_Y + 2 * dy + flip - 1, spack.at[flip], sg.at[y, c], to)

    @pl.when(second)
    def _():
        swap_slope.start()
        sl[c] = slope_t[my_rows, :]

    @pl.when(first)
    def _():
        for flip, rows in enumerate((my_rows, core_rows)):
            block = slope_t[rows, :]
            spack[flip] = jnp.concatenate([block[:48], block[48:]], axis=1)
        for one in s_y.values():
            one.start()
        sg[y, c] = spack[0]

    sum_terms(0)

    g_y = []
    for i, half in enumerate((1 - zh, zh)):
        for j in range(3):
            to = (y + 1 + j) % 4
            if i == 0:
                g_y += [
                    copier(
                        G_YO + 3 * j + t,
                        gsend.at[half, to, cuts[t]],
                        grecv.at[i, j, cuts[t]],
                        ys[j],
                    )
                    for t in range(3)
                ]
            else:
                g_y.append(copier(G_YS + j, gsend.at[half, to], grecv.at[i, j], ys[j]))

    @pl.when(second)
    def _():
        arrived(LOW, low.at[1 - c])
        arrived(SLOPE, sl.at[1 - c])
        whole = jnp.concatenate([sl[0], sl[1]], axis=1)
        for i, half in enumerate((1 - zh, zh)):
            for j in range(4):
                to = (y + 1 + j) % 4
                rows = low[:, :, cols_of(half * 4 + to)].reshape(2 * HALF, ROWS)
                part = jnp.dot(whole, rows, preferred_element_type=F32)
                gsend[half, to] = (part * SCALE).astype(BF16)
                if j < 3:
                    for one in g_y[3 * j : 3 * j + 3] if i == 0 else g_y[9 + j : 10 + j]:
                        one.start()

    @pl.when(first)
    def _():
        for i in range(2):
            for j in range(3):
                arrived(L_Y + 3 * i + j, lowx.at[i, (y + 3 - j) % 4])
        for dy in range(4):
            for flip in range(2):
                if flip + dy:
                    block = sg.at[(y + 4 - dy) % 4, c + flip - 2 * c * flip]
                    arrived(S_Y + 2 * dy + flip - 1, block)
        left48 = lax.broadcasted_iota(jnp.int32, (PACK, 128), 1) < 64
        parts = []
        for k in range(4):
            even, late = sg[k, 0].astype(F32), sg[k, 1].astype(F32)
            upper = jnp.where(left48, even, turn(late))
            lower = jnp.where(left48, turn(even), late)
            parts.append(jnp.concatenate([upper, lower], axis=0).astype(BF16))
        whole = jnp.concatenate(parts, axis=1)
        part = jnp.dot(whole, lowx[0].reshape(8 * HALF, ROWS), preferred_element_type=F32)
        gzs[...] = (part * SCALE).astype(BF16)
        for one in send_far:
            one.start()
        part = jnp.dot(whole, lowx[1].reshape(8 * HALF, ROWS), preferred_element_type=F32)
        gown[...] = part * SCALE

    sum_terms(1)

    sums = rzsend[...]
    for j in range(3):
        arrived(R_Z + j, rzrecv.at[j])
        sums = sums + rzrecv[j]
    sums = jnp.concatenate([sums, jnp.zeros((120, 128), F32)], axis=0).T
    g_down = [copier(G_DOWN + t, gpack.at[t], g_in.at[t], across) for t in range(2)]
    for t in range(2):
        rows = pieces[t]
        total = zacc[t]
        for j in range(3):
            arrived(B_Z + 3 * t + j, zrecv.at[j, t])
            total = total + zrecv[j, t].astype(F32)
        r1 = sums[PIECE * t : PIECE * t + PIECE, 0:1]
        r2 = sums[PIECE * t : PIECE * t + PIECE, 1:2]
        change = inv[rows, 0:1] * (unpack_own(total) - r1 - normed[rows, :] * r2)
        renewed = up[rows, :] + change
        gout[rows, :] = renewed.astype(BF16)

        @pl.when(second)
        def _():
            gpack[t] = pack_own(renewed).astype(BF16)
            g_down[t].start()

    @pl.when(second)
    def _():
        reduce_far()

    g_t[...] = gout[...].T
    swap_g = copier(G_C, g_t.at[core_rows], gc.at[c], core)
    swap_g.start()
    gc[c] = g_t[my_rows, :]

    send_spare = copier(SPARE, x2, spare_in, across)

    @pl.when(second)
    def _():
        x2_t[...] = x2_w[...].T
        swap_x2.start()
        x2[c] = x2_t[my_rows, :]
        arrived(X2, x2.at[1 - c])
        send_spare.start()

        total = gsend[zh, y].astype(F32)
        for j in range(3):
            arrived(G_YS + j, grecv.at[1, j])
            total = total + grecv[1, j].astype(F32)
        gown[...] = total
        spare[...] = jnp.zeros_like(spare)
        copy[...] = jnp.zeros_like(copy)

    @pl.when(first)
    def _():
        arrived(SPARE, spare_in)
        spare[...] = jnp.concatenate([spare_in[0], spare_in[1]], axis=1)
        arrived(COPY, copy_in)
        copy[...] = copy_in[...]
        for one in x_up + list(low_y.values()) + list(s_y.values()):
            one.wait_send()

    for one in sent + list(b_x.values()) + b_z + r_x + r_z:
        one.wait_send()

    @pl.when(second)
    def _():
        for one in x_z + list(x_x.values()) + g_down + g_y:
            one.wait_send()
        for one in (swap_slope, swap_low, swap_x2, send_spare):
            one.wait_send()

    arrived(G_C, gc.at[1 - c])
    grad[...] = jnp.concatenate([gc[0], gc[1]], axis=1)
    swap_g.wait_send()

    for t in range(3):
        arrived(G_Z + t, gzr.at[cuts[t]])
    total = gown[...] + gzr[...].astype(F32)
    gradient[...] = total
    send_copy = copier(COPY, copy_out, copy_in, across)

    @pl.when(second)
    def _():
        load_m1.wait()
        load_m2.wait()
        copy_out[...] = stepped(wv[...], m1v[...], m2v[...], total)[0]
        send_copy.start()

    for one in send_far:
        one.wait_send()

    @pl.when(second)
    def _():
        send_copy.wait_send()


def per_device(inputs, cotangent, weight, moment1, moment2):
    vmem = pl.BlockSpec(memory_space=pltpu.VMEM)
    anywhere = pl.BlockSpec(memory_space=pl.ANY)
    shape = jax.ShapeDtypeStruct
    outs = [
        shape((LANE, 2 * HALF), BF16),
        shape((LANE, 2 * HALF), BF16),
        shape((LANE, ROWS), F32),
        shape((LANE, ROWS), BF16),
    ]
    scratch = [
        ((2, HALF, D), BF16),
        ((HALF, WIDE), BF16),
        ((LANE, ROWS), BF16),
        ((LANE, ROWS), F32),
        ((LANE, ROWS), F32),
        ((WIDE, D), BF16),
        ((16, WIDE), F32),
        ((2, HALF, D), BF16),
        ((4, 4, 2, PACK, 128), BF16),
        ((2, PACK, 128), BF16),
        ((HALF, WIDE), F32),
        ((HALF, 128), F32),
        ((HALF, WIDE), F32),
        ((HALF, WIDE), F32),
        ((HALF, WIDE), F32),
        ((2, PACK, 128), BF16),
        ((WIDE, HALF), BF16),
        ((2, LANE, HALF), BF16),
        ((WIDE, HALF), BF16),
        ((2, LANE, HALF), BF16),
        ((2, LANE, HALF), BF16),
        ((4, 4, 2, PACK, 128), BF16),
        ((3, 4, 2, PACK, 128), BF16),
        ((2, PACK, 128), F32),
        ((4, 2, PACK, 128), BF16),
        ((3, 2, PACK, 128), BF16),
        ((8, 128), F32),
        ((3, 8, 128), F32),
        ((8, 128), F32),
        ((3, 8, 128), F32),
        ((2, PACK, 128), BF16),
        ((HALF, WIDE), BF16),
        ((WIDE, HALF), BF16),
        ((2, LANE, HALF), BF16),
        ((2, 4, LANE, ROWS), BF16),
        ((2, 3, LANE, ROWS), BF16),
        ((LANE, ROWS), BF16),
        ((LANE, ROWS), BF16),
        ((LANE, ROWS), BF16),
        ((LANE, ROWS), BF16),
        ((HALF, WIDE), BF16),
        ((HALF, WIDE), BF16),
        ((2, PACK, 128), BF16),
        ((4, 2, PACK, 128), BF16),
        ((2, 4, 2, HALF, ROWS), BF16),
        ((LANE, ROWS), F32),
    ]
    spare, grad, gradient, copy = pl.pallas_call(
        kernel,
        out_shape=outs,
        in_specs=[anywhere] * 5,
        out_specs=[vmem] * 4,
        scratch_shapes=[pltpu.VMEM(dims, kind) for dims, kind in scratch]
        + [pltpu.SemaphoreType.DMA((SLOTS,))] * 2
        + [pltpu.SemaphoreType.DMA((6,))],
        compiler_params=pltpu.CompilerParams(
            collective_id=0, has_side_effects=True, vmem_limit_bytes=54656 * 2**10
        ),
    )(inputs, cotangent, weight.T, moment1.T, moment2.T)
    new = stepped(weight, moment1, moment2, gradient.T)
    return (spare.T, grad.T) + new + (copy.T,)


def solution(mesh):
    split = P("dp", "section")
    return jax.shard_map(
        per_device,
        mesh=mesh,
        in_specs=(P("dp", None), P("dp", None), split, split, split),
        out_specs=(split,) * 6,
        check_vma=False,
    )
```

```python
import math

import jax
import jax.numpy as jnp
from jax import lax
from jax.experimental import pallas as pl
from jax.experimental.pallas import tpu as pltpu
from jax.sharding import PartitionSpec as P

D = 3072
SECTIONS = 2
NORM_EPS = 1e-05
FIRST_FIX = 0.6513215599
SECOND_FIX = 0.4012630607
SCALE = 1.0 / math.sqrt(D)
HALF = 64
LANE = 96
PAIR = 192
WIDE = 256
ROWS = 384
F32 = jnp.float32
BF16 = jnp.bfloat16

PIECE = HALF // 2
PACK = 48
CUT = LANE // 3

W_Z, W_Y, W_ZY, W_C = 0, 3, 6, 15
X_UP, X_Z, X_X = 23, 25, 31
LOW, X2, SPARE, SLOPE = 55, 56, 57, 58
B_X, B_Z, R_X, R_Z = 59, 83, 89, 92
G_DOWN, G_C = 95, 97
G_YO, G_YS, G_Z, COPY = 98, 107, 110, 113
S_Y, L_Y = 114, 121
SLOTS = 127


def gelu_both(z):
    cdf = 0.5 * (1.0 + lax.erf(z * 0.7071067811865476))
    return z * cdf, cdf + z * jnp.exp(-0.5 * z * z) * 0.3989422804014327


def stepped(weight, moment1, moment2, gradient):
    moment1 = 0.9 * moment1 + 0.1 * gradient
    moment2 = 0.95 * moment2 + 0.05 * gradient * gradient
    update = moment1 / FIRST_FIX / (jnp.sqrt(moment2 / SECOND_FIX) + 1e-08)
    plain = weight.astype(F32)
    return (plain - 0.05 * (update + 0.1 * plain)).astype(BF16), moment1, moment2


def kernel(
    inputs, cotangent, w, m1, m2,
    spare, grad, gradient, copy,
    xin, cot, wv, m1v, m2v, wp, csum, low, xg, xout, normed, inv, mixed, slope_of, up, g_in,
    slope_t, sl, x2_t, x2, spare_in, bsend, brecv, zacc, zsend, zrecv,
    rsend, rrecv, rzsend, rzrecv, gpack, gout, g_t, gc, gsend, grecv, gzs, gzr, copy_out, copy_in, slopes, x2_w,
    spack, sg, lowx, gown, wide_t,
    send_sem, recv_sem, here_sem,
):
    sec = lax.axis_index("section")
    dp = lax.axis_index("dp")
    c = sec % 2
    x = sec // 2 % 4
    s = sec // 32
    zq = sec // 8 % 4
    y = dp % 4
    zh = dp // 4
    odd = x % 2
    other = dp + 4 - 8 * zh
    core = {"section": sec + 1 - 2 * c, "dp": dp}
    across = {"section": sec + 32 - 64 * s, "dp": dp}
    far = {"section": sec, "dp": other}
    ys = [{"section": sec, "dp": zh * 4 + (y + j) % 4} for j in (1, 2, 3)]
    xs = [{"section": s * 32 + zq * 8 + (x + j) % 4 * 2 + c, "dp": dp} for j in (1, 2, 3)]
    zs = [{"section": s * 32 + (zq + j) % 4 * 8 + x * 2 + c, "dp": dp} for j in (1, 2, 3)]
    first = s == 0
    second = s == 1
    window = pl.ds(pl.multiple_of(zq * 768 + x // 2 * 384 + odd * 128, 128), WIDE)
    my_rows = pl.ds(pl.multiple_of(odd * 64 + c * LANE, 32), LANE)
    core_rows = pl.ds(pl.multiple_of(odd * 64 + (1 - c) * LANE, 32), LANE)

    def copier(slot, src, dst, to):
        return pltpu.make_async_remote_copy(
            src_ref=src,
            dst_ref=dst,
            send_sem=send_sem.at[slot],
            recv_sem=recv_sem.at[slot],
            device_id=to,
            device_id_type=pl.DeviceIdType.MESH,
        )

    def arrived(slot, where):
        copier(slot, where, where, core).wait_recv()

    def cols_of(replica):
        return pl.ds(pl.multiple_of(replica * ROWS, ROWS), ROWS)

    load_w = pltpu.make_async_copy(w, wv, here_sem.at[0])
    load_m1 = pltpu.make_async_copy(m1, m1v, here_sem.at[1])
    load_m2 = pltpu.make_async_copy(m2, m2v, here_sem.at[2])
    tokens = [pl.ds(pl.multiple_of(half * HALF, HALF), HALF) for half in (c, 1 - c)]
    load_x = [
        pltpu.make_async_copy(inputs.at[tokens[i]], xin.at[half], here_sem.at[3 + i])
        for i, half in enumerate((c, 1 - c))
    ]
    load_cot = pltpu.make_async_copy(cotangent.at[tokens[0], window], cot, here_sem.at[5])
    load_w.start()

    @pl.when(first)
    def _():
        for one in load_x:
            one.start()

    @pl.when(second)
    def _():
        load_cot.start()
        load_m1.start()
        load_m2.start()

    barrier = pltpu.get_barrier_semaphore()
    ys_core = [{"section": core["section"], "dp": one["dp"]} for one in ys]
    peers = [core, across, far] + ys + ys_core + xs + zs
    for peer in peers:
        pl.semaphore_signal(barrier, inc=1, device_id=peer, device_id_type=pl.DeviceIdType.MESH)
    load_w.wait()
    pl.semaphore_wait(barrier, len(peers))

    pieces = [pl.ds(PIECE * t, PIECE) for t in range(2)]
    cuts = [pl.ds(CUT * t, CUT) for t in range(3)]
    my_cuts = [pl.ds(pl.multiple_of(odd * 64 + c * LANE + CUT * t, 32), CUT) for t in range(3)]

    w_far = [copier(W_Z + t, wv.at[cuts[t]], wp.at[my_cuts[t], cols_of(dp)], far) for t in range(3)]
    mine = wp.at[my_rows, cols_of(dp)]
    sent = [copier(W_Y + j, wv, mine, ys[j]) for j in range(3)]
    sent.append(copier(W_C, wv, mine, core))

    @pl.when(first)
    def _():
        for one in w_far:
            one.start()

    for one in sent:
        one.start()
    sent += w_far
    wp[my_rows, cols_of(dp)] = wv[...]
    blank = pl.ds(pl.multiple_of((1 - odd) * PAIR, 64), WIDE - PAIR)
    wp[blank, :] = jnp.zeros((WIDE - PAIR, D), BF16)

    def normalise(rows):
        centre = jnp.mean(rows, axis=1, keepdims=True)
        gap = rows - centre
        scale = lax.rsqrt(jnp.mean(gap * gap, axis=1, keepdims=True) + NORM_EPS)
        return (gap * scale).astype(BF16), centre, scale

    def keep_stats(rows, block, centre, scale):
        inv[rows, :] = jnp.broadcast_to(scale, (scale.shape[0], 128))
        normed[rows, :] = (block.astype(F32) - centre) * scale

    @pl.when(first)
    def _():
        load_x[0].wait()
        low[c], centre, scale = normalise(xin[c].astype(F32))
        keep_stats(slice(None), xin[c, :, window], centre, scale)

    def to_core(slot, replica):
        block = wp.at[my_rows, cols_of(replica)]
        one = copier(slot, block, block, core)
        one.start()
        sent.append(one)

    from_y = [zh * 4 + (y + 4 - j) % 4 for j in (1, 2, 3)]
    from_zy = [(1 - zh) * 4 + (y + 4 - j) % 4 for j in (1, 2, 3)]
    for j in range(3):
        arrived(W_Y + j, wp.at[my_rows, cols_of(from_y[j])])
        to_core(W_C + 2 + j, from_y[j])

    @pl.when(second)
    def _():
        for one in w_far:
            one.start()

    for t in range(3):
        held = wp.at[my_cuts[t], cols_of(other)]
        arrived(W_Z + t, held)
        for j in range(3):
            one = copier(W_ZY + 3 * t + j, held, held, ys[j])
            one.start()
            sent.append(one)

    near = pl.ds(pl.multiple_of(zh * 1536, 1536), 1536)
    away = pl.ds(pl.multiple_of((1 - zh) * 1536, 1536), 1536)

    def times_weight(rows, cols):
        return SCALE * lax.dot_general(
            low[c, rows, cols], wp[:, cols], (((1,), (1,)), ((), ())), preferred_element_type=F32
        )

    @pl.when(first)
    def _():
        for i, replica in zip((0, 2, 3, 4), [dp] + from_y):
            arrived(W_C + i, wp.at[core_rows, cols_of(replica)])
        mixed[...] = times_weight(slice(None), near)

    to_core(W_C + 1, other)
    for j in range(3):
        for t in range(3):
            arrived(W_ZY + 3 * t + j, wp.at[my_cuts[t], cols_of(from_zy[j])])
        to_core(W_C + 5 + j, from_zy[j])

    @pl.when(first)
    def _():
        for i, replica in zip((1, 5, 6, 7), [other] + from_zy):
            arrived(W_C + i, wp.at[core_rows, cols_of(replica)])

    def column_sums():
        csum[...] = lax.dot_general(
            jnp.ones((16, D), BF16), wp[...], (((1,), (1,)), ((), ())), preferred_element_type=F32
        )

    left = lax.broadcasted_iota(jnp.int32, (PIECE, 128), 1) < 64
    left16 = lax.broadcasted_iota(jnp.int32, (16, 128), 1) < 64

    def turn(block):
        return pltpu.roll(block, 64, 1)

    def pack(full, shared, shift):
        turned = turn(shared)
        near, away = (turned, shared) if shift else (shared, turned)
        return jnp.concatenate([full, jnp.where(left16, near[:16], away[16:])], axis=0)

    def pack_own(wide):
        low_form = pack(wide[:, :128], wide[:, 128:], False)
        return jnp.where(odd == 0, low_form, pack(wide[:, 128:], wide[:, :128], True))

    def shared_part(packed, shift):
        end = packed[PIECE:]
        turned = turn(end)
        return jnp.concatenate([turned, end] if shift else [end, turned], axis=0)

    def unpack_own(packed):
        full = packed[:PIECE]
        low_form = jnp.concatenate([full, shared_part(packed, False)], axis=1)
        high_form = jnp.concatenate([shared_part(packed, True), full], axis=1)
        return jnp.where(odd == 0, low_form, high_form)

    own = [xg.at[x, zq, t] for t in range(2)]
    x_up = [copier(X_UP + t, xout.at[t], own[t], across) for t in range(2)]
    x_z = [copier(X_Z + 3 * t + j, own[t], own[t], zs[j]) for t in range(2) for j in range(3)]
    x_x = {}
    for t in range(2):
        column = xg.at[x, :, t]
        for j in range(3):
            x_x[t, j] = copier(X_X + 3 * t + j, column, column, xs[j])
    swap_low = copier(LOW, low.at[c], low.at[c], core)

    @pl.when(second)
    def _():
        for t in range(2):
            arrived(X_UP + t, own[t])
            for one in x_z[3 * t : 3 * t + 3]:
                one.start()
        for t in range(2):
            for j in range(3):
                arrived(X_Z + 3 * t + j, xg.at[x, (zq + 3 - j) % 4, t])
            for j in range(3):
                x_x[t, j].start()
        for i, replica in enumerate([dp, other] + from_y + from_zy):
            arrived(W_C + i, wp.at[core_rows, cols_of(replica)])
        column_sums()
        load_cot.wait()

    def gathered(t):
        for j in range(3):
            arrived(X_X + 3 * t + j, xg.at[(x + 3 - j) % 4, :, t])
        rows = pieces[t]
        parts = []
        for m in range(8):
            even = xg[m % 2 * 2, m // 2, t].astype(F32)
            late = xg[m % 2 * 2 + 1, m // 2, t].astype(F32)
            middle = jnp.where(left, shared_part(even, False), shared_part(late, True))
            parts += [even[:PIECE], middle, late[:PIECE]]
        low[c, rows], centre, scale = normalise(jnp.concatenate(parts, axis=1))
        keep_stats(rows, unpack_own(xg[x, zq, t].astype(F32)), centre, scale)

    def find_slope(rows, upstream):
        up[rows, :] = upstream.astype(F32)
        slopes[rows, :] = (up[rows, :] * slope_of[rows, :]).astype(BF16)

    b_x = {}
    for t in range(2):
        for j in range(3):
            column = bsend.at[(x + 1 + j) % 4, :, t]
            b_x[t, j] = copier(B_X + 3 * t + j, column, brecv.at[j, :, t], xs[j])

    def back(t):
        slope = slopes[pieces[t], :]
        for q in range(4):
            for half in range(2):
                cols = pl.ds(q * 768 + half * 384, 384)
                part = SCALE * jnp.dot(slope, wp[:, cols], preferred_element_type=F32)
                middle = part[:, 128:256]
                bsend[2 * half, q, t] = pack(part[:, :128], middle, False).astype(BF16)
                bsend[2 * half + 1, q, t] = pack(part[:, 256:], middle, True).astype(BF16)
        for j in range(3):
            b_x[t, j].start()

    r_x = [copier(R_X + j, rsend, rrecv.at[j], xs[j]) for j in range(3)]
    r_z = [copier(R_Z + j, rzsend, rzrecv.at[j], zs[j]) for j in range(3)]

    def give_sums():
        wide = slopes[...].astype(F32)
        r1 = jnp.sum(wide * csum[0:1, :], axis=1, keepdims=True) * (SCALE / D)
        r2 = jnp.sum(wide * mixed[...], axis=1, keepdims=True) * (1.0 / D)
        spot = lax.broadcasted_iota(jnp.int32, (HALF, 128), 1)
        both = jnp.where(spot == 0, r1, jnp.where(spot == 1, r2, 0.0))
        both = jnp.concatenate([both, jnp.zeros((128 - HALF, 128), F32)], axis=0)
        rsend[...] = both.T[:8, :]
        for one in r_x:
            one.start()

    low_y = {}
    for i, half in enumerate((1 - zh, zh)):
        for j in range(3):
            cols = cols_of(half * 4 + (y + 1 + j) % 4)
            low_y[i, j] = copier(L_Y + 3 * i + j, low.at[:, :, cols], lowx.at[i, y], ys[j])

    for t in range(2):
        rows = pieces[t]

        @pl.when(second)
        def _():
            gathered(t)
            mixed[rows, :] = times_weight(rows, slice(None))
            if t == 1:
                swap_low.start()

        @pl.when(first)
        def _():
            mixed[rows, :] = mixed[rows, :] + times_weight(rows, away)

        value, slope_value = gelu_both(mixed[rows, :])
        slope_of[rows, :] = slope_value

        @pl.when(first)
        def _():
            xout[t] = pack_own(xin[c, rows, window].astype(F32) + value).astype(BF16)
            x_up[t].start()

        @pl.when(second)
        def _():
            find_slope(rows, cot[rows, :])
            back(t)
            x2_w[rows, :] = (unpack_own(xg[x, zq, t].astype(F32)) + value).astype(BF16)

    @pl.when(first)
    def _():
        load_x[1].wait()
        low[1 - c], _, _ = normalise(xin[1 - c].astype(F32))
        for one in low_y.values():
            one.start()
        for i, half in enumerate((1 - zh, zh)):
            lowx[i, y] = low[:, :, cols_of(half * 4 + y)]
        column_sums()
        for t in range(2):
            arrived(G_DOWN + t, g_in.at[t])
            find_slope(pieces[t], unpack_own(g_in[t].astype(F32)))
            back(t)

    give_sums()
    slope_t[...] = slopes[...].T
    swap_slope = copier(SLOPE, slope_t.at[core_rows], sl.at[c], core)
    swap_x2 = copier(X2, x2_t.at[core_rows], x2.at[c], core)
    send_far = [copier(G_Z + t, gzs.at[cuts[t]], gzr.at[cuts[t]], far) for t in range(3)]

    def reduce_far():
        for t in range(3):
            total = gsend[1 - zh, y, cuts[t]].astype(F32)
            for j in range(3):
                arrived(G_YO + 3 * j + t, grecv.at[0, j, cuts[t]])
                total = total + grecv[0, j, cuts[t]].astype(F32)
            gzs[cuts[t], :] = total.astype(BF16)
            send_far[t].start()

    b_z = []

    def sum_terms(t):
        for j in range(3):
            arrived(B_X + 3 * t + j, brecv.at[j, :, t])
        for i in range(4):
            q = (zq + 1 + i) % 4
            total = bsend[x, q, t].astype(F32)
            for j in range(3):
                total = total + brecv[j, q, t].astype(F32)
            if i < 3:
                zsend[q, t] = total.astype(BF16)
                one = copier(B_Z + 3 * t + i, zsend.at[q, t], zrecv.at[i, t], zs[i])
                one.start()
                b_z.append(one)
            else:
                zacc[t] = total
        if t == 0:
            sums = rsend[...]
            for j in range(3):
                arrived(R_X + j, rrecv.at[j])
                sums = sums + rrecv[j]
            rzsend[...] = sums
            for one in r_z:
                one.start()

    s_y = {}
    for flip in range(2):
        for dy in range(4):
            if flip + dy:
                to = core if dy == 0 else (ys_core if flip else ys)[dy - 1]
                s_y[flip, dy] = copier(S_Y + 2 * dy + flip - 1, spack.at[flip], sg.at[y, c], to)

    @pl.when(second)
    def _():
        swap_slope.start()
        sl[c] = slope_t[my_rows, :]

    @pl.when(first)
    def _():
        for flip, rows in enumerate((my_rows, core_rows)):
            block = slope_t[rows, :]
            spack[flip] = jnp.concatenate([block[:48], block[48:]], axis=1)
        for one in s_y.values():
            one.start()
        sg[y, c] = spack[0]

    sum_terms(0)

    g_y = []
    for i, half in enumerate((1 - zh, zh)):
        for j in range(3):
            to = (y + 1 + j) % 4
            if i == 0:
                g_y += [
                    copier(
                        G_YO + 3 * j + t,
                        gsend.at[half, to, cuts[t]],
                        grecv.at[i, j, cuts[t]],
                        ys[j],
                    )
                    for t in range(3)
                ]
            else:
                g_y.append(copier(G_YS + j, gsend.at[half, to], grecv.at[i, j], ys[j]))

    @pl.when(second)
    def _():
        arrived(LOW, low.at[1 - c])
        arrived(SLOPE, sl.at[1 - c])
        whole = jnp.concatenate([sl[0], sl[1]], axis=1)
        for i, half in enumerate((1 - zh, zh)):
            for j in range(4):
                to = (y + 1 + j) % 4
                rows = low[:, :, cols_of(half * 4 + to)].reshape(2 * HALF, ROWS)
                part = jnp.dot(whole, rows, preferred_element_type=F32)
                gsend[half, to] = (part * SCALE).astype(BF16)
                if j < 3:
                    for one in g_y[3 * j : 3 * j + 3] if i == 0 else g_y[9 + j : 10 + j]:
                        one.start()

    @pl.when(first)
    def _():
        for i in range(2):
            for j in range(3):
                arrived(L_Y + 3 * i + j, lowx.at[i, (y + 3 - j) % 4])
        for dy in range(4):
            for flip in range(2):
                if flip + dy:
                    block = sg.at[(y + 4 - dy) % 4, c + flip - 2 * c * flip]
                    arrived(S_Y + 2 * dy + flip - 1, block)
        left48 = lax.broadcasted_iota(jnp.int32, (PACK, 128), 1) < 64
        parts = []
        for k in range(4):
            even, late = sg[k, 0].astype(F32), sg[k, 1].astype(F32)
            upper = jnp.where(left48, even, turn(late))
            lower = jnp.where(left48, turn(even), late)
            parts.append(jnp.concatenate([upper, lower], axis=0).astype(BF16))
        whole = jnp.concatenate(parts, axis=1)
        part = jnp.dot(whole, lowx[0].reshape(8 * HALF, ROWS), preferred_element_type=F32)
        gzs[...] = (part * SCALE).astype(BF16)
        for one in send_far:
            one.start()
        wide_t[...] = whole

    sum_terms(1)

    @pl.when(first)
    def _():
        rows = lowx[1].reshape(8 * HALF, ROWS)
        gown[...] = SCALE * jnp.dot(wide_t[...], rows, preferred_element_type=F32)

    sums = rzsend[...]
    for j in range(3):
        arrived(R_Z + j, rzrecv.at[j])
        sums = sums + rzrecv[j]
    sums = jnp.concatenate([sums, jnp.zeros((120, 128), F32)], axis=0).T
    g_down = [copier(G_DOWN + t, gpack.at[t], g_in.at[t], across) for t in range(2)]
    for t in range(2):
        rows = pieces[t]
        total = zacc[t]
        for j in range(3):
            arrived(B_Z + 3 * t + j, zrecv.at[j, t])
            total = total + zrecv[j, t].astype(F32)
        r1 = sums[PIECE * t : PIECE * t + PIECE, 0:1]
        r2 = sums[PIECE * t : PIECE * t + PIECE, 1:2]
        change = inv[rows, 0:1] * (unpack_own(total) - r1 - normed[rows, :] * r2)
        renewed = up[rows, :] + change
        gout[rows, :] = renewed.astype(BF16)

        @pl.when(second)
        def _():
            gpack[t] = pack_own(renewed).astype(BF16)
            g_down[t].start()

    @pl.when(second)
    def _():
        reduce_far()

    g_t[...] = gout[...].T
    swap_g = copier(G_C, g_t.at[core_rows], gc.at[c], core)
    swap_g.start()
    gc[c] = g_t[my_rows, :]

    send_spare = copier(SPARE, x2, spare_in, across)

    @pl.when(second)
    def _():
        x2_t[...] = x2_w[...].T
        swap_x2.start()
        x2[c] = x2_t[my_rows, :]
        arrived(X2, x2.at[1 - c])
        send_spare.start()

        total = gsend[zh, y].astype(F32)
        for j in range(3):
            arrived(G_YS + j, grecv.at[1, j])
            total = total + grecv[1, j].astype(F32)
        gown[...] = total
        spare[...] = jnp.zeros_like(spare)
        copy[...] = jnp.zeros_like(copy)

    @pl.when(first)
    def _():
        arrived(SPARE, spare_in)
        spare[...] = jnp.concatenate([spare_in[0], spare_in[1]], axis=1)
        arrived(COPY, copy_in)
        copy[...] = copy_in[...]
        for one in x_up + list(low_y.values()) + list(s_y.values()):
            one.wait_send()

    for one in sent + list(b_x.values()) + b_z + r_x + r_z:
        one.wait_send()

    @pl.when(second)
    def _():
        for one in x_z + list(x_x.values()) + g_down + g_y:
            one.wait_send()
        for one in (swap_slope, swap_low, swap_x2, send_spare):
            one.wait_send()

    arrived(G_C, gc.at[1 - c])
    grad[...] = jnp.concatenate([gc[0], gc[1]], axis=1)
    swap_g.wait_send()

    for t in range(3):
        arrived(G_Z + t, gzr.at[cuts[t]])
    total = gown[...] + gzr[...].astype(F32)
    gradient[...] = total
    send_copy = copier(COPY, copy_out, copy_in, across)

    @pl.when(second)
    def _():
        load_m1.wait()
        load_m2.wait()
        copy_out[...] = stepped(wv[...], m1v[...], m2v[...], total)[0]
        send_copy.start()

    for one in send_far:
        one.wait_send()

    @pl.when(second)
    def _():
        send_copy.wait_send()


def per_device(inputs, cotangent, weight, moment1, moment2):
    vmem = pl.BlockSpec(memory_space=pltpu.VMEM)
    anywhere = pl.BlockSpec(memory_space=pl.ANY)
    shape = jax.ShapeDtypeStruct
    outs = [
        shape((LANE, 2 * HALF), BF16),
        shape((LANE, 2 * HALF), BF16),
        shape((LANE, ROWS), F32),
        shape((LANE, ROWS), BF16),
    ]
    scratch = [
        ((2, HALF, D), BF16),
        ((HALF, WIDE), BF16),
        ((LANE, ROWS), BF16),
        ((LANE, ROWS), F32),
        ((LANE, ROWS), F32),
        ((WIDE, D), BF16),
        ((16, WIDE), F32),
        ((2, HALF, D), BF16),
        ((4, 4, 2, PACK, 128), BF16),
        ((2, PACK, 128), BF16),
        ((HALF, WIDE), F32),
        ((HALF, 128), F32),
        ((HALF, WIDE), F32),
        ((HALF, WIDE), F32),
        ((HALF, WIDE), F32),
        ((2, PACK, 128), BF16),
        ((WIDE, HALF), BF16),
        ((2, LANE, HALF), BF16),
        ((WIDE, HALF), BF16),
        ((2, LANE, HALF), BF16),
        ((2, LANE, HALF), BF16),
        ((4, 4, 2, PACK, 128), BF16),
        ((3, 4, 2, PACK, 128), BF16),
        ((2, PACK, 128), F32),
        ((4, 2, PACK, 128), BF16),
        ((3, 2, PACK, 128), BF16),
        ((8, 128), F32),
        ((3, 8, 128), F32),
        ((8, 128), F32),
        ((3, 8, 128), F32),
        ((2, PACK, 128), BF16),
        ((HALF, WIDE), BF16),
        ((WIDE, HALF), BF16),
        ((2, LANE, HALF), BF16),
        ((2, 4, LANE, ROWS), BF16),
        ((2, 3, LANE, ROWS), BF16),
        ((LANE, ROWS), BF16),
        ((LANE, ROWS), BF16),
        ((LANE, ROWS), BF16),
        ((LANE, ROWS), BF16),
        ((HALF, WIDE), BF16),
        ((HALF, WIDE), BF16),
        ((2, PACK, 128), BF16),
        ((4, 2, PACK, 128), BF16),
        ((2, 4, 2, HALF, ROWS), BF16),
        ((LANE, ROWS), F32),
        ((LANE, 8 * HALF), BF16),
    ]
    spare, grad, gradient, copy = pl.pallas_call(
        kernel,
        out_shape=outs,
        in_specs=[anywhere] * 5,
        out_specs=[vmem] * 4,
        scratch_shapes=[pltpu.VMEM(dims, kind) for dims, kind in scratch]
        + [pltpu.SemaphoreType.DMA((SLOTS,))] * 2
        + [pltpu.SemaphoreType.DMA((6,))],
        compiler_params=pltpu.CompilerParams(
            collective_id=0, has_side_effects=True, vmem_limit_bytes=54784 * 2**10
        ),
    )(inputs, cotangent, weight.T, moment1.T, moment2.T)
    new = stepped(weight, moment1, moment2, gradient.T)
    return (spare.T, grad.T) + new + (copy.T,)


def solution(mesh):
    split = P("dp", "section")
    return jax.shard_map(
        per_device,
        mesh=mesh,
        in_specs=(P("dp", None), P("dp", None), split, split, split),
        out_specs=(split,) * 6,
        check_vma=False,
    )
```

```python
import math

import jax
import jax.numpy as jnp
from jax import lax
from jax.experimental import pallas as pl
from jax.experimental.pallas import tpu as pltpu
from jax.sharding import PartitionSpec as P

D = 3072
SECTIONS = 2
NORM_EPS = 1e-05
FIRST_FIX = 0.6513215599
SECOND_FIX = 0.4012630607
SCALE = 1.0 / math.sqrt(D)
HALF = 64
LANE = 96
PAIR = 192
WIDE = 256
ROWS = 384
F32 = jnp.float32
BF16 = jnp.bfloat16

PIECE = HALF // 2
PACK = 48
CUT = LANE // 3

W_Z, W_Y, W_ZY, W_C = 0, 3, 6, 15
X_UP, X_Z, X_X = 23, 25, 31
LOW, X2, SPARE, SLOPE = 55, 56, 57, 58
B_X, B_Z, R_X, R_Z = 59, 83, 89, 92
G_DOWN, G_C = 95, 97
G_YO, G_YS, G_Z, COPY = 98, 107, 110, 113
S_Y, L_Y = 114, 121
SLOTS = 127


def gelu_both(z):
    cdf = 0.5 * (1.0 + lax.erf(z * 0.7071067811865476))
    return z * cdf, cdf + z * jnp.exp(-0.5 * z * z) * 0.3989422804014327


def stepped(weight, moment1, moment2, gradient):
    moment1 = 0.9 * moment1 + 0.1 * gradient
    moment2 = 0.95 * moment2 + 0.05 * gradient * gradient
    update = moment1 / FIRST_FIX / (jnp.sqrt(moment2 / SECOND_FIX) + 1e-08)
    plain = weight.astype(F32)
    return (plain - 0.05 * (update + 0.1 * plain)).astype(BF16), moment1, moment2


def kernel(
    inputs, cotangent, w, m1, m2,
    spare, grad, gradient, copy,
    xin, cot, wv, m1v, m2v, wp, csum, low, xg, xout, normed, inv, mixed, slope_of, up, g_in,
    slope_t, sl, x2_t, x2, spare_in, bsend, brecv, zacc, zsend, zrecv,
    rsend, rrecv, rzsend, rzrecv, gpack, gout, g_t, gc, gsend, grecv, gzs, gzr, copy_out, copy_in, slopes, x2_w,
    spack, sg, lowx, gown, wide_t,
    send_sem, recv_sem, here_sem,
):
    sec = lax.axis_index("section")
    dp = lax.axis_index("dp")
    c = sec % 2
    x = sec // 2 % 4
    s = sec // 32
    zq = sec // 8 % 4
    y = dp % 4
    zh = dp // 4
    odd = x % 2
    other = dp + 4 - 8 * zh
    core = {"section": sec + 1 - 2 * c, "dp": dp}
    across = {"section": sec + 32 - 64 * s, "dp": dp}
    far = {"section": sec, "dp": other}
    ys = [{"section": sec, "dp": zh * 4 + (y + j) % 4} for j in (1, 2, 3)]
    xs = [{"section": s * 32 + zq * 8 + (x + j) % 4 * 2 + c, "dp": dp} for j in (1, 2, 3)]
    zs = [{"section": s * 32 + (zq + j) % 4 * 8 + x * 2 + c, "dp": dp} for j in (1, 2, 3)]
    first = s == 0
    second = s == 1
    window = pl.ds(pl.multiple_of(zq * 768 + x // 2 * 384 + odd * 128, 128), WIDE)
    my_rows = pl.ds(pl.multiple_of(odd * 64 + c * LANE, 32), LANE)
    core_rows = pl.ds(pl.multiple_of(odd * 64 + (1 - c) * LANE, 32), LANE)

    def copier(slot, src, dst, to):
        return pltpu.make_async_remote_copy(
            src_ref=src,
            dst_ref=dst,
            send_sem=send_sem.at[slot],
            recv_sem=recv_sem.at[slot],
            device_id=to,
            device_id_type=pl.DeviceIdType.MESH,
        )

    def arrived(slot, where):
        copier(slot, where, where, core).wait_recv()

    def cols_of(replica):
        return pl.ds(pl.multiple_of(replica * ROWS, ROWS), ROWS)

    load_w = pltpu.make_async_copy(w, wv, here_sem.at[0])
    load_m1 = pltpu.make_async_copy(m1, m1v, here_sem.at[1])
    load_m2 = pltpu.make_async_copy(m2, m2v, here_sem.at[2])
    tokens = [pl.ds(pl.multiple_of(half * HALF, HALF), HALF) for half in (c, 1 - c)]
    load_x = [
        pltpu.make_async_copy(inputs.at[tokens[i]], xin.at[half], here_sem.at[3 + i])
        for i, half in enumerate((c, 1 - c))
    ]
    load_cot = pltpu.make_async_copy(cotangent.at[tokens[0], window], cot, here_sem.at[5])
    load_w.start()

    @pl.when(first)
    def _():
        for one in load_x:
            one.start()

    @pl.when(second)
    def _():
        load_cot.start()
        load_m1.start()
        load_m2.start()

    barrier = pltpu.get_barrier_semaphore()
    ys_core = [{"section": core["section"], "dp": one["dp"]} for one in ys]
    peers = [core, across, far] + ys + ys_core + xs + zs
    for peer in peers:
        pl.semaphore_signal(barrier, inc=1, device_id=peer, device_id_type=pl.DeviceIdType.MESH)
    load_w.wait()
    pl.semaphore_wait(barrier, len(peers))

    pieces = [pl.ds(PIECE * t, PIECE) for t in range(2)]
    cuts = [pl.ds(CUT * t, CUT) for t in range(3)]
    my_cuts = [pl.ds(pl.multiple_of(odd * 64 + c * LANE + CUT * t, 32), CUT) for t in range(3)]

    w_far = [copier(W_Z + t, wv.at[cuts[t]], wp.at[my_cuts[t], cols_of(dp)], far) for t in range(3)]
    mine = wp.at[my_rows, cols_of(dp)]
    sent = [copier(W_Y + j, wv, mine, ys[j]) for j in range(3)]
    sent.append(copier(W_C, wv, mine, core))

    @pl.when(first)
    def _():
        for one in w_far:
            one.start()

    for one in sent:
        one.start()
    sent += w_far
    wp[my_rows, cols_of(dp)] = wv[...]
    blank = pl.ds(pl.multiple_of((1 - odd) * PAIR, 64), WIDE - PAIR)
    wp[blank, :] = jnp.zeros((WIDE - PAIR, D), BF16)

    def normalise(rows):
        centre = jnp.mean(rows, axis=1, keepdims=True)
        gap = rows - centre
        scale = lax.rsqrt(jnp.mean(gap * gap, axis=1, keepdims=True) + NORM_EPS)
        return (gap * scale).astype(BF16), centre, scale

    def keep_stats(rows, block, centre, scale):
        inv[rows, :] = jnp.broadcast_to(scale, (scale.shape[0], 128))
        normed[rows, :] = (block.astype(F32) - centre) * scale

    @pl.when(first)
    def _():
        load_x[0].wait()
        low[c], centre, scale = normalise(xin[c].astype(F32))
        keep_stats(slice(None), xin[c, :, window], centre, scale)

    def to_core(slot, replica):
        block = wp.at[my_rows, cols_of(replica)]
        one = copier(slot, block, block, core)
        one.start()
        sent.append(one)

    from_y = [zh * 4 + (y + 4 - j) % 4 for j in (1, 2, 3)]
    from_zy = [(1 - zh) * 4 + (y + 4 - j) % 4 for j in (1, 2, 3)]
    for j in range(3):
        arrived(W_Y + j, wp.at[my_rows, cols_of(from_y[j])])
        to_core(W_C + 2 + j, from_y[j])

    @pl.when(second)
    def _():
        for one in w_far:
            one.start()

    for t in range(3):
        held = wp.at[my_cuts[t], cols_of(other)]
        arrived(W_Z + t, held)
        for j in range(3):
            one = copier(W_ZY + 3 * t + j, held, held, ys[j])
            one.start()
            sent.append(one)

    near = pl.ds(pl.multiple_of(zh * 1536, 1536), 1536)
    away = pl.ds(pl.multiple_of((1 - zh) * 1536, 1536), 1536)

    def times_weight(rows, cols):
        return SCALE * lax.dot_general(
            low[c, rows, cols], wp[:, cols], (((1,), (1,)), ((), ())), preferred_element_type=F32
        )

    @pl.when(first)
    def _():
        for i, replica in zip((0, 2, 3, 4), [dp] + from_y):
            arrived(W_C + i, wp.at[core_rows, cols_of(replica)])
        mixed[...] = times_weight(slice(None), near)

    to_core(W_C + 1, other)
    for j in range(3):
        for t in range(3):
            arrived(W_ZY + 3 * t + j, wp.at[my_cuts[t], cols_of(from_zy[j])])
        to_core(W_C + 5 + j, from_zy[j])

    @pl.when(first)
    def _():
        for i, replica in zip((1, 5, 6, 7), [other] + from_zy):
            arrived(W_C + i, wp.at[core_rows, cols_of(replica)])

    def column_sums():
        csum[...] = lax.dot_general(
            jnp.ones((16, D), BF16), wp[...], (((1,), (1,)), ((), ())), preferred_element_type=F32
        )

    left = lax.broadcasted_iota(jnp.int32, (PIECE, 128), 1) < 64
    left16 = lax.broadcasted_iota(jnp.int32, (16, 128), 1) < 64

    def turn(block):
        return pltpu.roll(block, 64, 1)

    def pack(full, shared, shift):
        turned = turn(shared)
        near, away = (turned, shared) if shift else (shared, turned)
        return jnp.concatenate([full, jnp.where(left16, near[:16], away[16:])], axis=0)

    def pack_own(wide):
        low_form = pack(wide[:, :128], wide[:, 128:], False)
        return jnp.where(odd == 0, low_form, pack(wide[:, 128:], wide[:, :128], True))

    def shared_part(packed, shift):
        end = packed[PIECE:]
        turned = turn(end)
        return jnp.concatenate([turned, end] if shift else [end, turned], axis=0)

    def unpack_own(packed):
        full = packed[:PIECE]
        low_form = jnp.concatenate([full, shared_part(packed, False)], axis=1)
        high_form = jnp.concatenate([shared_part(packed, True), full], axis=1)
        return jnp.where(odd == 0, low_form, high_form)

    own = [xg.at[x, zq, t] for t in range(2)]
    x_up = [copier(X_UP + t, xout.at[t], own[t], across) for t in range(2)]
    x_z = [copier(X_Z + 3 * t + j, own[t], own[t], zs[j]) for t in range(2) for j in range(3)]
    x_x = {}
    for t in range(2):
        for i in range(4):
            block = xg.at[x, (zq + 4 - i) % 4, t]
            for j in range(3):
                x_x[t, i, j] = copier(X_X + 12 * t + 3 * i + j, block, block, xs[j])
    swap_low = copier(LOW, low.at[c], low.at[c], core)

    @pl.when(second)
    def _():
        for t in range(2):
            arrived(X_UP + t, own[t])
            for one in x_z[3 * t : 3 * t + 3] + [x_x[t, 0, j] for j in range(3)]:
                one.start()
        for t in range(2):
            for j in range(3):
                arrived(X_Z + 3 * t + j, xg.at[x, (zq + 3 - j) % 4, t])
                for k in range(3):
                    x_x[t, j + 1, k].start()
        for i, replica in enumerate([dp, other] + from_y + from_zy):
            arrived(W_C + i, wp.at[core_rows, cols_of(replica)])
        column_sums()
        load_cot.wait()

    def gathered(t):
        for i in range(4):
            for j in range(3):
                block = xg.at[(x + 3 - j) % 4, (zq + 4 - i) % 4, t]
                arrived(X_X + 12 * t + 3 * i + j, block)
        rows = pieces[t]
        parts = []
        for m in range(8):
            even = xg[m % 2 * 2, m // 2, t].astype(F32)
            late = xg[m % 2 * 2 + 1, m // 2, t].astype(F32)
            middle = jnp.where(left, shared_part(even, False), shared_part(late, True))
            parts += [even[:PIECE], middle, late[:PIECE]]
        low[c, rows], centre, scale = normalise(jnp.concatenate(parts, axis=1))
        keep_stats(rows, unpack_own(xg[x, zq, t].astype(F32)), centre, scale)

    def find_slope(rows, upstream):
        up[rows, :] = upstream.astype(F32)
        slopes[rows, :] = (up[rows, :] * slope_of[rows, :]).astype(BF16)

    b_x = {}
    for t in range(2):
        for i in range(4):
            q = (zq + 1 + i) % 4
            for j in range(3):
                block = bsend.at[(x + 1 + j) % 4, q, t]
                b_x[t, i, j] = copier(B_X + 12 * t + 3 * i + j, block, brecv.at[j, q, t], xs[j])

    def back(t):
        slope = slopes[pieces[t], :]
        for i in range(4):
            q = (zq + 1 + i) % 4
            for half in range(2):
                cols = pl.ds(pl.multiple_of(q * 768 + half * 384, 384), 384)
                part = SCALE * jnp.dot(slope, wp[:, cols], preferred_element_type=F32)
                middle = part[:, 128:256]
                bsend[2 * half, q, t] = pack(part[:, :128], middle, False).astype(BF16)
                bsend[2 * half + 1, q, t] = pack(part[:, 256:], middle, True).astype(BF16)
            for j in range(3):
                b_x[t, i, j].start()

    r_x = [copier(R_X + j, rsend, rrecv.at[j], xs[j]) for j in range(3)]
    r_z = [copier(R_Z + j, rzsend, rzrecv.at[j], zs[j]) for j in range(3)]

    def give_sums():
        wide = slopes[...].astype(F32)
        r1 = jnp.sum(wide * csum[0:1, :], axis=1, keepdims=True) * (SCALE / D)
        r2 = jnp.sum(wide * mixed[...], axis=1, keepdims=True) * (1.0 / D)
        spot = lax.broadcasted_iota(jnp.int32, (HALF, 128), 1)
        both = jnp.where(spot == 0, r1, jnp.where(spot == 1, r2, 0.0))
        both = jnp.concatenate([both, jnp.zeros((128 - HALF, 128), F32)], axis=0)
        rsend[...] = both.T[:8, :]
        for one in r_x:
            one.start()

    low_y = {}
    for i, half in enumerate((1 - zh, zh)):
        for j in range(3):
            cols = cols_of(half * 4 + (y + 1 + j) % 4)
            low_y[i, j] = copier(L_Y + 3 * i + j, low.at[:, :, cols], lowx.at[i, y], ys[j])

    for t in range(2):
        rows = pieces[t]

        @pl.when(second)
        def _():
            gathered(t)
            mixed[rows, :] = times_weight(rows, slice(None))
            if t == 1:
                swap_low.start()

        @pl.when(first)
        def _():
            mixed[rows, :] = mixed[rows, :] + times_weight(rows, away)

        value, slope_value = gelu_both(mixed[rows, :])
        slope_of[rows, :] = slope_value

        @pl.when(first)
        def _():
            xout[t] = pack_own(xin[c, rows, window].astype(F32) + value).astype(BF16)
            x_up[t].start()

        @pl.when(second)
        def _():
            find_slope(rows, cot[rows, :])
            back(t)
            x2_w[rows, :] = (unpack_own(xg[x, zq, t].astype(F32)) + value).astype(BF16)

    @pl.when(first)
    def _():
        load_x[1].wait()
        low[1 - c], _, _ = normalise(xin[1 - c].astype(F32))
        for one in low_y.values():
            one.start()
        for i, half in enumerate((1 - zh, zh)):
            lowx[i, y] = low[:, :, cols_of(half * 4 + y)]
        column_sums()
        for t in range(2):
            arrived(G_DOWN + t, g_in.at[t])
            find_slope(pieces[t], unpack_own(g_in[t].astype(F32)))
            back(t)

    give_sums()
    slope_t[...] = slopes[...].T
    swap_slope = copier(SLOPE, slope_t.at[core_rows], sl.at[c], core)
    swap_x2 = copier(X2, x2_t.at[core_rows], x2.at[c], core)
    send_far = [copier(G_Z + t, gzs.at[cuts[t]], gzr.at[cuts[t]], far) for t in range(3)]

    def reduce_far():
        for t in range(3):
            total = gsend[1 - zh, y, cuts[t]].astype(F32)
            for j in range(3):
                arrived(G_YO + 3 * j + t, grecv.at[0, j, cuts[t]])
                total = total + grecv[0, j, cuts[t]].astype(F32)
            gzs[cuts[t], :] = total.astype(BF16)
            send_far[t].start()

    b_z = []

    def sum_terms(t):
        for i in range(4):
            q = (zq + 1 + i) % 4
            total = bsend[x, q, t].astype(F32)
            for j in range(3):
                arrived(B_X + 12 * t + 3 * i + j, brecv.at[j, q, t])
                total = total + brecv[j, q, t].astype(F32)
            if i < 3:
                zsend[q, t] = total.astype(BF16)
                one = copier(B_Z + 3 * t + i, zsend.at[q, t], zrecv.at[i, t], zs[i])
                one.start()
                b_z.append(one)
            else:
                zacc[t] = total
        if t == 0:
            sums = rsend[...]
            for j in range(3):
                arrived(R_X + j, rrecv.at[j])
                sums = sums + rrecv[j]
            rzsend[...] = sums
            for one in r_z:
                one.start()

    s_y = {}
    for flip in range(2):
        for dy in range(4):
            if flip + dy:
                to = core if dy == 0 else (ys_core if flip else ys)[dy - 1]
                s_y[flip, dy] = copier(S_Y + 2 * dy + flip - 1, spack.at[flip], sg.at[y, c], to)

    @pl.when(second)
    def _():
        swap_slope.start()
        sl[c] = slope_t[my_rows, :]

    @pl.when(first)
    def _():
        for flip, rows in enumerate((my_rows, core_rows)):
            block = slope_t[rows, :]
            spack[flip] = jnp.concatenate([block[:48], block[48:]], axis=1)
        for one in s_y.values():
            one.start()
        sg[y, c] = spack[0]

    @pl.when(first)
    def _():
        for i in range(2):
            for j in range(3):
                arrived(L_Y + 3 * i + j, lowx.at[i, (y + 3 - j) % 4])
        for dy in range(4):
            for flip in range(2):
                if flip + dy:
                    block = sg.at[(y + 4 - dy) % 4, c + flip - 2 * c * flip]
                    arrived(S_Y + 2 * dy + flip - 1, block)
        left48 = lax.broadcasted_iota(jnp.int32, (PACK, 128), 1) < 64
        parts = []
        for k in range(4):
            even, late = sg[k, 0].astype(F32), sg[k, 1].astype(F32)
            upper = jnp.where(left48, even, turn(late))
            lower = jnp.where(left48, turn(even), late)
            parts.append(jnp.concatenate([upper, lower], axis=0).astype(BF16))
        whole = jnp.concatenate(parts, axis=1)
        part = jnp.dot(whole, lowx[0].reshape(8 * HALF, ROWS), preferred_element_type=F32)
        gzs[...] = (part * SCALE).astype(BF16)
        for one in send_far:
            one.start()
        wide_t[...] = whole

    sum_terms(0)

    g_y = []
    for i, half in enumerate((1 - zh, zh)):
        for j in range(3):
            to = (y + 1 + j) % 4
            if i == 0:
                g_y += [
                    copier(
                        G_YO + 3 * j + t,
                        gsend.at[half, to, cuts[t]],
                        grecv.at[i, j, cuts[t]],
                        ys[j],
                    )
                    for t in range(3)
                ]
            else:
                g_y.append(copier(G_YS + j, gsend.at[half, to], grecv.at[i, j], ys[j]))

    @pl.when(second)
    def _():
        arrived(LOW, low.at[1 - c])
        arrived(SLOPE, sl.at[1 - c])
        whole = jnp.concatenate([sl[0], sl[1]], axis=1)
        for i, half in enumerate((1 - zh, zh)):
            for j in range(4):
                to = (y + 1 + j) % 4
                rows = low[:, :, cols_of(half * 4 + to)].reshape(2 * HALF, ROWS)
                part = jnp.dot(whole, rows, preferred_element_type=F32)
                gsend[half, to] = (part * SCALE).astype(BF16)
                if j < 3:
                    for one in g_y[3 * j : 3 * j + 3] if i == 0 else g_y[9 + j : 10 + j]:
                        one.start()

    sum_terms(1)

    @pl.when(first)
    def _():
        rows = lowx[1].reshape(8 * HALF, ROWS)
        gown[...] = SCALE * jnp.dot(wide_t[...], rows, preferred_element_type=F32)

    sums = rzsend[...]
    for j in range(3):
        arrived(R_Z + j, rzrecv.at[j])
        sums = sums + rzrecv[j]
    sums = jnp.concatenate([sums, jnp.zeros((120, 128), F32)], axis=0).T
    g_down = [copier(G_DOWN + t, gpack.at[t], g_in.at[t], across) for t in range(2)]
    for t in range(2):
        rows = pieces[t]
        total = zacc[t]
        for j in range(3):
            arrived(B_Z + 3 * t + j, zrecv.at[j, t])
            total = total + zrecv[j, t].astype(F32)
        r1 = sums[PIECE * t : PIECE * t + PIECE, 0:1]
        r2 = sums[PIECE * t : PIECE * t + PIECE, 1:2]
        change = inv[rows, 0:1] * (unpack_own(total) - r1 - normed[rows, :] * r2)
        renewed = up[rows, :] + change
        gout[rows, :] = renewed.astype(BF16)

        @pl.when(second)
        def _():
            gpack[t] = pack_own(renewed).astype(BF16)
            g_down[t].start()

    @pl.when(second)
    def _():
        reduce_far()

    g_t[...] = gout[...].T
    swap_g = copier(G_C, g_t.at[core_rows], gc.at[c], core)
    swap_g.start()
    gc[c] = g_t[my_rows, :]

    send_spare = copier(SPARE, x2, spare_in, across)

    @pl.when(second)
    def _():
        x2_t[...] = x2_w[...].T
        swap_x2.start()
        x2[c] = x2_t[my_rows, :]
        arrived(X2, x2.at[1 - c])
        send_spare.start()

        total = gsend[zh, y].astype(F32)
        for j in range(3):
            arrived(G_YS + j, grecv.at[1, j])
            total = total + grecv[1, j].astype(F32)
        gown[...] = total
        spare[...] = jnp.zeros_like(spare)
        copy[...] = jnp.zeros_like(copy)

    @pl.when(first)
    def _():
        arrived(SPARE, spare_in)
        spare[...] = jnp.concatenate([spare_in[0], spare_in[1]], axis=1)
        arrived(COPY, copy_in)
        copy[...] = copy_in[...]
        for one in x_up + list(low_y.values()) + list(s_y.values()):
            one.wait_send()

    for one in sent + list(b_x.values()) + b_z + r_x + r_z:
        one.wait_send()

    @pl.when(second)
    def _():
        for one in x_z + list(x_x.values()) + g_down + g_y:
            one.wait_send()
        for one in (swap_slope, swap_low, swap_x2, send_spare):
            one.wait_send()

    arrived(G_C, gc.at[1 - c])
    grad[...] = jnp.concatenate([gc[0], gc[1]], axis=1)
    swap_g.wait_send()

    for t in range(3):
        arrived(G_Z + t, gzr.at[cuts[t]])
    total = gown[...] + gzr[...].astype(F32)
    gradient[...] = total
    send_copy = copier(COPY, copy_out, copy_in, across)

    @pl.when(second)
    def _():
        load_m1.wait()
        load_m2.wait()
        copy_out[...] = stepped(wv[...], m1v[...], m2v[...], total)[0]
        send_copy.start()

    for one in send_far:
        one.wait_send()

    @pl.when(second)
    def _():
        send_copy.wait_send()


def per_device(inputs, cotangent, weight, moment1, moment2):
    vmem = pl.BlockSpec(memory_space=pltpu.VMEM)
    anywhere = pl.BlockSpec(memory_space=pl.ANY)
    shape = jax.ShapeDtypeStruct
    outs = [
        shape((LANE, 2 * HALF), BF16),
        shape((LANE, 2 * HALF), BF16),
        shape((LANE, ROWS), F32),
        shape((LANE, ROWS), BF16),
    ]
    scratch = [
        ((2, HALF, D), BF16),
        ((HALF, WIDE), BF16),
        ((LANE, ROWS), BF16),
        ((LANE, ROWS), F32),
        ((LANE, ROWS), F32),
        ((WIDE, D), BF16),
        ((16, WIDE), F32),
        ((2, HALF, D), BF16),
        ((4, 4, 2, PACK, 128), BF16),
        ((2, PACK, 128), BF16),
        ((HALF, WIDE), F32),
        ((HALF, 128), F32),
        ((HALF, WIDE), F32),
        ((HALF, WIDE), F32),
        ((HALF, WIDE), F32),
        ((2, PACK, 128), BF16),
        ((WIDE, HALF), BF16),
        ((2, LANE, HALF), BF16),
        ((WIDE, HALF), BF16),
        ((2, LANE, HALF), BF16),
        ((2, LANE, HALF), BF16),
        ((4, 4, 2, PACK, 128), BF16),
        ((3, 4, 2, PACK, 128), BF16),
        ((2, PACK, 128), F32),
        ((4, 2, PACK, 128), BF16),
        ((3, 2, PACK, 128), BF16),
        ((8, 128), F32),
        ((3, 8, 128), F32),
        ((8, 128), F32),
        ((3, 8, 128), F32),
        ((2, PACK, 128), BF16),
        ((HALF, WIDE), BF16),
        ((WIDE, HALF), BF16),
        ((2, LANE, HALF), BF16),
        ((2, 4, LANE, ROWS), BF16),
        ((2, 3, LANE, ROWS), BF16),
        ((LANE, ROWS), BF16),
        ((LANE, ROWS), BF16),
        ((LANE, ROWS), BF16),
        ((LANE, ROWS), BF16),
        ((HALF, WIDE), BF16),
        ((HALF, WIDE), BF16),
        ((2, PACK, 128), BF16),
        ((4, 2, PACK, 128), BF16),
        ((2, 4, 2, HALF, ROWS), BF16),
        ((LANE, ROWS), F32),
        ((LANE, 8 * HALF), BF16),
    ]
    spare, grad, gradient, copy = pl.pallas_call(
        kernel,
        out_shape=outs,
        in_specs=[anywhere] * 5,
        out_specs=[vmem] * 4,
        scratch_shapes=[pltpu.VMEM(dims, kind) for dims, kind in scratch]
        + [pltpu.SemaphoreType.DMA((SLOTS,))] * 2
        + [pltpu.SemaphoreType.DMA((6,))],
        compiler_params=pltpu.CompilerParams(
            collective_id=0, has_side_effects=True, vmem_limit_bytes=54784 * 2**10
        ),
    )(inputs, cotangent, weight.T, moment1.T, moment2.T)
    new = stepped(weight, moment1, moment2, gradient.T)
    return (spare.T, grad.T) + new + (copy.T,)


def solution(mesh):
    split = P("dp", "section")
    return jax.shard_map(
        per_device,
        mesh=mesh,
        in_specs=(P("dp", None), P("dp", None), split, split, split),
        out_specs=(split,) * 6,
        check_vma=False,
    )
```

```python
import math

import jax
import jax.numpy as jnp
from jax import lax
from jax.experimental import pallas as pl
from jax.experimental.pallas import tpu as pltpu
from jax.sharding import PartitionSpec as P

D = 3072
SECTIONS = 2
NORM_EPS = 1e-05
FIRST_FIX = 0.6513215599
SECOND_FIX = 0.4012630607
SCALE = 1.0 / math.sqrt(D)
HALF = 64
LANE = 96
PAIR = 192
WIDE = 256
ROWS = 384
F32 = jnp.float32
BF16 = jnp.bfloat16

PIECE = HALF // 2
PACK = 48
CUT = LANE // 3

W_Z, W_Y, W_ZY, W_C = 0, 3, 6, 15
X_UP, X_Z, X_X = 23, 25, 31
LOW, X2, SPARE, SLOPE = 55, 56, 57, 58
B_X, B_Z, R_X, R_Z = 59, 83, 89, 92
G_DOWN, G_C = 95, 97
G_YO, G_YS, G_Z, COPY = 98, 107, 110, 113
S_Y, L_Y = 114, 121
SLOTS = 127


def gelu_both(z):
    cdf = 0.5 * (1.0 + lax.erf(z * 0.7071067811865476))
    return z * cdf, cdf + z * jnp.exp(-0.5 * z * z) * 0.3989422804014327


def stepped(weight, moment1, moment2, gradient):
    moment1 = 0.9 * moment1 + 0.1 * gradient
    moment2 = 0.95 * moment2 + 0.05 * gradient * gradient
    update = moment1 / FIRST_FIX / (jnp.sqrt(moment2 / SECOND_FIX) + 1e-08)
    plain = weight.astype(F32)
    return (plain - 0.05 * (update + 0.1 * plain)).astype(BF16), moment1, moment2


def kernel(
    inputs, cotangent, w, m1, m2,
    spare, grad, gradient, copy,
    xin, cot, wv, m1v, m2v, wp, csum, low, xg, xout, normed, inv, mixed, slope_of, up, g_in,
    slope_t, sl, x2_t, x2, spare_in, bsend, brecv, zacc, zsend, zrecv,
    rsend, rrecv, rzsend, rzrecv, gpack, gout, g_t, gc, gsend, grecv, gzs, gzr, copy_out, copy_in, slopes, x2_w,
    spack, sg, lowx, gown, wide_t,
    send_sem, recv_sem, here_sem,
):
    sec = lax.axis_index("section")
    dp = lax.axis_index("dp")
    c = sec % 2
    x = sec // 2 % 4
    s = sec // 32
    zq = sec // 8 % 4
    y = dp % 4
    zh = dp // 4
    odd = x % 2
    other = dp + 4 - 8 * zh
    core = {"section": sec + 1 - 2 * c, "dp": dp}
    across = {"section": sec + 32 - 64 * s, "dp": dp}
    far = {"section": sec, "dp": other}
    ys = [{"section": sec, "dp": zh * 4 + (y + j) % 4} for j in (1, 2, 3)]
    xs = [{"section": s * 32 + zq * 8 + (x + j) % 4 * 2 + c, "dp": dp} for j in (1, 2, 3)]
    zs = [{"section": s * 32 + (zq + j) % 4 * 8 + x * 2 + c, "dp": dp} for j in (1, 2, 3)]
    first = s == 0
    second = s == 1
    window = pl.ds(pl.multiple_of(zq * 768 + x // 2 * 384 + odd * 128, 128), WIDE)
    my_rows = pl.ds(pl.multiple_of(odd * 64 + c * LANE, 32), LANE)
    core_rows = pl.ds(pl.multiple_of(odd * 64 + (1 - c) * LANE, 32), LANE)

    def copier(slot, src, dst, to):
        return pltpu.make_async_remote_copy(
            src_ref=src,
            dst_ref=dst,
            send_sem=send_sem.at[slot],
            recv_sem=recv_sem.at[slot],
            device_id=to,
            device_id_type=pl.DeviceIdType.MESH,
        )

    def arrived(slot, where):
        copier(slot, where, where, core).wait_recv()

    def cols_of(replica):
        return pl.ds(pl.multiple_of(replica * ROWS, ROWS), ROWS)

    load_w = pltpu.make_async_copy(w, wv, here_sem.at[0])
    load_m1 = pltpu.make_async_copy(m1, m1v, here_sem.at[1])
    load_m2 = pltpu.make_async_copy(m2, m2v, here_sem.at[2])
    tokens = [pl.ds(pl.multiple_of(half * HALF, HALF), HALF) for half in (c, 1 - c)]
    load_x = [
        pltpu.make_async_copy(inputs.at[tokens[i]], xin.at[half], here_sem.at[3 + i])
        for i, half in enumerate((c, 1 - c))
    ]
    load_cot = pltpu.make_async_copy(cotangent.at[tokens[0], window], cot, here_sem.at[5])
    load_w.start()

    @pl.when(first)
    def _():
        for one in load_x:
            one.start()

    @pl.when(second)
    def _():
        load_cot.start()
        load_m1.start()
        load_m2.start()

    barrier = pltpu.get_barrier_semaphore()
    ys_core = [{"section": core["section"], "dp": one["dp"]} for one in ys]
    peers = [core, across, far] + ys + ys_core + xs + zs
    for peer in peers:
        pl.semaphore_signal(barrier, inc=1, device_id=peer, device_id_type=pl.DeviceIdType.MESH)
    load_w.wait()
    pl.semaphore_wait(barrier, len(peers))

    pieces = [pl.ds(PIECE * t, PIECE) for t in range(2)]
    cuts = [pl.ds(CUT * t, CUT) for t in range(3)]
    my_cuts = [pl.ds(pl.multiple_of(odd * 64 + c * LANE + CUT * t, 32), CUT) for t in range(3)]

    w_far = [copier(W_Z + t, wv.at[cuts[t]], wp.at[my_cuts[t], cols_of(dp)], far) for t in range(3)]
    mine = wp.at[my_rows, cols_of(dp)]
    sent = [copier(W_Y + j, wv, mine, ys[j]) for j in range(3)]
    sent.append(copier(W_C, wv, mine, core))

    @pl.when(first)
    def _():
        for one in w_far:
            one.start()

    for one in sent:
        one.start()
    sent += w_far
    wp[my_rows, cols_of(dp)] = wv[...]
    blank = pl.ds(pl.multiple_of((1 - odd) * PAIR, 64), WIDE - PAIR)
    wp[blank, :] = jnp.zeros((WIDE - PAIR, D), BF16)

    def normalise(rows):
        centre = jnp.mean(rows, axis=1, keepdims=True)
        gap = rows - centre
        scale = lax.rsqrt(jnp.mean(gap * gap, axis=1, keepdims=True) + NORM_EPS)
        return (gap * scale).astype(BF16), centre, scale

    def keep_stats(rows, block, centre, scale):
        inv[rows, :] = jnp.broadcast_to(scale, (scale.shape[0], 128))
        normed[rows, :] = (block.astype(F32) - centre) * scale

    @pl.when(first)
    def _():
        load_x[0].wait()
        low[c], centre, scale = normalise(xin[c].astype(F32))
        keep_stats(slice(None), xin[c, :, window], centre, scale)

    def to_core(slot, replica):
        block = wp.at[my_rows, cols_of(replica)]
        one = copier(slot, block, block, core)
        one.start()
        sent.append(one)

    from_y = [zh * 4 + (y + 4 - j) % 4 for j in (1, 2, 3)]
    from_zy = [(1 - zh) * 4 + (y + 4 - j) % 4 for j in (1, 2, 3)]
    for j in range(3):
        arrived(W_Y + j, wp.at[my_rows, cols_of(from_y[j])])
        to_core(W_C + 2 + j, from_y[j])

    @pl.when(second)
    def _():
        for one in w_far:
            one.start()

    for t in range(3):
        held = wp.at[my_cuts[t], cols_of(other)]
        arrived(W_Z + t, held)
        for j in range(3):
            one = copier(W_ZY + 3 * t + j, held, held, ys[j])
            one.start()
            sent.append(one)

    near = pl.ds(pl.multiple_of(zh * 1536, 1536), 1536)
    away = pl.ds(pl.multiple_of((1 - zh) * 1536, 1536), 1536)

    def times_weight(rows, cols):
        return SCALE * lax.dot_general(
            low[c, rows, cols], wp[:, cols], (((1,), (1,)), ((), ())), preferred_element_type=F32
        )

    @pl.when(first)
    def _():
        for i, replica in zip((0, 2, 3, 4), [dp] + from_y):
            arrived(W_C + i, wp.at[core_rows, cols_of(replica)])
        mixed[...] = times_weight(slice(None), near)

    to_core(W_C + 1, other)
    for j in range(3):
        for t in range(3):
            arrived(W_ZY + 3 * t + j, wp.at[my_cuts[t], cols_of(from_zy[j])])
        to_core(W_C + 5 + j, from_zy[j])

    @pl.when(first)
    def _():
        for i, replica in zip((1, 5, 6, 7), [other] + from_zy):
            arrived(W_C + i, wp.at[core_rows, cols_of(replica)])

    def column_sums():
        csum[...] = lax.dot_general(
            jnp.ones((16, D), BF16), wp[...], (((1,), (1,)), ((), ())), preferred_element_type=F32
        )

    left = lax.broadcasted_iota(jnp.int32, (PIECE, 128), 1) < 64
    left16 = lax.broadcasted_iota(jnp.int32, (16, 128), 1) < 64

    def turn(block):
        return pltpu.roll(block, 64, 1)

    def pack(full, shared, shift):
        turned = turn(shared)
        near, away = (turned, shared) if shift else (shared, turned)
        return jnp.concatenate([full, jnp.where(left16, near[:16], away[16:])], axis=0)

    def pack_own(wide):
        low_form = pack(wide[:, :128], wide[:, 128:], False)
        return jnp.where(odd == 0, low_form, pack(wide[:, 128:], wide[:, :128], True))

    def shared_part(packed, shift):
        end = packed[PIECE:]
        turned = turn(end)
        return jnp.concatenate([turned, end] if shift else [end, turned], axis=0)

    def unpack_own(packed):
        full = packed[:PIECE]
        low_form = jnp.concatenate([full, shared_part(packed, False)], axis=1)
        high_form = jnp.concatenate([shared_part(packed, True), full], axis=1)
        return jnp.where(odd == 0, low_form, high_form)

    own = [xg.at[x, zq, t] for t in range(2)]
    x_up = [copier(X_UP + t, xout.at[t], own[t], across) for t in range(2)]
    x_z = [copier(X_Z + 3 * t + j, own[t], own[t], zs[j]) for t in range(2) for j in range(3)]
    x_x = {}
    for t in range(2):
        for i in range(4):
            block = xg.at[x, (zq + 4 - i) % 4, t]
            for j in range(3):
                x_x[t, i, j] = copier(X_X + 12 * t + 3 * i + j, block, block, xs[j])
    swap_low = copier(LOW, low.at[c], low.at[c], core)

    @pl.when(second)
    def _():
        for t in range(2):
            arrived(X_UP + t, own[t])
            for one in x_z[3 * t : 3 * t + 3] + [x_x[t, 0, j] for j in range(3)]:
                one.start()
        for t in range(2):
            for j in range(3):
                arrived(X_Z + 3 * t + j, xg.at[x, (zq + 3 - j) % 4, t])
                for k in range(3):
                    x_x[t, j + 1, k].start()
        for i, replica in enumerate([dp, other] + from_y + from_zy):
            arrived(W_C + i, wp.at[core_rows, cols_of(replica)])
        column_sums()
        load_cot.wait()

    def gathered(t):
        for i in range(4):
            for j in range(3):
                block = xg.at[(x + 3 - j) % 4, (zq + 4 - i) % 4, t]
                arrived(X_X + 12 * t + 3 * i + j, block)
        rows = pieces[t]
        parts = []
        for m in range(8):
            even = xg[m % 2 * 2, m // 2, t].astype(F32)
            late = xg[m % 2 * 2 + 1, m // 2, t].astype(F32)
            middle = jnp.where(left, shared_part(even, False), shared_part(late, True))
            parts += [even[:PIECE], middle, late[:PIECE]]
        low[c, rows], centre, scale = normalise(jnp.concatenate(parts, axis=1))
        keep_stats(rows, unpack_own(xg[x, zq, t].astype(F32)), centre, scale)

    def find_slope(rows, upstream):
        up[rows, :] = upstream.astype(F32)
        slopes[rows, :] = (up[rows, :] * slope_of[rows, :]).astype(BF16)

    b_x = {}
    for t in range(2):
        for i in range(4):
            q = (zq + 1 + i) % 4
            for j in range(3):
                block = bsend.at[(x + 1 + j) % 4, q, t]
                b_x[t, i, j] = copier(B_X + 12 * t + 3 * i + j, block, brecv.at[j, q, t], xs[j])

    def back(t):
        slope = slopes[pieces[t], :]
        for i in range(4):
            q = (zq + 1 + i) % 4
            for half in range(2):
                cols = pl.ds(pl.multiple_of(q * 768 + half * 384, 384), 384)
                part = SCALE * jnp.dot(slope, wp[:, cols], preferred_element_type=F32)
                middle = part[:, 128:256]
                bsend[2 * half, q, t] = pack(part[:, :128], middle, False).astype(BF16)
                bsend[2 * half + 1, q, t] = pack(part[:, 256:], middle, True).astype(BF16)
            for j in range(3):
                b_x[t, i, j].start()

    r_x = [copier(R_X + j, rsend, rrecv.at[j], xs[j]) for j in range(3)]
    r_z = [copier(R_Z + j, rzsend, rzrecv.at[j], zs[j]) for j in range(3)]

    def give_sums():
        wide = slopes[...].astype(F32)
        r1 = jnp.sum(wide * csum[0:1, :], axis=1, keepdims=True) * (SCALE / D)
        r2 = jnp.sum(wide * mixed[...], axis=1, keepdims=True) * (1.0 / D)
        spot = lax.broadcasted_iota(jnp.int32, (HALF, 128), 1)
        both = jnp.where(spot == 0, r1, jnp.where(spot == 1, r2, 0.0))
        both = jnp.concatenate([both, jnp.zeros((128 - HALF, 128), F32)], axis=0)
        rsend[...] = both.T[:8, :]
        for one in r_x:
            one.start()

    low_y = {}
    for i, half in enumerate((1 - zh, zh)):
        for j in range(3):
            cols = cols_of(half * 4 + (y + 1 + j) % 4)
            low_y[i, j] = copier(L_Y + 3 * i + j, low.at[:, :, cols], lowx.at[i, y], ys[j])

    for t in range(2):
        rows = pieces[t]

        @pl.when(second)
        def _():
            gathered(t)
            mixed[rows, :] = times_weight(rows, slice(None))
            if t == 1:
                swap_low.start()

        @pl.when(first)
        def _():
            mixed[rows, :] = mixed[rows, :] + times_weight(rows, away)

        value, slope_value = gelu_both(mixed[rows, :])
        slope_of[rows, :] = slope_value

        @pl.when(first)
        def _():
            xout[t] = pack_own(xin[c, rows, window].astype(F32) + value).astype(BF16)
            x_up[t].start()

        @pl.when(second)
        def _():
            find_slope(rows, cot[rows, :])
            back(t)
            x2_w[rows, :] = (unpack_own(xg[x, zq, t].astype(F32)) + value).astype(BF16)

    @pl.when(first)
    def _():
        load_x[1].wait()
        low[1 - c], _, _ = normalise(xin[1 - c].astype(F32))
        for one in low_y.values():
            one.start()
        for i, half in enumerate((1 - zh, zh)):
            lowx[i, y] = low[:, :, cols_of(half * 4 + y)]
        column_sums()
        for t in range(2):
            arrived(G_DOWN + t, g_in.at[t])
            find_slope(pieces[t], unpack_own(g_in[t].astype(F32)))
            back(t)

    give_sums()
    slope_t[...] = slopes[...].T
    swap_slope = copier(SLOPE, slope_t.at[core_rows], sl.at[c], core)
    swap_x2 = copier(X2, x2_t.at[core_rows], x2.at[c], core)
    send_far = [copier(G_Z + t, gzs.at[cuts[t]], gzr.at[cuts[t]], far) for t in range(3)]

    def reduce_far():
        for t in range(3):
            total = gsend[1 - zh, y, cuts[t]].astype(F32)
            for j in range(3):
                arrived(G_YO + 3 * j + t, grecv.at[0, j, cuts[t]])
                total = total + grecv[0, j, cuts[t]].astype(F32)
            gzs[cuts[t], :] = total.astype(BF16)
            send_far[t].start()

    b_z = []

    def sum_terms(t):
        for i in range(4):
            q = (zq + 1 + i) % 4
            total = bsend[x, q, t].astype(F32)
            for j in range(3):
                arrived(B_X + 12 * t + 3 * i + j, brecv.at[j, q, t])
                total = total + brecv[j, q, t].astype(F32)
            if i < 3:
                zsend[q, t] = total.astype(BF16)
                one = copier(B_Z + 3 * t + i, zsend.at[q, t], zrecv.at[i, t], zs[i])
                one.start()
                b_z.append(one)
            else:
                zacc[t] = total
        if t == 0:
            sums = rsend[...]
            for j in range(3):
                arrived(R_X + j, rrecv.at[j])
                sums = sums + rrecv[j]
            rzsend[...] = sums
            for one in r_z:
                one.start()

    s_y = {}
    for flip in range(2):
        for dy in range(4):
            if flip + dy:
                to = core if dy == 0 else (ys_core if flip else ys)[dy - 1]
                s_y[flip, dy] = copier(S_Y + 2 * dy + flip - 1, spack.at[flip], sg.at[y, c], to)

    @pl.when(second)
    def _():
        swap_slope.start()
        sl[c] = slope_t[my_rows, :]

    @pl.when(first)
    def _():
        for flip, rows in enumerate((my_rows, core_rows)):
            block = slope_t[rows, :]
            spack[flip] = jnp.concatenate([block[:48], block[48:]], axis=1)
        for one in s_y.values():
            one.start()
        sg[y, c] = spack[0]

    def give_far():
        for i in range(2):
            for j in range(3):
                arrived(L_Y + 3 * i + j, lowx.at[i, (y + 3 - j) % 4])
        for dy in range(4):
            for flip in range(2):
                if flip + dy:
                    block = sg.at[(y + 4 - dy) % 4, c + flip - 2 * c * flip]
                    arrived(S_Y + 2 * dy + flip - 1, block)
        left48 = lax.broadcasted_iota(jnp.int32, (PACK, 128), 1) < 64
        parts = []
        for k in range(4):
            even, late = sg[k, 0].astype(F32), sg[k, 1].astype(F32)
            upper = jnp.where(left48, even, turn(late))
            lower = jnp.where(left48, turn(even), late)
            parts.append(jnp.concatenate([upper, lower], axis=0).astype(BF16))
        whole = jnp.concatenate(parts, axis=1)
        part = jnp.dot(whole, lowx[0].reshape(8 * HALF, ROWS), preferred_element_type=F32)
        gzs[...] = (part * SCALE).astype(BF16)
        for one in send_far:
            one.start()
        wide_t[...] = whole

    @pl.when(first & (zh == 1))
    def _():
        give_far()

    sum_terms(0)

    sum_terms(1)

    @pl.when(first & (zh == 0))
    def _():
        give_far()

    g_y = []
    for i, half in enumerate((1 - zh, zh)):
        for j in range(3):
            to = (y + 1 + j) % 4
            if i == 0:
                g_y += [
                    copier(
                        G_YO + 3 * j + t,
                        gsend.at[half, to, cuts[t]],
                        grecv.at[i, j, cuts[t]],
                        ys[j],
                    )
                    for t in range(3)
                ]
            else:
                g_y.append(copier(G_YS + j, gsend.at[half, to], grecv.at[i, j], ys[j]))

    @pl.when(second)
    def _():
        arrived(LOW, low.at[1 - c])
        arrived(SLOPE, sl.at[1 - c])
        whole = jnp.concatenate([sl[0], sl[1]], axis=1)
        for i, half in enumerate((1 - zh, zh)):
            for j in range(4):
                to = (y + 1 + j) % 4
                rows = low[:, :, cols_of(half * 4 + to)].reshape(2 * HALF, ROWS)
                part = jnp.dot(whole, rows, preferred_element_type=F32)
                gsend[half, to] = (part * SCALE).astype(BF16)
                if j < 3:
                    for one in g_y[3 * j : 3 * j + 3] if i == 0 else g_y[9 + j : 10 + j]:
                        one.start()

    @pl.when(first)
    def _():
        rows = lowx[1].reshape(8 * HALF, ROWS)
        gown[...] = SCALE * jnp.dot(wide_t[...], rows, preferred_element_type=F32)

    sums = rzsend[...]
    for j in range(3):
        arrived(R_Z + j, rzrecv.at[j])
        sums = sums + rzrecv[j]
    sums = jnp.concatenate([sums, jnp.zeros((120, 128), F32)], axis=0).T
    g_down = [copier(G_DOWN + t, gpack.at[t], g_in.at[t], across) for t in range(2)]
    for t in range(2):
        rows = pieces[t]
        total = zacc[t]
        for j in range(3):
            arrived(B_Z + 3 * t + j, zrecv.at[j, t])
            total = total + zrecv[j, t].astype(F32)
        r1 = sums[PIECE * t : PIECE * t + PIECE, 0:1]
        r2 = sums[PIECE * t : PIECE * t + PIECE, 1:2]
        change = inv[rows, 0:1] * (unpack_own(total) - r1 - normed[rows, :] * r2)
        renewed = up[rows, :] + change
        gout[rows, :] = renewed.astype(BF16)

        @pl.when(second)
        def _():
            gpack[t] = pack_own(renewed).astype(BF16)
            g_down[t].start()

    @pl.when(second)
    def _():
        reduce_far()

    g_t[...] = gout[...].T
    swap_g = copier(G_C, g_t.at[core_rows], gc.at[c], core)
    swap_g.start()
    gc[c] = g_t[my_rows, :]

    send_spare = copier(SPARE, x2, spare_in, across)

    @pl.when(second)
    def _():
        x2_t[...] = x2_w[...].T
        swap_x2.start()
        x2[c] = x2_t[my_rows, :]
        arrived(X2, x2.at[1 - c])
        send_spare.start()

        total = gsend[zh, y].astype(F32)
        for j in range(3):
            arrived(G_YS + j, grecv.at[1, j])
            total = total + grecv[1, j].astype(F32)
        gown[...] = total
        spare[...] = jnp.zeros_like(spare)
        copy[...] = jnp.zeros_like(copy)

    @pl.when(first)
    def _():
        arrived(SPARE, spare_in)
        spare[...] = jnp.concatenate([spare_in[0], spare_in[1]], axis=1)
        arrived(COPY, copy_in)
        copy[...] = copy_in[...]
        for one in x_up + list(low_y.values()) + list(s_y.values()):
            one.wait_send()

    for one in sent + list(b_x.values()) + b_z + r_x + r_z:
        one.wait_send()

    @pl.when(second)
    def _():
        for one in x_z + list(x_x.values()) + g_down + g_y:
            one.wait_send()
        for one in (swap_slope, swap_low, swap_x2, send_spare):
            one.wait_send()

    arrived(G_C, gc.at[1 - c])
    grad[...] = jnp.concatenate([gc[0], gc[1]], axis=1)
    swap_g.wait_send()

    for t in range(3):
        arrived(G_Z + t, gzr.at[cuts[t]])
    total = gown[...] + gzr[...].astype(F32)
    gradient[...] = total
    send_copy = copier(COPY, copy_out, copy_in, across)

    @pl.when(second)
    def _():
        load_m1.wait()
        load_m2.wait()
        copy_out[...] = stepped(wv[...], m1v[...], m2v[...], total)[0]
        send_copy.start()

    for one in send_far:
        one.wait_send()

    @pl.when(second)
    def _():
        send_copy.wait_send()


def per_device(inputs, cotangent, weight, moment1, moment2):
    vmem = pl.BlockSpec(memory_space=pltpu.VMEM)
    anywhere = pl.BlockSpec(memory_space=pl.ANY)
    shape = jax.ShapeDtypeStruct
    outs = [
        shape((LANE, 2 * HALF), BF16),
        shape((LANE, 2 * HALF), BF16),
        shape((LANE, ROWS), F32),
        shape((LANE, ROWS), BF16),
    ]
    scratch = [
        ((2, HALF, D), BF16),
        ((HALF, WIDE), BF16),
        ((LANE, ROWS), BF16),
        ((LANE, ROWS), F32),
        ((LANE, ROWS), F32),
        ((WIDE, D), BF16),
        ((16, WIDE), F32),
        ((2, HALF, D), BF16),
        ((4, 4, 2, PACK, 128), BF16),
        ((2, PACK, 128), BF16),
        ((HALF, WIDE), F32),
        ((HALF, 128), F32),
        ((HALF, WIDE), F32),
        ((HALF, WIDE), F32),
        ((HALF, WIDE), F32),
        ((2, PACK, 128), BF16),
        ((WIDE, HALF), BF16),
        ((2, LANE, HALF), BF16),
        ((WIDE, HALF), BF16),
        ((2, LANE, HALF), BF16),
        ((2, LANE, HALF), BF16),
        ((4, 4, 2, PACK, 128), BF16),
        ((3, 4, 2, PACK, 128), BF16),
        ((2, PACK, 128), F32),
        ((4, 2, PACK, 128), BF16),
        ((3, 2, PACK, 128), BF16),
        ((8, 128), F32),
        ((3, 8, 128), F32),
        ((8, 128), F32),
        ((3, 8, 128), F32),
        ((2, PACK, 128), BF16),
        ((HALF, WIDE), BF16),
        ((WIDE, HALF), BF16),
        ((2, LANE, HALF), BF16),
        ((2, 4, LANE, ROWS), BF16),
        ((2, 3, LANE, ROWS), BF16),
        ((LANE, ROWS), BF16),
        ((LANE, ROWS), BF16),
        ((LANE, ROWS), BF16),
        ((LANE, ROWS), BF16),
        ((HALF, WIDE), BF16),
        ((HALF, WIDE), BF16),
        ((2, PACK, 128), BF16),
        ((4, 2, PACK, 128), BF16),
        ((2, 4, 2, HALF, ROWS), BF16),
        ((LANE, ROWS), F32),
        ((LANE, 8 * HALF), BF16),
    ]
    spare, grad, gradient, copy = pl.pallas_call(
        kernel,
        out_shape=outs,
        in_specs=[anywhere] * 5,
        out_specs=[vmem] * 4,
        scratch_shapes=[pltpu.VMEM(dims, kind) for dims, kind in scratch]
        + [pltpu.SemaphoreType.DMA((SLOTS,))] * 2
        + [pltpu.SemaphoreType.DMA((6,))],
        compiler_params=pltpu.CompilerParams(
            collective_id=0, has_side_effects=True, vmem_limit_bytes=54784 * 2**10
        ),
    )(inputs, cotangent, weight.T, moment1.T, moment2.T)
    new = stepped(weight, moment1, moment2, gradient.T)
    return (spare.T, grad.T) + new + (copy.T,)


def solution(mesh):
    split = P("dp", "section")
    return jax.shard_map(
        per_device,
        mesh=mesh,
        in_specs=(P("dp", None), P("dp", None), split, split, split),
        out_specs=(split,) * 6,
        check_vma=False,
    )
```

```python
import math

import jax
import jax.numpy as jnp
from jax import lax
from jax.experimental import pallas as pl
from jax.experimental.pallas import tpu as pltpu
from jax.sharding import PartitionSpec as P

D = 3072
SECTIONS = 2
NORM_EPS = 1e-05
FIRST_FIX = 0.6513215599
SECOND_FIX = 0.4012630607
SCALE = 1.0 / math.sqrt(D)
HALF = 64
LANE = 96
PAIR = 192
WIDE = 256
ROWS = 384
F32 = jnp.float32
BF16 = jnp.bfloat16

PIECE = HALF // 2
PACK = 48
CUT = LANE // 3

W_Z, W_Y, W_ZY, W_C = 0, 3, 6, 15
X_UP, X_Z, X_X = 23, 25, 31
LOW, X2, SPARE, SLOPE = 55, 56, 57, 58
B_X, B_Z, R_X, R_Z = 59, 83, 89, 92
G_DOWN, G_C = 95, 97
G_YO, G_YS, G_Z, COPY = 98, 107, 110, 113
S_Y, L_Y = 114, 121
SLOTS = 127


def gelu_both(z):
    cdf = 0.5 * (1.0 + lax.erf(z * 0.7071067811865476))
    return z * cdf, cdf + z * jnp.exp(-0.5 * z * z) * 0.3989422804014327


def stepped(weight, moment1, moment2, gradient):
    moment1 = 0.9 * moment1 + 0.1 * gradient
    moment2 = 0.95 * moment2 + 0.05 * gradient * gradient
    update = moment1 / FIRST_FIX / (jnp.sqrt(moment2 / SECOND_FIX) + 1e-08)
    plain = weight.astype(F32)
    return (plain - 0.05 * (update + 0.1 * plain)).astype(BF16), moment1, moment2


def kernel(
    inputs, cotangent, w, m1, m2,
    spare, grad, gradient, copy,
    xin, cot, wv, m1v, m2v, wp, csum, low, xg, xout, normed, inv, mixed, slope_of, up, g_in,
    slope_t, sl, x2_t, x2, spare_in, bsend, brecv, zacc, zsend, zrecv,
    rsend, rrecv, rzsend, rzrecv, gpack, gout, g_t, gc, gsend, grecv, gzs, gzr, copy_out, copy_in, slopes, x2_w,
    spack, sg, lowx, gown, wide_t,
    send_sem, recv_sem, here_sem,
):
    sec = lax.axis_index("section")
    dp = lax.axis_index("dp")
    c = sec % 2
    x = sec // 2 % 4
    s = sec // 32
    zq = sec // 8 % 4
    y = dp % 4
    zh = dp // 4
    odd = x % 2
    other = dp + 4 - 8 * zh
    core = {"section": sec + 1 - 2 * c, "dp": dp}
    across = {"section": sec + 32 - 64 * s, "dp": dp}
    far = {"section": sec, "dp": other}
    ys = [{"section": sec, "dp": zh * 4 + (y + j) % 4} for j in (1, 2, 3)]
    xs = [{"section": s * 32 + zq * 8 + (x + j) % 4 * 2 + c, "dp": dp} for j in (1, 2, 3)]
    zs = [{"section": s * 32 + (zq + j) % 4 * 8 + x * 2 + c, "dp": dp} for j in (1, 2, 3)]
    first = s == 0
    second = s == 1
    window = pl.ds(pl.multiple_of(zq * 768 + x // 2 * 384 + odd * 128, 128), WIDE)
    my_rows = pl.ds(pl.multiple_of(odd * 64 + c * LANE, 32), LANE)
    core_rows = pl.ds(pl.multiple_of(odd * 64 + (1 - c) * LANE, 32), LANE)

    def copier(slot, src, dst, to):
        return pltpu.make_async_remote_copy(
            src_ref=src,
            dst_ref=dst,
            send_sem=send_sem.at[slot],
            recv_sem=recv_sem.at[slot],
            device_id=to,
            device_id_type=pl.DeviceIdType.MESH,
        )

    def arrived(slot, where):
        copier(slot, where, where, core).wait_recv()

    def cols_of(replica):
        return pl.ds(pl.multiple_of(replica * ROWS, ROWS), ROWS)

    load_w = pltpu.make_async_copy(w, wv, here_sem.at[0])
    load_m1 = pltpu.make_async_copy(m1, m1v, here_sem.at[1])
    load_m2 = pltpu.make_async_copy(m2, m2v, here_sem.at[2])
    tokens = [pl.ds(pl.multiple_of(half * HALF, HALF), HALF) for half in (c, 1 - c)]
    load_x = [
        pltpu.make_async_copy(inputs.at[tokens[i]], xin.at[half], here_sem.at[3 + i])
        for i, half in enumerate((c, 1 - c))
    ]
    load_cot = pltpu.make_async_copy(cotangent.at[tokens[0], window], cot, here_sem.at[5])
    load_w.start()

    @pl.when(first)
    def _():
        for one in load_x:
            one.start()

    @pl.when(second)
    def _():
        load_cot.start()
        load_m1.start()
        load_m2.start()

    barrier = pltpu.get_barrier_semaphore()
    ys_core = [{"section": core["section"], "dp": one["dp"]} for one in ys]
    peers = [core, across, far] + ys + ys_core + xs + zs
    for peer in peers:
        pl.semaphore_signal(barrier, inc=1, device_id=peer, device_id_type=pl.DeviceIdType.MESH)
    load_w.wait()
    pl.semaphore_wait(barrier, len(peers))

    pieces = [pl.ds(PIECE * t, PIECE) for t in range(2)]
    cuts = [pl.ds(CUT * t, CUT) for t in range(3)]
    my_cuts = [pl.ds(pl.multiple_of(odd * 64 + c * LANE + CUT * t, 32), CUT) for t in range(3)]

    w_far = [copier(W_Z + t, wv.at[cuts[t]], wp.at[my_cuts[t], cols_of(dp)], far) for t in range(3)]
    mine = wp.at[my_rows, cols_of(dp)]
    sent = [copier(W_Y + j, wv, mine, ys[j]) for j in range(3)]
    sent.append(copier(W_C, wv, mine, core))

    @pl.when(first)
    def _():
        for one in w_far:
            one.start()

    for one in sent:
        one.start()
    sent += w_far
    wp[my_rows, cols_of(dp)] = wv[...]
    blank = pl.ds(pl.multiple_of((1 - odd) * PAIR, 64), WIDE - PAIR)
    wp[blank, :] = jnp.zeros((WIDE - PAIR, D), BF16)

    def normalise(rows):
        centre = jnp.mean(rows, axis=1, keepdims=True)
        gap = rows - centre
        scale = lax.rsqrt(jnp.mean(gap * gap, axis=1, keepdims=True) + NORM_EPS)
        return (gap * scale).astype(BF16), centre, scale

    def keep_stats(rows, block, centre, scale):
        inv[rows, :] = jnp.broadcast_to(scale, (scale.shape[0], 128))
        normed[rows, :] = (block.astype(F32) - centre) * scale

    @pl.when(first)
    def _():
        load_x[0].wait()
        low[c], centre, scale = normalise(xin[c].astype(F32))
        keep_stats(slice(None), xin[c, :, window], centre, scale)

    def to_core(slot, replica):
        block = wp.at[my_rows, cols_of(replica)]
        one = copier(slot, block, block, core)
        one.start()
        sent.append(one)

    from_y = [zh * 4 + (y + 4 - j) % 4 for j in (1, 2, 3)]
    from_zy = [(1 - zh) * 4 + (y + 4 - j) % 4 for j in (1, 2, 3)]
    for j in range(3):
        arrived(W_Y + j, wp.at[my_rows, cols_of(from_y[j])])
        to_core(W_C + 2 + j, from_y[j])

    @pl.when(second)
    def _():
        for one in w_far:
            one.start()

    for t in range(3):
        held = wp.at[my_cuts[t], cols_of(other)]
        arrived(W_Z + t, held)
        for j in range(3):
            one = copier(W_ZY + 3 * t + j, held, held, ys[j])
            one.start()
            sent.append(one)

    near = pl.ds(pl.multiple_of(zh * 1536, 1536), 1536)
    away = pl.ds(pl.multiple_of((1 - zh) * 1536, 1536), 1536)

    def times_weight(rows, cols):
        return SCALE * lax.dot_general(
            low[c, rows, cols], wp[:, cols], (((1,), (1,)), ((), ())), preferred_element_type=F32
        )

    @pl.when(first)
    def _():
        for i, replica in zip((0, 2, 3, 4), [dp] + from_y):
            arrived(W_C + i, wp.at[core_rows, cols_of(replica)])
        mixed[...] = times_weight(slice(None), near)

    to_core(W_C + 1, other)
    for j in range(3):
        for t in range(3):
            arrived(W_ZY + 3 * t + j, wp.at[my_cuts[t], cols_of(from_zy[j])])
        to_core(W_C + 5 + j, from_zy[j])

    @pl.when(first)
    def _():
        for i, replica in zip((1, 5, 6, 7), [other] + from_zy):
            arrived(W_C + i, wp.at[core_rows, cols_of(replica)])

    def column_sums():
        csum[...] = lax.dot_general(
            jnp.ones((16, D), BF16), wp[...], (((1,), (1,)), ((), ())), preferred_element_type=F32
        )

    left = lax.broadcasted_iota(jnp.int32, (PIECE, 128), 1) < 64
    left16 = lax.broadcasted_iota(jnp.int32, (16, 128), 1) < 64

    def turn(block):
        return pltpu.roll(block, 64, 1)

    def pack(full, shared, shift):
        turned = turn(shared)
        near, away = (turned, shared) if shift else (shared, turned)
        return jnp.concatenate([full, jnp.where(left16, near[:16], away[16:])], axis=0)

    def pack_own(wide):
        low_form = pack(wide[:, :128], wide[:, 128:], False)
        return jnp.where(odd == 0, low_form, pack(wide[:, 128:], wide[:, :128], True))

    def shared_part(packed, shift):
        end = packed[PIECE:]
        turned = turn(end)
        return jnp.concatenate([turned, end] if shift else [end, turned], axis=0)

    def unpack_own(packed):
        full = packed[:PIECE]
        low_form = jnp.concatenate([full, shared_part(packed, False)], axis=1)
        high_form = jnp.concatenate([shared_part(packed, True), full], axis=1)
        return jnp.where(odd == 0, low_form, high_form)

    own = [xg.at[x, zq, t] for t in range(2)]
    x_up = [copier(X_UP + t, xout.at[t], own[t], across) for t in range(2)]
    x_z = [copier(X_Z + 3 * t + j, own[t], own[t], zs[j]) for t in range(2) for j in range(3)]
    x_x = {}
    for t in range(2):
        for i in range(4):
            block = xg.at[x, (zq + 4 - i) % 4, t]
            for j in range(3):
                x_x[t, i, j] = copier(X_X + 12 * t + 3 * i + j, block, block, xs[j])
    swap_low = copier(LOW, low.at[c], low.at[c], core)

    @pl.when(second)
    def _():
        for t in range(2):
            arrived(X_UP + t, own[t])
            for one in x_z[3 * t : 3 * t + 3] + [x_x[t, 0, j] for j in range(3)]:
                one.start()
        for t in range(2):
            for j in range(3):
                arrived(X_Z + 3 * t + j, xg.at[x, (zq + 3 - j) % 4, t])
                for k in range(3):
                    x_x[t, j + 1, k].start()
        for i, replica in enumerate([dp, other] + from_y + from_zy):
            arrived(W_C + i, wp.at[core_rows, cols_of(replica)])
        load_cot.wait()

    def gathered(t):
        for i in range(4):
            for j in range(3):
                block = xg.at[(x + 3 - j) % 4, (zq + 4 - i) % 4, t]
                arrived(X_X + 12 * t + 3 * i + j, block)
        rows = pieces[t]
        parts = []
        for m in range(8):
            even = xg[m % 2 * 2, m // 2, t].astype(F32)
            late = xg[m % 2 * 2 + 1, m // 2, t].astype(F32)
            middle = jnp.where(left, shared_part(even, False), shared_part(late, True))
            parts += [even[:PIECE], middle, late[:PIECE]]
        low[c, rows], centre, scale = normalise(jnp.concatenate(parts, axis=1))
        keep_stats(rows, unpack_own(xg[x, zq, t].astype(F32)), centre, scale)

    def find_slope(rows, upstream):
        up[rows, :] = upstream.astype(F32)
        slopes[rows, :] = (up[rows, :] * slope_of[rows, :]).astype(BF16)

    b_x = {}
    for t in range(2):
        for i in range(4):
            q = (zq + 1 + i) % 4
            for j in range(3):
                block = bsend.at[(x + 1 + j) % 4, q, t]
                b_x[t, i, j] = copier(B_X + 12 * t + 3 * i + j, block, brecv.at[j, q, t], xs[j])

    def back(t):
        slope = slopes[pieces[t], :]
        for i in range(4):
            q = (zq + 1 + i) % 4
            for half in range(2):
                cols = pl.ds(pl.multiple_of(q * 768 + half * 384, 384), 384)
                part = SCALE * jnp.dot(slope, wp[:, cols], preferred_element_type=F32)
                middle = part[:, 128:256]
                bsend[2 * half, q, t] = pack(part[:, :128], middle, False).astype(BF16)
                bsend[2 * half + 1, q, t] = pack(part[:, 256:], middle, True).astype(BF16)
            for j in range(3):
                b_x[t, i, j].start()

    r_x = [copier(R_X + j, rsend, rrecv.at[j], xs[j]) for j in range(3)]
    r_z = [copier(R_Z + j, rzsend, rzrecv.at[j], zs[j]) for j in range(3)]

    def give_sums():
        wide = slopes[...].astype(F32)
        r1 = jnp.sum(wide * csum[0:1, :], axis=1, keepdims=True) * (SCALE / D)
        r2 = jnp.sum(wide * mixed[...], axis=1, keepdims=True) * (1.0 / D)
        spot = lax.broadcasted_iota(jnp.int32, (HALF, 128), 1)
        both = jnp.where(spot == 0, r1, jnp.where(spot == 1, r2, 0.0))
        both = jnp.concatenate([both, jnp.zeros((128 - HALF, 128), F32)], axis=0)
        rsend[...] = both.T[:8, :]
        for one in r_x:
            one.start()

    low_y = {}
    for i, half in enumerate((1 - zh, zh)):
        for j in range(3):
            cols = cols_of(half * 4 + (y + 1 + j) % 4)
            low_y[i, j] = copier(L_Y + 3 * i + j, low.at[:, :, cols], lowx.at[i, y], ys[j])

    for t in range(2):
        rows = pieces[t]

        @pl.when(second)
        def _():
            gathered(t)
            mixed[rows, :] = times_weight(rows, slice(None))
            if t == 1:
                swap_low.start()

        @pl.when(first)
        def _():
            mixed[rows, :] = mixed[rows, :] + times_weight(rows, away)

        value, slope_value = gelu_both(mixed[rows, :])
        slope_of[rows, :] = slope_value

        @pl.when(first)
        def _():
            xout[t] = pack_own(xin[c, rows, window].astype(F32) + value).astype(BF16)
            x_up[t].start()

        @pl.when(second)
        def _():
            find_slope(rows, cot[rows, :])
            back(t)
            x2_w[rows, :] = (unpack_own(xg[x, zq, t].astype(F32)) + value).astype(BF16)

    @pl.when(first)
    def _():
        load_x[1].wait()
        low[1 - c], _, _ = normalise(xin[1 - c].astype(F32))
        for one in low_y.values():
            one.start()
        for i, half in enumerate((1 - zh, zh)):
            lowx[i, y] = low[:, :, cols_of(half * 4 + y)]
        column_sums()
        for t in range(2):
            arrived(G_DOWN + t, g_in.at[t])
            find_slope(pieces[t], unpack_own(g_in[t].astype(F32)))
            back(t)

    @pl.when(second)
    def _():
        column_sums()

    give_sums()
    slope_t[...] = slopes[...].T
    swap_slope = copier(SLOPE, slope_t.at[core_rows], sl.at[c], core)
    swap_x2 = copier(X2, x2_t.at[core_rows], x2.at[c], core)
    send_far = [copier(G_Z + t, gzs.at[cuts[t]], gzr.at[cuts[t]], far) for t in range(3)]

    def reduce_far():
        for t in range(3):
            total = gsend[1 - zh, y, cuts[t]].astype(F32)
            for j in range(3):
                arrived(G_YO + 3 * j + t, grecv.at[0, j, cuts[t]])
                total = total + grecv[0, j, cuts[t]].astype(F32)
            gzs[cuts[t], :] = total.astype(BF16)
            send_far[t].start()

    b_z = []

    def sum_terms(t):
        for i in range(4):
            q = (zq + 1 + i) % 4
            total = bsend[x, q, t].astype(F32)
            for j in range(3):
                arrived(B_X + 12 * t + 3 * i + j, brecv.at[j, q, t])
                total = total + brecv[j, q, t].astype(F32)
            if i < 3:
                zsend[q, t] = total.astype(BF16)
                one = copier(B_Z + 3 * t + i, zsend.at[q, t], zrecv.at[i, t], zs[i])
                one.start()
                b_z.append(one)
            else:
                zacc[t] = total
        if t == 0:
            sums = rsend[...]
            for j in range(3):
                arrived(R_X + j, rrecv.at[j])
                sums = sums + rrecv[j]
            rzsend[...] = sums
            for one in r_z:
                one.start()

    s_y = {}
    for flip in range(2):
        for dy in range(4):
            if flip + dy:
                to = core if dy == 0 else (ys_core if flip else ys)[dy - 1]
                s_y[flip, dy] = copier(S_Y + 2 * dy + flip - 1, spack.at[flip], sg.at[y, c], to)

    @pl.when(second)
    def _():
        swap_slope.start()
        sl[c] = slope_t[my_rows, :]

    @pl.when(first)
    def _():
        for flip, rows in enumerate((my_rows, core_rows)):
            block = slope_t[rows, :]
            spack[flip] = jnp.concatenate([block[:48], block[48:]], axis=1)
        for one in s_y.values():
            one.start()
        sg[y, c] = spack[0]

    def give_far():
        for i in range(2):
            for j in range(3):
                arrived(L_Y + 3 * i + j, lowx.at[i, (y + 3 - j) % 4])
        for dy in range(4):
            for flip in range(2):
                if flip + dy:
                    block = sg.at[(y + 4 - dy) % 4, c + flip - 2 * c * flip]
                    arrived(S_Y + 2 * dy + flip - 1, block)
        left48 = lax.broadcasted_iota(jnp.int32, (PACK, 128), 1) < 64
        parts = []
        for k in range(4):
            even, late = sg[k, 0].astype(F32), sg[k, 1].astype(F32)
            upper = jnp.where(left48, even, turn(late))
            lower = jnp.where(left48, turn(even), late)
            parts.append(jnp.concatenate([upper, lower], axis=0).astype(BF16))
        whole = jnp.concatenate(parts, axis=1)
        part = jnp.dot(whole, lowx[0].reshape(8 * HALF, ROWS), preferred_element_type=F32)
        gzs[...] = (part * SCALE).astype(BF16)
        for one in send_far:
            one.start()
        wide_t[...] = whole

    @pl.when(first & (zh == 1))
    def _():
        give_far()

    sum_terms(0)

    sum_terms(1)

    @pl.when(first & (zh == 0))
    def _():
        give_far()

    g_y = []
    for i, half in enumerate((1 - zh, zh)):
        for j in range(3):
            to = (y + 1 + j) % 4
            if i == 0:
                g_y += [
                    copier(
                        G_YO + 3 * j + t,
                        gsend.at[half, to, cuts[t]],
                        grecv.at[i, j, cuts[t]],
                        ys[j],
                    )
                    for t in range(3)
                ]
            else:
                g_y.append(copier(G_YS + j, gsend.at[half, to], grecv.at[i, j], ys[j]))

    @pl.when(second)
    def _():
        arrived(LOW, low.at[1 - c])
        arrived(SLOPE, sl.at[1 - c])
        whole = jnp.concatenate([sl[0], sl[1]], axis=1)
        for i, half in enumerate((1 - zh, zh)):
            for j in range(4):
                to = (y + 1 + j) % 4
                rows = low[:, :, cols_of(half * 4 + to)].reshape(2 * HALF, ROWS)
                part = jnp.dot(whole, rows, preferred_element_type=F32)
                gsend[half, to] = (part * SCALE).astype(BF16)
                if j < 3:
                    for one in g_y[3 * j : 3 * j + 3] if i == 0 else g_y[9 + j : 10 + j]:
                        one.start()

    sums = rzsend[...]
    for j in range(3):
        arrived(R_Z + j, rzrecv.at[j])
        sums = sums + rzrecv[j]
    sums = jnp.concatenate([sums, jnp.zeros((120, 128), F32)], axis=0).T
    g_down = [copier(G_DOWN + t, gpack.at[t], g_in.at[t], across) for t in range(2)]
    for t in range(2):
        rows = pieces[t]
        total = zacc[t]
        for j in range(3):
            arrived(B_Z + 3 * t + j, zrecv.at[j, t])
            total = total + zrecv[j, t].astype(F32)
        r1 = sums[PIECE * t : PIECE * t + PIECE, 0:1]
        r2 = sums[PIECE * t : PIECE * t + PIECE, 1:2]
        change = inv[rows, 0:1] * (unpack_own(total) - r1 - normed[rows, :] * r2)
        renewed = up[rows, :] + change
        gout[rows, :] = renewed.astype(BF16)

        @pl.when(second)
        def _():
            gpack[t] = pack_own(renewed).astype(BF16)
            g_down[t].start()

    @pl.when(second)
    def _():
        reduce_far()

    g_t[...] = gout[...].T
    swap_g = copier(G_C, g_t.at[core_rows], gc.at[c], core)
    swap_g.start()
    gc[c] = g_t[my_rows, :]

    @pl.when(first)
    def _():
        rows = lowx[1].reshape(8 * HALF, ROWS)
        gown[...] = SCALE * jnp.dot(wide_t[...], rows, preferred_element_type=F32)

    send_spare = copier(SPARE, x2, spare_in, across)

    @pl.when(second)
    def _():
        x2_t[...] = x2_w[...].T
        swap_x2.start()
        x2[c] = x2_t[my_rows, :]
        arrived(X2, x2.at[1 - c])
        send_spare.start()

        total = gsend[zh, y].astype(F32)
        for j in range(3):
            arrived(G_YS + j, grecv.at[1, j])
            total = total + grecv[1, j].astype(F32)
        gown[...] = total
        spare[...] = jnp.zeros_like(spare)
        copy[...] = jnp.zeros_like(copy)

    @pl.when(first)
    def _():
        arrived(SPARE, spare_in)
        spare[...] = jnp.concatenate([spare_in[0], spare_in[1]], axis=1)
        arrived(COPY, copy_in)
        copy[...] = copy_in[...]
        for one in x_up + list(low_y.values()) + list(s_y.values()):
            one.wait_send()

    for one in sent + list(b_x.values()) + b_z + r_x + r_z:
        one.wait_send()

    @pl.when(second)
    def _():
        for one in x_z + list(x_x.values()) + g_down + g_y:
            one.wait_send()
        for one in (swap_slope, swap_low, swap_x2, send_spare):
            one.wait_send()

    arrived(G_C, gc.at[1 - c])
    grad[...] = jnp.concatenate([gc[0], gc[1]], axis=1)
    swap_g.wait_send()

    for t in range(3):
        arrived(G_Z + t, gzr.at[cuts[t]])
    total = gown[...] + gzr[...].astype(F32)
    gradient[...] = total
    send_copy = copier(COPY, copy_out, copy_in, across)

    @pl.when(second)
    def _():
        load_m1.wait()
        load_m2.wait()
        copy_out[...] = stepped(wv[...], m1v[...], m2v[...], total)[0]
        send_copy.start()

    for one in send_far:
        one.wait_send()

    @pl.when(second)
    def _():
        send_copy.wait_send()


def per_device(inputs, cotangent, weight, moment1, moment2):
    vmem = pl.BlockSpec(memory_space=pltpu.VMEM)
    anywhere = pl.BlockSpec(memory_space=pl.ANY)
    shape = jax.ShapeDtypeStruct
    outs = [
        shape((LANE, 2 * HALF), BF16),
        shape((LANE, 2 * HALF), BF16),
        shape((LANE, ROWS), F32),
        shape((LANE, ROWS), BF16),
    ]
    scratch = [
        ((2, HALF, D), BF16),
        ((HALF, WIDE), BF16),
        ((LANE, ROWS), BF16),
        ((LANE, ROWS), F32),
        ((LANE, ROWS), F32),
        ((WIDE, D), BF16),
        ((16, WIDE), F32),
        ((2, HALF, D), BF16),
        ((4, 4, 2, PACK, 128), BF16),
        ((2, PACK, 128), BF16),
        ((HALF, WIDE), F32),
        ((HALF, 128), F32),
        ((HALF, WIDE), F32),
        ((HALF, WIDE), F32),
        ((HALF, WIDE), F32),
        ((2, PACK, 128), BF16),
        ((WIDE, HALF), BF16),
        ((2, LANE, HALF), BF16),
        ((WIDE, HALF), BF16),
        ((2, LANE, HALF), BF16),
        ((2, LANE, HALF), BF16),
        ((4, 4, 2, PACK, 128), BF16),
        ((3, 4, 2, PACK, 128), BF16),
        ((2, PACK, 128), F32),
        ((4, 2, PACK, 128), BF16),
        ((3, 2, PACK, 128), BF16),
        ((8, 128), F32),
        ((3, 8, 128), F32),
        ((8, 128), F32),
        ((3, 8, 128), F32),
        ((2, PACK, 128), BF16),
        ((HALF, WIDE), BF16),
        ((WIDE, HALF), BF16),
        ((2, LANE, HALF), BF16),
        ((2, 4, LANE, ROWS), BF16),
        ((2, 3, LANE, ROWS), BF16),
        ((LANE, ROWS), BF16),
        ((LANE, ROWS), BF16),
        ((LANE, ROWS), BF16),
        ((LANE, ROWS), BF16),
        ((HALF, WIDE), BF16),
        ((HALF, WIDE), BF16),
        ((2, PACK, 128), BF16),
        ((4, 2, PACK, 128), BF16),
        ((2, 4, 2, HALF, ROWS), BF16),
        ((LANE, ROWS), F32),
        ((LANE, 8 * HALF), BF16),
    ]
    spare, grad, gradient, copy = pl.pallas_call(
        kernel,
        out_shape=outs,
        in_specs=[anywhere] * 5,
        out_specs=[vmem] * 4,
        scratch_shapes=[pltpu.VMEM(dims, kind) for dims, kind in scratch]
        + [pltpu.SemaphoreType.DMA((SLOTS,))] * 2
        + [pltpu.SemaphoreType.DMA((6,))],
        compiler_params=pltpu.CompilerParams(
            collective_id=0, has_side_effects=True, vmem_limit_bytes=54784 * 2**10
        ),
    )(inputs, cotangent, weight.T, moment1.T, moment2.T)
    new = stepped(weight, moment1, moment2, gradient.T)
    return (spare.T, grad.T) + new + (copy.T,)


def solution(mesh):
    split = P("dp", "section")
    return jax.shard_map(
        per_device,
        mesh=mesh,
        in_specs=(P("dp", None), P("dp", None), split, split, split),
        out_specs=(split,) * 6,
        check_vma=False,
    )
```
